32 devices in a mesh: ex: 8 (over z, y), ez: 4 (over x, core).
Axes of the slice: x: 2, y: 2, z: 4, core: 2. Of those that a mesh axis runs over, the one named last changes fastest.
Arguments:
- potential: float32 [64, 16, 32], P('ex', None, 'ez'), may hold values from -1.5 to 0.5
- basis_start: bfloat16 [8, 4, 2, 1728, 128], P('ex', 'ez'), may hold values from -6 to 6
Outputs:
- diagonal_blocks: float32 [8, 128, 4, 2, 128], P('ex', 'ez')
- coupling_blocks: float32 [8, 128, 4, 2, 3, 128], P('ex', 'ez')
The draws below stay inside these ranges and needn't reach their ends.
All inputs are finite; a program needn't handle non-finite values.
Results may differ from the reference program's by a relative error of at most 0.0003.
Values sent between devices are 32-bit elements; how exact they have to be, the bound alone decides.
No kernel may reach another device: no remote copies, remote signals or barrier semaphores. Data moves between devices by JAX's collectives and lax.ppermute only.
A program may use at most 64 MiB of HBM per device.

```python
import jax
import jax.numpy as jnp
from jax import lax

G = 8
NB = 128
EY = 2
FILTER = 3
NXE = 8
NZE = 4
EXT = 12
EXT3 = 1728
NXG = 64
NYG = 16
NZG = 32


def shard_levels(own_key, extent, pieces, least, high):
    factor_of, own = 1.0, jax.random.fold_in(own_key, 6)
    for dim, shards_of in pieces:
        draws = jnp.exp(jax.random.uniform(jax.random.fold_in(own, dim), (shards_of,), jnp.float32, least / len(pieces), high / len(pieces)))
        factor_of = factor_of * jnp.repeat(draws, extent[dim] // shards_of).reshape([-1 if axis == dim else 1 for axis in range(len(extent))])
    return factor_of


def normal_values(key, dims, spread, limit, split=(), held_as=jnp.bfloat16):
    drawn = jax.random.normal(key, dims, jnp.float32) * spread
    if len(split) > 0:
        drawn = shard_levels(key, dims, split, -0.22, 0.18) * drawn
    return jnp.clip(drawn, min=-limit, max=limit).astype(held_as)


def setup_inputs(seed: int = 0) -> dict:
    keys = jax.random.split(jax.random.key(seed), 3)
    potential = jnp.clip(-1.5 + 2.0 * jax.random.uniform(keys[0], (NXG, NYG, NZG), jnp.float32) ** shard_levels(keys[0], (NXG, NYG, NZG), ((0, 8), (2, 4)), -0.2, 0.2), -1.5, 0.5)
    basis_start = normal_values(keys[1], (NXE, NZE, EY, EXT3, NB), 1.0, 6.0, ((0, 8), (1, 4)))
    return dict(potential=potential, basis_start=basis_start)


center = 6.5
halfwidth = 5.5
penalty = 1.0
highest = lax.Precision.HIGHEST

def apply_hamiltonian(field, potential_box):
    padded = jnp.pad(field, ((1, 1), (1, 1), (1, 1), (0, 0)))
    beside = padded[2:, 1:-1, 1:-1] + padded[:-2, 1:-1, 1:-1]
    beside = beside + padded[1:-1, 2:, 1:-1] + padded[1:-1, :-2, 1:-1]
    beside = beside + padded[1:-1, 1:-1, 2:] + padded[1:-1, 1:-1, :-2]
    return 3.0 * field - 0.5 * beside + potential_box[:, :, :, None] * field

def local_basis(initial, potential_box):
    box_side = potential_box.shape[0]
    margin = (box_side - G) // 2
    columns = initial.shape[-1]
    previous = initial.astype(jnp.float32).reshape(box_side, box_side, box_side, columns)
    current = (apply_hamiltonian(previous, potential_box) - center * previous) / halfwidth
    for iteration in range(FILTER - 1):
        following = 2.0 / halfwidth * (apply_hamiltonian(current, potential_box) - center * current) - previous
        previous, current = (current, following)
    flattened = current.reshape(box_side ** 3, columns)
    intersection = lax.dot_general(flattened.astype(jnp.float32), flattened.astype(jnp.float32), (((0,), (0,)), ((), ())), precision=highest, preferred_element_type=jnp.float32)
    factor = jnp.linalg.cholesky(intersection)
    interior = current[margin:margin + G, margin:margin + G, margin:margin + G].reshape(G ** 3, columns)
    solved = jax.scipy.linalg.solve_triangular(factor, interior.T, lower=True)
    return solved.T.reshape(G, G, G, columns)

def forward_difference(basis, dimension):
    differences = jnp.diff(basis, axis=dimension)
    widths = [(0, 0)] * basis.ndim
    widths[dimension] = (0, 1)
    return jnp.pad(differences, widths)

def volume_terms(basis, inner_potential):
    gradients = [forward_difference(basis, dimension) for dimension in (1, 2, 3)]
    weighted = jnp.concatenate([0.5 * gradients[0], 0.5 * gradients[1], 0.5 * gradients[2], inner_potential[..., None] * basis], axis=1)
    plain_side = jnp.concatenate(gradients + [basis], axis=1)
    elements = basis.shape[0]
    columns = basis.shape[-1]
    weighted = weighted.reshape(elements, -1, columns)
    plain_side = plain_side.reshape(elements, -1, columns)
    return jnp.einsum('epi,epj->iej', weighted, plain_side, precision=highest)

def face_traces(basis):
    points = basis.shape[1]
    elements = basis.shape[0]
    columns = basis.shape[-1]
    plus_layers = []
    minus_layers = []
    for dimension in (1, 2, 3):
        outer_last = lax.index_in_dim(basis, points - 1, dimension, keepdims=False)
        inner_last = lax.index_in_dim(basis, points - 2, dimension, keepdims=False)
        outer_first = lax.index_in_dim(basis, 0, dimension, keepdims=False)
        inner_first = lax.index_in_dim(basis, 1, dimension, keepdims=False)
        plus_layers.append(jnp.stack([outer_last, outer_last - inner_last], axis=1))
        minus_layers.append(jnp.stack([outer_first, inner_first - outer_first], axis=1))
    plus_traces = jnp.stack(plus_layers, axis=1).reshape(elements, 3, 2, points * points, columns)
    minus_traces = jnp.stack(minus_layers, axis=1).reshape(elements, 3, 2, points * points, columns)
    return (plus_traces, minus_traces)

def face_diagonal(plus_traces, minus_traces):
    side_plus = -0.25 * plus_traces[:, :, 1] + 0.5 * penalty * plus_traces[:, :, 0]
    side_minus = 0.25 * minus_traces[:, :, 1] + 0.5 * penalty * minus_traces[:, :, 0]
    direct = jnp.einsum('ekpi,ekpj->iej', side_plus, plus_traces[:, :, 0], precision=highest)
    direct = direct + jnp.einsum('ekpi,ekpj->iej', side_minus, minus_traces[:, :, 0], precision=highest)
    mirror = jnp.einsum('ekpi,ekpj->iej', plus_traces[:, :, 0], side_plus, precision=highest)
    mirror = mirror + jnp.einsum('ekpi,ekpj->iej', minus_traces[:, :, 0], side_minus, precision=highest)
    return direct + mirror

def coupling(plus_traces, next_traces):
    weighted = 0.25 * plus_traces[:, :, 1] - penalty * plus_traces[:, :, 0]
    result = jnp.einsum('ekpi,ekpj->iekj', weighted, next_traces[:, :, 0], precision=highest)
    return result - 0.25 * jnp.einsum('ekpi,ekpj->iekj', plus_traces[:, :, 0], next_traces[:, :, 1], precision=highest)

def reference(potential, basis_start):
    margin = G // 4
    padded = jnp.pad(potential, margin, mode='wrap')

    def slab_basis(x_index):
        slab_start = lax.dynamic_index_in_dim(basis_start, x_index, 0, keepdims=False).reshape(NZE * EY, EXT3, NB)

        def one_element(element):
            z_index = element // EY
            y_index = element % EY
            potential_box = lax.dynamic_slice(padded, (x_index * G, y_index * G, z_index * G), (EXT, EXT, EXT))
            initial = lax.dynamic_index_in_dim(slab_start, element, 0, keepdims=False)
            return local_basis(initial, potential_box)
        return lax.map(one_element, jnp.arange(NZE * EY, dtype=jnp.int32))

    def slab_potential(x_index):
        layers = lax.dynamic_slice_in_dim(potential, x_index * G, G, 0)
        return layers.reshape(G, EY, G, NZE, G).transpose(3, 1, 0, 2, 4).reshape(NZE * EY, G, G, G)

    def assemble(carry, x_index):
        basis = slab_basis(x_index)
        plus_traces, minus_traces = face_traces(basis)
        diagonal = volume_terms(basis, slab_potential(x_index)) + face_diagonal(plus_traces, minus_traces)
        own_minus = minus_traces.reshape(NZE, EY, 3, 2, G * G, NB)
        from_y = jnp.roll(own_minus[:, :, 1], -1, axis=1).reshape(NZE * EY, 2, G * G, NB)
        from_z = jnp.roll(own_minus[:, :, 2], -1, axis=0).reshape(NZE * EY, 2, G * G, NB)
        next_traces = jnp.stack([carry, from_y, from_z], axis=1)
        coupled = coupling(plus_traces, next_traces)
        return (minus_traces[:, 0], (diagonal.reshape(NB, NZE, EY, NB), coupled.reshape(NB, NZE, EY, 3, NB)))
    first_minus = face_traces(slab_basis(jnp.int32(0)))[1][:, 0]
    unused, outputs = lax.scan(assemble, first_minus, jnp.arange(NXE, dtype=jnp.int32), reverse=True)
    return (outputs[0], outputs[1])
```

```python
import functools

import jax
import jax.numpy as jnp
from jax import lax
from jax.experimental import pallas as pl
from jax.experimental.pallas import tpu as pltpu
from jax.sharding import PartitionSpec as P

G = 8
FILTER = 3

center = 6.5
halfwidth = 5.5

f32 = jnp.float32
bf16 = jnp.bfloat16

LEAD = 8
COL = 16
BLOCK = 8


def split(value):
    high = value.astype(bf16)
    return high, (value - high.astype(f32)).astype(bf16)


def product(a, b, dims):
    dims = (dims, ((), ()))
    dot = functools.partial(lax.dot_general, dimension_numbers=dims, preferred_element_type=f32)
    return dot(a[0], b[0]) + (dot(a[0], b[1]) + dot(a[1], b[0]))


NN = ((1,), (0,))
NT = ((1,), (1,))
TN = ((0,), (0,))


def bcast_row(value, k):
    return jnp.broadcast_to(value[k : k + 1, :], value.shape)


def bcast_lane(value, k, lanes):
    return jnp.broadcast_to(value[:, k : k + 1], (value.shape[0], lanes))


def inverse_factors(matrix_ref, inverse_ref):
    count, size, width = matrix_ref.shape
    row = lax.broadcasted_iota(jnp.int32, (BLOCK, size), 0)
    for start in range(0, size, BLOCK):
        rows = slice(start, start + BLOCK)
        solved = []
        for e in range(count):
            panel = [matrix_ref[e, rows, :size], matrix_ref[e, rows, size:]]
            columns = [bcast_lane(panel[0], start + j, size) for j in range(BLOCK)]
            kept = jnp.zeros_like(panel[1])
            pivots = jnp.ones_like(panel[1])
            for k in range(BLOCK):
                here = row == k
                pivot = bcast_row(columns[k], k)
                reciprocal = 1.0 / pivot
                kept = jnp.where(here, panel[1], kept)
                pivots = jnp.where(here, pivot, pivots)
                for j in range(k + 1, BLOCK):
                    scaled = bcast_row(columns[j], k) * reciprocal
                    columns[j] = jnp.where(here, scaled, columns[j] - columns[k] * scaled)
                for part in range(2):
                    scaled = bcast_row(panel[part], k) * reciprocal
                    panel[part] = jnp.where(here, scaled, panel[part] - columns[k] * scaled)
            inverse_ref[e, rows, :] = kept * lax.rsqrt(pivots)
            solved.append(panel)
        for below in range(start + BLOCK, size, BLOCK):
            for e in range(count):
                left = matrix_ref[e, below : below + BLOCK, :size]
                right = matrix_ref[e, below : below + BLOCK, size:]
                factors = [bcast_lane(left, start + k, size) for k in range(BLOCK)]
                for k in range(BLOCK):
                    left = left - factors[k] * bcast_row(solved[e][0], k)
                    right = right - factors[k] * bcast_row(solved[e][1], k)
                matrix_ref[e, below : below + BLOCK, :size] = left
                matrix_ref[e, below : below + BLOCK, size:] = right


def basis_kernel(
    elements,
    side,
    own_ref,
    x_before_ref,
    x_after_ref,
    z_before_ref,
    z_after_ref,
    start_ref,
    minus_x_ref,
    minus_z_ref,
    plus_ref,
    near_ref,
    box_ref,
    scaled_ref,
    flat_ref,
    field_a,
    field_b,
    pair_ref,
    inner_ref,
    applied_ref,
    matrix_ref,
    inverse_ref,
):
    margin = (side - G) // 2
    columns = start_ref.shape[-1]
    y_points = own_ref.shape[-1]
    slab = side * side

    box_ref[...] = jnp.zeros_like(box_ref)
    inner = slice(margin, margin + G)
    box_ref[inner, inner, :y_points] = own_ref[...]
    box_ref[:margin, inner, :y_points] = x_before_ref[...]
    box_ref[margin + G :, inner, :y_points] = x_after_ref[...]
    box_ref[:, :margin, :y_points] = z_before_ref[...]
    box_ref[:, margin + G : side, :y_points] = z_after_ref[...]

    for ref in (field_a, field_b):
        for e in range(elements):
            ref[e, 0] = jnp.zeros(ref.shape[2:], f32)
            ref[e, side + 1] = jnp.zeros(ref.shape[2:], f32)
    inside = lax.broadcasted_iota(jnp.int32, (COL, columns), 0) < side
    zero_rows = jnp.zeros((LEAD, columns), f32)

    def prepare(x, carry):
        rows = box_ref[x]
        for y in range(y_points):
            scaled_ref[x, y] = (bcast_lane(rows, y, columns) + (3.0 - center)) * (1.0 / halfwidth)
        for e in range(elements):
            flat_ref[:slab] = start_ref[e, pl.ds(pl.multiple_of(x * slab, 16), slab), :].astype(f32)
            for y in range(side):
                value = jnp.where(inside, flat_ref[side * y : side * y + COL], 0.0)
                field_a[e, x + 1, LEAD + COL * y : LEAD + COL * (y + 1)] = value
            for ref in (field_a, field_b):
                ref[e, x + 1, :LEAD] = zero_rows
                ref[e, x + 1, LEAD + COL * side :] = zero_rows
        return carry

    lax.fori_loop(0, side, prepare, 0)

    def sweep(source, target, first, last):
        def at_x(x, carry):
            for e in range(elements):

                def column(y):
                    return source[e, x + 1, LEAD + COL * y : LEAD + COL * (y + 1)]

                before, here = None, column(0)
                for y in range(side):
                    low = LEAD + COL * y
                    after = column(y + 1) if y + 1 < side else None
                    beside = source[e, x, low : low + COL] + source[e, x + 2, low : low + COL]
                    beside = beside + (
                        source[e, x + 1, low - 1 : low - 1 + COL]
                        + source[e, x + 1, low + 1 : low + 1 + COL]
                    )
                    if before is not None:
                        beside = beside + before
                    if after is not None:
                        beside = beside + after
                    y_point = (e * G - margin + y) % y_points
                    value = scaled_ref[x, y_point] * here - (0.5 / halfwidth) * beside
                    if not first:
                        value = (value + value) - target[e, x + 1, low : low + COL]
                    value = jnp.where(inside, value, 0.0)
                    target[e, x + 1, low : low + COL] = value
                    if last:
                        high, rest = split(value)
                        at = pl.multiple_of(x * (side * COL), COL) + COL * y
                        pair_ref[e, pl.ds(at, COL), :columns] = high
                        pair_ref[e, pl.ds(at, COL), columns:] = rest
                    before, here = here, after
            return carry

        lax.fori_loop(0, side, at_x, 0)

    fields = (field_a, field_b)
    for step in range(FILTER):
        sweep(fields[step % 2], fields[(step + 1) % 2], step == 0, step == FILTER - 1)
    field = fields[FILTER % 2]

    identity = (
        lax.broadcasted_iota(jnp.int32, (columns, columns), 0)
        == lax.broadcasted_iota(jnp.int32, (columns, columns), 1)
    ).astype(f32)
    for e in range(elements):
        both = lax.dot_general(
            pair_ref[e, :, :columns], pair_ref[e], (TN, ((), ())), preferred_element_type=f32
        )
        cross = both[:, columns:]
        matrix_ref[e, :, :columns] = both[:, :columns] + (cross + cross.T)
        matrix_ref[e, :, columns:] = identity

    inverse_factors(matrix_ref, inverse_ref)

    z = lax.broadcasted_iota(jnp.int32, (G, columns), 0)
    edge = (z == 1) | (z == G - 1)
    weight_down = jnp.where(z == 0, 0.0, jnp.where(edge, 0.25, 0.5))
    edge = (z == 0) | (z == G - 2)
    weight_up = jnp.where(z == G - 1, 0.0, jnp.where(edge, 0.25, 0.5))

    def link(i):
        return 0.25 if i in (0, G - 2) else 0.5

    def point_rows(e, x, y):
        low = LEAD + COL * (margin + y) + margin
        return field[e, margin + x + 1, low : low + G]

    for e in range(elements):
        for x in range(G):
            for y in range(0, G, 2):
                inner_pair, applied_pair = [], []
                for yy in (y, y + 1):
                    here = point_rows(e, x, yy)
                    potential = scaled_ref[margin + x, (e * G + yy) % y_points, margin : margin + G]
                    value = (halfwidth * potential + center) * here
                    value = value - weight_down * pltpu.roll(here, 1, 0)
                    value = value - weight_up * pltpu.roll(here, G - 1, 0)
                    if x > 0:
                        value = value - link(x - 1) * point_rows(e, x - 1, yy)
                    if x < G - 1:
                        value = value - link(x) * point_rows(e, x + 1, yy)
                    if yy > 0:
                        value = value - link(yy - 1) * point_rows(e, x, yy - 1)
                    if yy < G - 1:
                        value = value - link(yy) * point_rows(e, x, yy + 1)
                    inner_pair.append(here)
                    applied_pair.append(value)
                at = slice((x * G + y) * G, (x * G + y + 2) * G)
                for ref, pair in ((inner_ref, inner_pair), (applied_ref, applied_pair)):
                    high, rest = split(jnp.concatenate(pair, axis=0))
                    ref[e, at, :columns] = high
                    ref[e, at, columns:] = rest

    def layer(e, d, i):
        if d == 0:
            return [point_rows(e, i, y) for y in range(G)]
        if d == 1:
            return [point_rows(e, x, i) for x in range(G)]
        low = LEAD + COL * margin + margin + i
        return [field[e, margin + x + 1, pl.ds(low, G, stride=COL)] for x in range(G)]

    minus, plus, inverse = [], [], []
    for e in range(elements):
        inverse.append(split(inverse_ref[e]))
        minus_rows, plus_rows = [], []
        for d in range(3):
            minus_rows += layer(e, d, 0) + layer(e, d, 1)
            last, inside_last = layer(e, d, G - 1), layer(e, d, G - 2)
            plus_rows += [-(0.5 * a + 0.25 * b) for a, b in zip(last, inside_last)]
            plus_rows += [-0.25 * a for a in last]
        minus.append(product(split(jnp.concatenate(minus_rows, 0)), inverse[e], NT))
        plus.append(product(inverse[e], split(jnp.concatenate(plus_rows, 0)), NT))

    face = 2 * G * G
    for e in range(elements):
        minus_x_ref[e] = minus[e][:face]
        minus_z_ref[e] = minus[e][2 * face :]
        plus_ref[e, 0] = plus[e][:, :face]
        plus_ref[e, 1] = plus[e][:, 2 * face :]
        both = lax.dot_general(
            inner_ref[e, :, :columns], applied_ref[e], (TN, ((), ())), preferred_element_type=f32
        )
        raw = both[:, :columns] + both[:, columns:]
        raw = raw + lax.dot_general(
            inner_ref[e, :, columns:],
            applied_ref[e, :, :columns],
            (TN, ((), ())),
            preferred_element_type=f32,
        )
        half = product(inverse[e], split(raw), NN)
        near_ref[0, e] = product(split(half), inverse[e], NT)
        following = minus[(e + 1) % elements][face : 2 * face]
        near_ref[1, e] = product(split(plus[e][:, face : 2 * face]), split(following), NN)


def coupling_kernel(count, plus_ref, next_x_ref, next_z_ref, near_ref, *rest):
    out_refs, far_ref = rest[:-1], rest[-1]
    elements = plus_ref.shape[0]
    rows = plus_ref.shape[2] // count
    me = lax.axis_index("ez")
    for e in range(elements):
        for d, ref in ((0, next_x_ref), (1, next_z_ref)):
            far_ref[d, e] = product(split(plus_ref[e, d]), split(ref[e]), NN)
    for step in range(count):
        at = pl.ds(pl.multiple_of(lax.rem(me + step, count) * rows, rows), rows)
        for e in range(elements):
            for slot, (ref, d) in enumerate(
                ((near_ref, 0), (far_ref, 0), (near_ref, 1), (far_ref, 1))
            ):
                out_refs[step][:, elements * slot + e, :] = ref[d, e, at, :]


def assemble_kernel(count, *refs):
    in_refs, diagonal_ref, coupling_ref = refs[:count], refs[count], refs[count + 1]
    elements = diagonal_ref.shape[2]
    me = lax.axis_index("ez")
    for step in range(count):
        z = lax.rem(me + (count - step), count)
        diagonal_ref[:, z] = in_refs[step][:, :elements]
        coupling_ref[:, z] = in_refs[step][:, elements:]


def vmem(count):
    return [pl.BlockSpec(memory_space=pltpu.VMEM)] * count


def shift(block, axis, distance):
    count = lax.axis_size(axis)
    return lax.ppermute(block, axis, [(i, (i + distance) % count) for i in range(count)])


def local(potential, basis_start):
    elements, points, columns = basis_start.shape[2:]
    side = round(points ** (1 / 3))
    margin = (side - G) // 2
    y_points = potential.shape[1]
    count = lax.axis_size("ez")
    starts = basis_start.reshape(elements, points, columns)
    own = potential.transpose(0, 2, 1)
    x_before = shift(own[G - margin :], "ex", 1)
    x_after = shift(own[:margin], "ex", -1)
    tall = jnp.concatenate([x_before, own, x_after], axis=0)
    z_before = shift(tall[:, G - margin :], "ez", 1)
    z_after = shift(tall[:, :margin], "ez", -1)

    face = 2 * G * G
    shape = jax.ShapeDtypeStruct
    minus_x, minus_z, plus, near = pl.pallas_call(
        functools.partial(basis_kernel, elements, side),
        out_shape=[
            shape((elements, face, columns), f32),
            shape((elements, face, columns), f32),
            shape((elements, 2, columns, face), f32),
            shape((2, elements, columns, columns), f32),
        ],
        in_specs=vmem(6),
        out_specs=vmem(4),
        scratch_shapes=[
            pltpu.VMEM((side, COL, 128), f32),
            pltpu.VMEM((side, y_points, COL, columns), f32),
            pltpu.VMEM((side * side + COL, columns), f32),
            pltpu.VMEM((elements, side + 2, LEAD + COL * side + LEAD, columns), f32),
            pltpu.VMEM((elements, side + 2, LEAD + COL * side + LEAD, columns), f32),
            pltpu.VMEM((elements, side * side * COL, 2 * columns), bf16),
            pltpu.VMEM((elements, G**3, 2 * columns), bf16),
            pltpu.VMEM((elements, G**3, 2 * columns), bf16),
            pltpu.VMEM((elements, columns, 2 * columns), f32),
            pltpu.VMEM((elements, columns, columns), f32),
        ],
        compiler_params=pltpu.CompilerParams(vmem_limit_bytes=32 * 2**20),
        name="basis",
    )(own, x_before, x_after, z_before, z_after, starts)

    next_x = shift(minus_x, "ex", -1)
    next_z = shift(minus_z, "ez", -1)
    rows = columns // count
    blocks = pl.pallas_call(
        functools.partial(coupling_kernel, count),
        out_shape=[shape((rows, 4 * elements, columns), f32)] * count,
        in_specs=vmem(4),
        out_specs=vmem(count),
        scratch_shapes=[pltpu.VMEM((2, elements, columns, columns), f32)],
        compiler_params=pltpu.CompilerParams(vmem_limit_bytes=16 * 2**20),
        name="coupling",
    )(plus, next_x, next_z, near)
    arrived = [blocks[0]] + [shift(blocks[step], "ez", step) for step in range(1, count)]
    diagonal, coupled = pl.pallas_call(
        functools.partial(assemble_kernel, count),
        out_shape=[
            shape((rows, count, elements, columns), f32),
            shape((rows, count, 3 * elements, columns), f32),
        ],
        in_specs=vmem(count),
        out_specs=vmem(2),
        compiler_params=pltpu.CompilerParams(vmem_limit_bytes=16 * 2**20),
        name="assemble",
    )(*arrived)
    coupled = coupled.reshape(rows, count, 3, elements, columns).transpose(0, 1, 3, 2, 4)
    return (diagonal[None], coupled[None])


def solution(mesh):
    return jax.shard_map(
        local,
        mesh=mesh,
        in_specs=(P("ex", None, "ez"), P("ex", "ez", None, None, None)),
        out_specs=(P("ex", "ez", None, None, None), P("ex", "ez", None, None, None, None)),
        check_vma=False,
    )
```

```python
import functools

import jax
import jax.numpy as jnp
from jax import lax
from jax.experimental import pallas as pl
from jax.experimental.pallas import tpu as pltpu
from jax.sharding import PartitionSpec as P

G = 8
FILTER = 3

center = 6.5
halfwidth = 5.5

f32 = jnp.float32
bf16 = jnp.bfloat16

LEAD = 8
COL = 16
BLOCK = 8
PANEL = 32


def split(value):
    high = value.astype(bf16)
    return high, (value - high.astype(f32)).astype(bf16)


def weights(pair, transposed):
    high, low = pair
    empty = jnp.zeros_like(low)
    if transposed:
        upper = jnp.concatenate([high, high], axis=1)
        lower = jnp.concatenate([low, empty], axis=1)
        return jnp.concatenate([upper, lower], axis=0)
    upper = jnp.concatenate([high, low], axis=1)
    lower = jnp.concatenate([high, empty], axis=1)
    return jnp.concatenate([upper, lower], axis=0)


def product(value, held, transposed):
    pair = jnp.concatenate(split(value), axis=1)
    dims = (((1,), (1 if transposed else 0,)), ((), ()))
    both = lax.dot_general(pair, held, dims, preferred_element_type=f32)
    half = both.shape[1] // 2
    return both[:, :half] + both[:, half:]


def bcast_row(value, k):
    return jnp.broadcast_to(value[k : k + 1, :], value.shape)


def bcast_lane(value, k, lanes):
    return jnp.broadcast_to(value[:, k : k + 1], (value.shape[0], lanes))


def triple(value):
    high, rest = split(value)
    low = (value - high.astype(f32) - rest.astype(f32)).astype(bf16)
    return high, rest, low


def inverse_factors(matrix_ref, inverse_ref):
    count, size, width = matrix_ref.shape
    row = lax.broadcasted_iota(jnp.int32, (BLOCK, size), 0)
    for top in range(0, size, PANEL):
        bottom = top + PANEL
        kept = [[] for _ in range(count)]
        for start in range(top, bottom, BLOCK):
            rows = slice(start, start + BLOCK)
            for e in range(count):
                panel = [matrix_ref[e, rows, :size], matrix_ref[e, rows, size:]]
                columns = [bcast_lane(panel[0], start + j, size) for j in range(BLOCK)]
                pivot_rows = list(panel)
                pivots = None
                pivot = bcast_row(columns[0], 0)
                for k in range(BLOCK):
                    here = row == k
                    reciprocal = 1.0 / pivot
                    pivots = pivot if pivots is None else jnp.where(row >= k, pivot, pivots)
                    if k > 0:
                        pivot_rows = [
                            jnp.where(here, new, old) for new, old in zip(panel, pivot_rows)
                        ]
                    if k + 1 < BLOCK:
                        beside = bcast_row(columns[k + 1], k)
                        pivot = bcast_row(columns[k + 1], k + 1) - (beside * beside) * reciprocal
                    for j in range(k + 1, BLOCK):
                        scaled = bcast_row(columns[j], k) * reciprocal
                        columns[j] = jnp.where(here, scaled, columns[j] - columns[k] * scaled)
                    for part in range(2):
                        scaled = bcast_row(panel[part], k) * reciprocal
                        panel[part] = jnp.where(here, scaled, panel[part] - columns[k] * scaled)
                scale = lax.rsqrt(pivots)
                kept[e].append([part * scale for part in pivot_rows])
                inverse_ref[e, rows, :] = kept[e][-1][1]
                for below in range(start + BLOCK, bottom, BLOCK):
                    at = slice(below, below + BLOCK)
                    left, right = matrix_ref[e, at, :size], matrix_ref[e, at, size:]
                    terms = [[], []]
                    for k in range(BLOCK):
                        factor = bcast_lane(left, start + k, size)
                        for part in range(2):
                            terms[part].append(factor * bcast_row(panel[part], k))
                    for part in range(2):
                        while len(terms[part]) > 1:
                            pairs = zip(terms[part][::2], terms[part][1::2])
                            terms[part] = [x + y for x, y in pairs]
                    matrix_ref[e, at, :size] = left - terms[0][0]
                    matrix_ref[e, at, size:] = right - terms[1][0]
        if bottom == size:
            break
        for e in range(count):
            parts = [jnp.concatenate([b[i] for b in kept[e]], axis=0) for i in range(2)]
            left = triple(parts[0])
            both = [jnp.concatenate(p, axis=1) for p in zip(left, triple(parts[1]))]
            order = ((0, 0), (0, 1), (1, 0), (0, 2), (2, 0), (1, 1))
            taken = lax.dot_general(
                jnp.concatenate([left[i] for i, _ in order], axis=0),
                jnp.concatenate([both[j] for _, j in order], axis=0),
                (((0,), (0,)), ((), ())),
                preferred_element_type=f32,
            )
            matrix_ref[e, bottom:, :] = matrix_ref[e, bottom:, :] - taken[bottom:]


def is_inside(side, columns):
    return lax.broadcasted_iota(jnp.int32, (COL, columns), 0) < side


def zero_ends(ref, elements, side):
    for e in range(elements):
        ref[e, 0] = jnp.zeros(ref.shape[2:], f32)
        ref[e, side + 1] = jnp.zeros(ref.shape[2:], f32)
        for x in range(side):
            ref[e, x + 1, :LEAD] = jnp.zeros((LEAD, ref.shape[-1]), f32)
            ref[e, x + 1, LEAD + COL * side :] = jnp.zeros((LEAD, ref.shape[-1]), f32)


def sweep(source, scaled_ref, previous, target, pair_ref, margin):
    elements, side = source.shape[0], source.shape[1] - 2
    columns = source.shape[-1]
    y_points = scaled_ref.shape[1]
    inside = is_inside(side, columns)

    def at_x(x, carry):
        for e in range(elements):

            def column(y):
                return source[e, x + 1, LEAD + COL * y : LEAD + COL * (y + 1)]

            before, here = None, column(0)
            for y in range(side):
                low = LEAD + COL * y
                after = column(y + 1) if y + 1 < side else None
                beside = source[e, x, low : low + COL] + source[e, x + 2, low : low + COL]
                beside = beside + (
                    source[e, x + 1, low - 1 : low - 1 + COL]
                    + source[e, x + 1, low + 1 : low + 1 + COL]
                )
                if before is not None:
                    beside = beside + before
                if after is not None:
                    beside = beside + after
                y_point = (e * G - margin + y) % y_points
                value = scaled_ref[x, y_point] * here - (0.5 / halfwidth) * beside
                if previous is not None:
                    value = (value + value) - previous[e, x + 1, low : low + COL]
                value = jnp.where(inside, value, 0.0)
                target[e, x + 1, low : low + COL] = value
                if pair_ref is not None:
                    high, rest = split(value)
                    at = pl.multiple_of(x * (side * COL), COL) + COL * y
                    pair_ref[e, pl.ds(at, COL), :columns] = high
                    pair_ref[e, pl.ds(at, COL), columns:] = rest
                before, here = here, after
        return carry

    lax.fori_loop(0, side, at_x, 0)


def first_kernel(
    margin,
    own_ref,
    start_ref,
    held_ref,
    field_ref,
    first_ref,
    scaled_ref,
    box_ref,
    copy_ref,
    flat_ref,
    own_arrived,
    arrived,
):
    elements, columns = start_ref.shape[0], start_ref.shape[-1]
    side, y_points = scaled_ref.shape[:2]
    slab = side * side

    def part(e, x):
        at = pl.ds(pl.multiple_of(x * slab, 16), slab)
        return pltpu.make_async_copy(start_ref.at[e, at], copy_ref.at[e, at], arrived.at[e, x])

    own = pltpu.make_async_copy(own_ref, held_ref, own_arrived)
    own.start()
    for x in range(side):
        for e in range(elements):
            part(e, x).start()
    zero_ends(field_ref, elements, side)
    zero_ends(first_ref, elements, side)
    inside = is_inside(side, columns)
    box_ref[...] = jnp.zeros_like(box_ref)
    own.wait()
    box_ref[margin : margin + G, margin : margin + G, :y_points] = held_ref[...]

    def prepare(x, carry):
        rows = (box_ref[x] + (3.0 - center)) * (1.0 / halfwidth)
        for y in range(y_points):
            scaled_ref[x, y] = bcast_lane(rows, y, columns)
        for e in range(elements):
            part(e, x).wait()
            flat_ref[e, :slab] = copy_ref[e, pl.ds(pl.multiple_of(x * slab, 16), slab), :].astype(f32)
            for y in range(side):
                value = jnp.where(inside, flat_ref[e, side * y : side * y + COL], 0.0)
                field_ref[e, x + 1, LEAD + COL * y : LEAD + COL * (y + 1)] = value
        return carry

    lax.fori_loop(0, side, prepare, 0)
    sweep(field_ref, scaled_ref, None, first_ref, None, margin)


def point_rows(field, margin, e, x, y):
    low = LEAD + COL * (margin + y) + margin
    return field[e, margin + x + 1, low : low + G]


def layer(field, margin, e, d, i):
    if d == 0:
        return [point_rows(field, margin, e, i, y) for y in range(G)]
    if d == 1:
        return [point_rows(field, margin, e, x, i) for x in range(G)]
    low = LEAD + COL * margin + margin + i
    return [field[e, margin + x + 1, pl.ds(low, G, stride=COL)] for x in range(G)]


def basis_kernel(
    margin,
    x_before_ref,
    x_after_ref,
    z_before_ref,
    z_after_ref,
    start_in,
    first_in,
    scaled_in,
    minus_x_ref,
    minus_z_ref,
    inverse_ref,
    start_ref,
    first_ref,
    scaled_ref,
    box_ref,
    pair_ref,
    matrix_ref,
):
    elements, columns = start_ref.shape[0], start_ref.shape[-1]
    side, y_points = scaled_ref.shape[:2]
    box_ref[...] = jnp.zeros_like(box_ref)
    box_ref[:margin, margin : margin + G, :y_points] = x_before_ref[...]
    box_ref[margin + G :, margin : margin + G, :y_points] = x_after_ref[...]
    box_ref[:, :margin, :y_points] = z_before_ref[...]
    box_ref[:, margin + G : side, :y_points] = z_after_ref[...]

    def complete(x, carry):
        rows = box_ref[x] * (1.0 / halfwidth)
        for y in range(y_points):
            added = bcast_lane(rows, y, columns)
            scaled_ref[x, y] = scaled_in[x, y] + added
            for e in range(elements):
                box_y = (y - e * G + margin) % y_points
                if box_y < side:
                    at = slice(LEAD + COL * box_y, LEAD + COL * (box_y + 1))
                    first_ref[e, x + 1, at] = first_in[e, x + 1, at] + added * start_in[e, x + 1, at]
        return carry

    lax.fori_loop(0, side, complete, 0, unroll=3)
    source, field = first_ref, start_ref
    for step in range(1, FILTER):
        last = step == FILTER - 1
        sweep(source, scaled_ref, field, field, pair_ref if last else None, margin)
        source, field = field, source
    field = source

    identity = (
        lax.broadcasted_iota(jnp.int32, (columns, columns), 0)
        == lax.broadcasted_iota(jnp.int32, (columns, columns), 1)
    ).astype(f32)
    for e in range(elements):
        both = lax.dot_general(
            pair_ref[e, :, :columns],
            pair_ref[e],
            (((0,), (0,)), ((), ())),
            preferred_element_type=f32,
        )
        cross = both[:, columns:]
        matrix_ref[e, :, :columns] = both[:, :columns] + (cross + cross.T)
        matrix_ref[e, :, columns:] = identity

    inverse_factors(matrix_ref, inverse_ref)

    for e in range(elements):
        held = weights(split(inverse_ref[e]), True)
        for d, ref in ((0, minus_x_ref), (2, minus_z_ref)):
            rows = layer(field, margin, e, d, 0) + layer(field, margin, e, d, 1)
            ref[e] = product(jnp.concatenate(rows, 0), held, True)


def near_kernel(
    count,
    margin,
    inverse_ref,
    field,
    scaled_ref,
    plus_ref,
    *rest,
):
    out_refs = rest[:count]
    inner_ref, applied_ref, near_ref = rest[count:]
    elements, columns = inverse_ref.shape[0], inverse_ref.shape[-1]
    y_points = scaled_ref.shape[1]

    z = lax.broadcasted_iota(jnp.int32, (G, columns), 0)
    edge = (z == 1) | (z == G - 1)
    weight_down = jnp.where(z == 0, 0.0, jnp.where(edge, 0.25, 0.5))
    edge = (z == 0) | (z == G - 2)
    weight_up = jnp.where(z == G - 1, 0.0, jnp.where(edge, 0.25, 0.5))

    def link(i):
        return 0.25 if i in (0, G - 2) else 0.5

    for e in range(elements):
        for x in range(G):
            for y in range(0, G, 2):
                inner_pair, applied_pair = [], []
                for yy in (y, y + 1):
                    here = point_rows(field, margin, e, x, yy)
                    potential = scaled_ref[margin + x, (e * G + yy) % y_points, margin : margin + G]
                    value = (halfwidth * potential + center) * here
                    value = value - weight_down * pltpu.roll(here, 1, 0)
                    value = value - weight_up * pltpu.roll(here, G - 1, 0)
                    if x > 0:
                        value = value - link(x - 1) * point_rows(field, margin, e, x - 1, yy)
                    if x < G - 1:
                        value = value - link(x) * point_rows(field, margin, e, x + 1, yy)
                    if yy > 0:
                        value = value - link(yy - 1) * point_rows(field, margin, e, x, yy - 1)
                    if yy < G - 1:
                        value = value - link(yy) * point_rows(field, margin, e, x, yy + 1)
                    inner_pair.append(here)
                    applied_pair.append(value)
                at = slice((x * G + y) * G, (x * G + y + 2) * G)
                for ref, pair in ((inner_ref, inner_pair), (applied_ref, applied_pair)):
                    high, low = split(jnp.concatenate(pair, axis=0))
                    ref[e, at, :columns] = high
                    ref[e, at, columns:] = low

    face = 2 * G * G
    minus, plus, held = [], [], []
    for e in range(elements):
        held.append(weights(split(inverse_ref[e]), True))
        rows = layer(field, margin, e, 1, 0) + layer(field, margin, e, 1, 1)
        for d in range(3):
            last = layer(field, margin, e, d, G - 1)
            before = layer(field, margin, e, d, G - 2)
            rows += [-(0.5 * a + 0.25 * b) for a, b in zip(last, before)]
            rows += [-0.25 * a for a in last]
        faces = product(jnp.concatenate(rows, 0), held[e], True)
        minus.append(faces[:face])
        plus.append(faces[face : 2 * face].T)
        plus_ref[e, 0] = plus[e]
        plus[e] = faces[2 * face : 3 * face].T
        plus_ref[e, 1] = faces[3 * face :].T

    for e in range(elements):
        both = lax.dot_general(
            inner_ref[e, :, :columns],
            applied_ref[e],
            (((0,), (0,)), ((), ())),
            preferred_element_type=f32,
        )
        raw = both[:, :columns] + both[:, columns:]
        raw = raw + lax.dot_general(
            inner_ref[e, :, columns:],
            applied_ref[e, :, :columns],
            (((0,), (0,)), ((), ())),
            preferred_element_type=f32,
        )
        half = product(inverse_ref[e], weights(split(raw), False), False)
        near_ref[0, e] = product(half, held[e], True)
        following = weights(split(minus[(e + 1) % elements]), False)
        near_ref[1, e] = product(plus[e], following, False)
    send_rows(count, near_ref, out_refs)


def send_rows(count, blocks_ref, out_refs):
    kinds, elements, size = blocks_ref.shape[:3]
    rows = size // count
    me = lax.axis_index("ez")
    for step in range(count):
        at = pl.ds(pl.multiple_of(lax.rem(me + step, count) * rows, rows), rows)
        for kind in range(kinds):
            for e in range(elements):
                out_refs[step][:, elements * kind + e, :] = blocks_ref[kind, e, at, :]


def far_kernel(count, plus_ref, next_x_ref, next_z_ref, *rest):
    out_refs, far_ref = rest[:-1], rest[-1]
    for e in range(plus_ref.shape[0]):
        for d, ref in ((0, next_x_ref), (1, next_z_ref)):
            far_ref[d, e] = product(plus_ref[e, d], weights(split(ref[e]), False), False)
    send_rows(count, far_ref, out_refs)


def assemble_kernel(count, *refs):
    near_refs, far_refs = refs[:count], refs[count : 2 * count]
    diagonal_ref, coupling_ref = refs[2 * count :]
    elements = diagonal_ref.shape[2]
    me = lax.axis_index("ez")
    for step in range(count):
        z = lax.rem(me + (count - step), count)
        diagonal_ref[:, z] = near_refs[step][:, :elements]
        coupling_ref[:, z, 1] = near_refs[step][:, elements:]
        coupling_ref[:, z, 0] = far_refs[step][:, :elements]
        coupling_ref[:, z, 2] = far_refs[step][:, elements:]


def vmem(count):
    return [pl.BlockSpec(memory_space=pltpu.VMEM)] * count


def shift(block, axis, distance):
    count = lax.axis_size(axis)
    return lax.ppermute(block, axis, [(i, (i + distance) % count) for i in range(count)])


def local(potential, basis_start):
    elements, points, columns = basis_start.shape[2:]
    side = round(points ** (1 / 3))
    margin = (side - G) // 2
    y_points = potential.shape[1]
    count = lax.axis_size("ez")
    starts = basis_start.reshape(elements, points, columns)
    own = potential.transpose(0, 2, 1)
    x_before = shift(own, "ex", 1)[G - margin :]
    x_after = shift(own[:margin], "ex", -1)

    shape = jax.ShapeDtypeStruct
    field = shape((elements, side + 2, LEAD + COL * side + LEAD, columns), f32)
    scaled = shape((side, y_points, COL, columns), f32)
    held, start, first, own_scaled = pl.pallas_call(
        functools.partial(first_kernel, margin),
        out_shape=[shape(own.shape, f32), field, field, scaled],
        in_specs=[pl.BlockSpec(memory_space=pltpu.HBM)] * 2,
        out_specs=vmem(4),
        scratch_shapes=[
            pltpu.VMEM((side, COL, 128), f32),
            pltpu.VMEM(starts.shape, bf16),
            pltpu.VMEM((elements, side * side + COL, columns), f32),
            pltpu.SemaphoreType.DMA,
            pltpu.SemaphoreType.DMA((elements, side)),
        ],
        compiler_params=pltpu.CompilerParams(vmem_limit_bytes=24 * 2**20),
        cost_estimate=pl.CostEstimate(flops=10**8, bytes_accessed=10**7, transcendentals=0),
        name="first",
    )(own, starts)
    tall = jnp.concatenate([x_before, held, x_after], axis=0)
    z_before = shift(tall[:, G - margin :], "ez", 1)
    z_after = shift(tall[:, :margin], "ez", -1)

    face = shape((elements, 2 * G * G, columns), f32)
    square = shape((elements, columns, columns), f32)
    minus_x, minus_z, inverse, _, filtered, whole_scaled = pl.pallas_call(
        functools.partial(basis_kernel, margin),
        out_shape=[face, face, square, field, field, scaled],
        in_specs=vmem(7),
        out_specs=vmem(6),
        input_output_aliases={4: 3, 5: 4, 6: 5},
        scratch_shapes=[
            pltpu.VMEM((side, COL, 128), f32),
            pltpu.VMEM((elements, side * side * COL, 2 * columns), bf16),
            pltpu.VMEM((elements, columns, 2 * columns), f32),
        ],
        compiler_params=pltpu.CompilerParams(vmem_limit_bytes=32 * 2**20),
        name="basis",
    )(x_before, x_after, z_before, z_after, start, first, own_scaled)

    next_x = shift(minus_x, "ex", -1)
    next_z = shift(minus_z, "ez", -1)
    block = shape((columns // count, 2 * elements, columns), f32)
    plus, *near = pl.pallas_call(
        functools.partial(near_kernel, count, margin),
        out_shape=[shape((elements, 2, columns, 2 * G * G), f32)] + [block] * count,
        in_specs=vmem(3),
        out_specs=vmem(1 + count),
        scratch_shapes=[
            pltpu.VMEM((elements, G**3, 2 * columns), bf16),
            pltpu.VMEM((elements, G**3, 2 * columns), bf16),
            pltpu.VMEM((2, elements, columns, columns), f32),
        ],
        compiler_params=pltpu.CompilerParams(vmem_limit_bytes=24 * 2**20),
        cost_estimate=pl.CostEstimate(flops=10**8, bytes_accessed=10**7, transcendentals=0),
        name="near",
    )(inverse, filtered, whole_scaled)
    near = list(near[:1]) + [shift(near[step], "ez", step) for step in range(1, count)]

    far = pl.pallas_call(
        functools.partial(far_kernel, count),
        out_shape=[block] * count,
        in_specs=vmem(3),
        out_specs=vmem(count),
        scratch_shapes=[pltpu.VMEM((2, elements, columns, columns), f32)],
        compiler_params=pltpu.CompilerParams(vmem_limit_bytes=16 * 2**20),
        name="far",
    )(plus, next_x, next_z)
    far = list(far[:1]) + [shift(far[step], "ez", step) for step in range(1, count)]

    rows = columns // count
    diagonal, coupled = pl.pallas_call(
        functools.partial(assemble_kernel, count),
        out_shape=[
            shape((rows, count, elements, columns), f32),
            shape((rows, count, 3, elements, columns), f32),
        ],
        in_specs=vmem(2 * count),
        out_specs=vmem(2),
        compiler_params=pltpu.CompilerParams(vmem_limit_bytes=16 * 2**20),
        name="assemble",
    )(*near, *far)
    return (diagonal[None], coupled.transpose(0, 1, 3, 2, 4)[None])


def solution(mesh):
    return jax.shard_map(
        local,
        mesh=mesh,
        in_specs=(P("ex", None, "ez"), P("ex", "ez", None, None, None)),
        out_specs=(P("ex", "ez", None, None, None), P("ex", "ez", None, None, None, None)),
        check_vma=False,
    )
```

```python
import functools

import jax
import jax.numpy as jnp
from jax import lax
from jax.experimental import pallas as pl
from jax.experimental.pallas import tpu as pltpu
from jax.sharding import PartitionSpec as P

G = 8
FILTER = 3

center = 6.5
halfwidth = 5.5

f32 = jnp.float32
bf16 = jnp.bfloat16

LEAD = 8
COL = 16
BLOCK = 16


def split(value):
    high = value.astype(bf16)
    return high, (value - high.astype(f32)).astype(bf16)


def weights(pair, transposed):
    high, low = pair
    empty = jnp.zeros_like(low)
    if transposed:
        upper = jnp.concatenate([high, high], axis=1)
        lower = jnp.concatenate([low, empty], axis=1)
        return jnp.concatenate([upper, lower], axis=0)
    upper = jnp.concatenate([high, low], axis=1)
    lower = jnp.concatenate([high, empty], axis=1)
    return jnp.concatenate([upper, lower], axis=0)


def product(value, held, transposed):
    pair = jnp.concatenate(split(value), axis=1)
    dims = (((1,), (1 if transposed else 0,)), ((), ()))
    both = lax.dot_general(pair, held, dims, preferred_element_type=f32)
    half = both.shape[1] // 2
    return both[:, :half] + both[:, half:]


def bcast_row(value, k):
    return jnp.broadcast_to(value[k : k + 1, :], value.shape)


def bcast_lane(value, k, lanes):
    return jnp.broadcast_to(value[:, k : k + 1], (value.shape[0], lanes))


def triple(value):
    high, rest = split(value)
    low = (value - high.astype(f32) - rest.astype(f32)).astype(bf16)
    return high, rest, low


def pack(values):
    first, second = values
    half = first.shape[1] // 2
    left = lax.broadcasted_iota(jnp.int32, first.shape, 1) < half
    return (
        jnp.where(left, first, pltpu.roll(second, half, 1)),
        jnp.where(left, pltpu.roll(first, half, 1), second),
    )


def tree_sum(terms):
    while len(terms) > 1:
        terms = [a + b for a, b in zip(terms[::2], terms[1::2])] + terms[len(terms) & ~1 :]
    return terms[0]


def inverse_factors(matrix_ref, inverse_ref):
    size = matrix_ref.shape[1]
    half = size // 2
    row = lax.broadcasted_iota(jnp.int32, (BLOCK, size), 0)
    lane = lax.broadcasted_iota(jnp.int32, (BLOCK, size), 1)
    other = jnp.where(lane < half, 0, half)

    def columns_of(value, at):
        return jnp.take_along_axis(value, other + at, axis=1)

    for top in (0, half):
        parts = (0, 1, 2) if top == 0 else (1, 2, 3)
        pivot_part = 0 if top == 0 else 1
        kept = []
        for start in range(top, top + half, BLOCK):
            rows = slice(start, start + BLOCK)
            panel = [matrix_ref[part, rows, :] for part in parts]
            at = start - top
            columns = [columns_of(panel[0], at + j) for j in range(BLOCK)]
            pivot_rows = list(panel)
            pivot = bcast_row(columns[0], 0)
            pivots = pivot
            for k in range(BLOCK):
                reciprocal = 1.0 / pivot
                if k > 0:
                    pivots = jnp.where(row >= k, pivot, pivots)
                    pivot_rows = [
                        jnp.where(row >= k, new, old) for new, old in zip(panel, pivot_rows)
                    ]
                if k + 1 < BLOCK:
                    beside = bcast_row(columns[k + 1], k)
                    pivot = bcast_row(columns[k + 1], k + 1) - (beside * beside) * reciprocal
                factor = jnp.where(row == k, 0.0, columns[k]) * reciprocal
                for j in range(k + 1, BLOCK):
                    columns[j] = columns[j] - factor * bcast_row(columns[j], k)
                panel = [value - factor * bcast_row(value, k) for value in panel]
            reciprocals = 1.0 / pivots
            solved = [value * reciprocals for value in panel]
            scale = lax.rsqrt(pivots)
            kept.append([value * scale for value in pivot_rows])
            inverse_ref[0, rows, :] = kept[-1][parts.index(2)]
            if 3 in parts:
                inverse_ref[1, rows, :] = kept[-1][parts.index(3)]
            else:
                inverse_ref[1, rows, :] = jnp.zeros((BLOCK, size), f32)
            for below in range(start + BLOCK, top + half, BLOCK):
                rows = slice(below, below + BLOCK)
                values = [matrix_ref[part, rows, :] for part in parts]
                factors = [columns_of(values[0], at + k) for k in range(BLOCK)]
                for part, value, taken in zip(parts, values, solved):
                    terms = [factors[k] * bcast_row(taken, k) for k in range(BLOCK)]
                    matrix_ref[part, rows, :] = value - tree_sum(terms)
        if top == 0:
            right = [jnp.concatenate([k[i] for k in kept], axis=0) for i in (1, 2)]
            left = triple(right[0])
            both = [jnp.concatenate(p, axis=1) for p in zip(left, triple(right[1]))]
            order = ((0, 0), (0, 1), (1, 0), (0, 2), (2, 0), (1, 1))
            taken = lax.dot_general(
                jnp.concatenate([left[i] for i, _ in order], axis=0),
                jnp.concatenate([both[j] for _, j in order], axis=0),
                (((0,), (0,)), ((), ())),
                preferred_element_type=f32,
            )
            is_left = lax.broadcasted_iota(jnp.int32, (half, size), 1) < half
            for i, part in enumerate((1, 2)):
                at = slice(size * i, size * (i + 1))
                mine = jnp.where(is_left, taken[:half, at], taken[half:, at])
                matrix_ref[part, half:, :] = matrix_ref[part, half:, :] - mine


def zero_ends(ref, elements, side):
    for e in range(elements):
        ref[e, 0] = jnp.zeros(ref.shape[2:], f32)
        ref[e, side + 1] = jnp.zeros(ref.shape[2:], f32)
        for x in range(side):
            ref[e, x + 1, :LEAD] = jnp.zeros((LEAD, ref.shape[-1]), f32)
            ref[e, x + 1, LEAD + COL * side :] = jnp.zeros((LEAD, ref.shape[-1]), f32)


def beside_weight(side, columns):
    inside = lax.broadcasted_iota(jnp.int32, (COL, columns), 0) < side
    return jnp.where(inside, 1.0 / halfwidth, 0.0)


def slab_step(x, source, scaled_ref, previous, target, pair_ref, margin):
    elements, side = source.shape[0], source.shape[1] - 2
    columns = source.shape[-1]
    weight = beside_weight(side, columns)
    if previous is None:
        weight = 0.5 * weight
    for e in range(elements):

        def column(y):
            return source[e, x + 1, LEAD + COL * y : LEAD + COL * (y + 1)]

        before, here = None, column(0)
        for y in range(side):
            low = LEAD + COL * y
            after = column(y + 1) if y + 1 < side else None
            beside = source[e, x, low : low + COL] + source[e, x + 2, low : low + COL]
            beside = beside + (
                source[e, x + 1, low - 1 : low - 1 + COL]
                + source[e, x + 1, low + 1 : low + 1 + COL]
            )
            if before is not None:
                beside = beside + before
            if after is not None:
                beside = beside + after
            if previous is None:
                value = -weight * beside
            else:
                scaled = scaled_ref[x, (e * G - margin + y) % scaled_ref.shape[1]]
                value = scaled * here - weight * beside - previous[e, x + 1, low : low + COL]
            target[e, x + 1, low : low + COL] = value
            if pair_ref is not None:
                high, rest = split(value)
                at = pl.multiple_of(x * (side * COL), COL) + COL * y
                pair_ref[e, pl.ds(at, COL), :columns] = high
                pair_ref[e, pl.ds(at, COL), columns:] = rest
            before, here = here, after


def first_kernel(start_ref, field_ref, first_ref, flat_ref):
    elements, columns = start_ref.shape[0], start_ref.shape[-1]
    side = field_ref.shape[1] - 2
    slab = side * side
    zero_ends(field_ref, elements, side)
    zero_ends(first_ref, elements, side)
    inside = lax.broadcasted_iota(jnp.int32, (COL, columns), 0) < side

    def prepare(x, carry):
        for e in range(elements):
            flat_ref[e, :slab] = start_ref[e, pl.ds(pl.multiple_of(x * slab, 16), slab), :].astype(f32)
            for y in range(side):
                value = jnp.where(inside, flat_ref[e, side * y : side * y + COL], 0.0)
                field_ref[e, x + 1, LEAD + COL * y : LEAD + COL * (y + 1)] = value
        return carry

    lax.fori_loop(0, side, prepare, 0)

    def step(x, carry):
        slab_step(x, field_ref, None, None, first_ref, None, 0)
        return carry

    lax.fori_loop(0, side, step, 0)


def point_rows(field, margin, e, x, y):
    low = LEAD + COL * (margin + y) + margin
    return field[e, margin + x + 1, low : low + G]


def layer(field, margin, e, d, i):
    if d == 0:
        return [point_rows(field, margin, e, i, y) for y in range(G)]
    if d == 1:
        return [point_rows(field, margin, e, x, i) for x in range(G)]
    low = LEAD + COL * margin + margin + i
    return [field[e, margin + x + 1, pl.ds(low, G, stride=COL)] for x in range(G)]


def potential_part(x, box_ref, margin, scaled_ref, first_in, start_in, first_ref):
    elements, columns = start_in.shape[0], start_in.shape[-1]
    side, y_points = scaled_ref.shape[:2]
    rows = box_ref[x]
    for y in range(y_points):
        scaled = bcast_lane(rows, y, columns)
        scaled_ref[x, y] = scaled
        scaled = 0.5 * scaled
        for e in range(elements):
            box_y = (y - e * G + margin) % y_points
            if box_y < side:
                at = slice(LEAD + COL * box_y, LEAD + COL * (box_y + 1))
                first_ref[e, x + 1, at] = first_in[e, x + 1, at] + scaled * start_in[e, x + 1, at]


def steps(ranges, first_ref, start_ref, scaled_ref, pair_ref, margin):
    fields = (first_ref, start_ref)
    for index in range(1, FILTER):
        source, target = fields
        pair = pair_ref if index == FILTER - 1 else None

        def next_step(x, carry):
            slab_step(x, source, scaled_ref, target, target, pair, margin)
            return carry

        lax.fori_loop(*ranges(index), next_step, 0)
        fields = fields[::-1]
    return fields[0]


def overlaps(pair_ref, low, high):
    columns = pair_ref.shape[-1] // 2
    return [
        lax.dot_general(
            pair_ref[e, low:high, :columns],
            pair_ref[e, low:high],
            (((0,), (0,)), ((), ())),
            preferred_element_type=f32,
        )
        for e in range(pair_ref.shape[0])
    ]


def middle_kernel(
    margin,
    low_ref,
    z_before_ref,
    z_after_ref,
    start_in,
    first_in,
    start_ref,
    first_ref,
    scaled_ref,
    pair_ref,
    overlap_ref,
    box_ref,
):
    side, y_points = scaled_ref.shape[:2]
    end = side - margin
    box_ref[...] = jnp.zeros_like(box_ref)
    box_ref[:end, margin : margin + G, :y_points] = low_ref[...]
    box_ref[:end, :margin, :y_points] = z_before_ref[...]
    box_ref[:end, margin + G : side, :y_points] = z_after_ref[...]

    def complete(x, carry):
        potential_part(x, box_ref, margin, scaled_ref, first_in, start_in, first_ref)
        return carry

    lax.fori_loop(0, end, complete, 0, unroll=2)
    steps(lambda i: (0, end - i), first_ref, start_ref, scaled_ref, pair_ref, margin)
    for e, value in enumerate(overlaps(pair_ref, 0, (end - FILTER + 1) * side * COL)):
        overlap_ref[e] = value


def basis_kernel(
    margin,
    x_after_ref,
    z_before_ref,
    z_after_ref,
    start_in,
    first_in,
    scaled_in,
    pair_in,
    overlap_ref,
    minus_x_ref,
    minus_z_ref,
    inverse_ref,
    start_ref,
    first_ref,
    scaled_ref,
    pair_ref,
    box_ref,
    matrix_ref,
    packed_ref,
):
    elements, columns = start_ref.shape[0], start_ref.shape[-1]
    side, y_points = scaled_ref.shape[:2]
    end = side - margin
    box_ref[...] = jnp.zeros_like(box_ref)
    box_ref[end:, margin : margin + G, :y_points] = x_after_ref[...]
    box_ref[end:, :margin, :y_points] = z_before_ref[...]
    box_ref[end:, margin + G : side, :y_points] = z_after_ref[...]
    for x in range(end, side):
        potential_part(x, box_ref, margin, scaled_ref, first_in, start_in, first_ref)
    field = steps(
        lambda i: (end - i, side), first_ref, start_ref, scaled_ref, pair_ref, margin
    )
    rest = overlaps(pair_ref, (end - FILTER + 1) * side * COL, side * side * COL)

    identity = (
        lax.broadcasted_iota(jnp.int32, (columns, columns), 0)
        == lax.broadcasted_iota(jnp.int32, (columns, columns), 1)
    ).astype(f32)
    grams = []
    for e in range(elements):
        products = overlap_ref[e] + rest[e]
        cross = products[:, columns:]
        grams.append(products[:, :columns] + (cross + cross.T))
    for e in range(0, elements, 2):
        pairs = [grams[e], grams[min(e + 1, elements - 1)]]
        for i, value in enumerate(pack(pairs) + pack([identity, identity])):
            matrix_ref[i] = value
        inverse_factors(matrix_ref, packed_ref)
        solved = pack([packed_ref[0], packed_ref[1]])
        for i in range(min(2, elements - e)):
            inverse_ref[e + i] = solved[i]

    for e in range(elements):
        held = weights(split(inverse_ref[e]), True)
        for d, ref in ((0, minus_x_ref), (2, minus_z_ref)):
            rows = layer(field, margin, e, d, 0) + layer(field, margin, e, d, 1)
            ref[e] = product(jnp.concatenate(rows, 0), held, True)


def near_kernel(
    count,
    margin,
    inverse_ref,
    field,
    scaled_ref,
    plus_ref,
    *rest,
):
    out_refs = rest[:count]
    inner_ref, applied_ref, near_ref = rest[count:]
    elements, columns = inverse_ref.shape[0], inverse_ref.shape[-1]
    y_points = scaled_ref.shape[1]

    z = lax.broadcasted_iota(jnp.int32, (G, columns), 0)
    edge = (z == 1) | (z == G - 1)
    weight_down = jnp.where(z == 0, 0.0, jnp.where(edge, 0.25, 0.5))
    edge = (z == 0) | (z == G - 2)
    weight_up = jnp.where(z == G - 1, 0.0, jnp.where(edge, 0.25, 0.5))

    def link(i):
        return 0.25 if i in (0, G - 2) else 0.5

    for e in range(elements):
        for x in range(G):
            for y in range(0, G, 2):
                inner_pair, applied_pair = [], []
                for yy in (y, y + 1):
                    here = point_rows(field, margin, e, x, yy)
                    potential = scaled_ref[margin + x, (e * G + yy) % y_points, margin : margin + G]
                    value = (0.5 * halfwidth * potential + center) * here
                    value = value - weight_down * pltpu.roll(here, 1, 0)
                    value = value - weight_up * pltpu.roll(here, G - 1, 0)
                    if x > 0:
                        value = value - link(x - 1) * point_rows(field, margin, e, x - 1, yy)
                    if x < G - 1:
                        value = value - link(x) * point_rows(field, margin, e, x + 1, yy)
                    if yy > 0:
                        value = value - link(yy - 1) * point_rows(field, margin, e, x, yy - 1)
                    if yy < G - 1:
                        value = value - link(yy) * point_rows(field, margin, e, x, yy + 1)
                    inner_pair.append(here)
                    applied_pair.append(value)
                at = slice((x * G + y) * G, (x * G + y + 2) * G)
                for ref, pair in ((inner_ref, inner_pair), (applied_ref, applied_pair)):
                    high, low = split(jnp.concatenate(pair, axis=0))
                    ref[e, at, :columns] = high
                    ref[e, at, columns:] = low

    face = 2 * G * G
    minus, plus, held = [], [], []
    for e in range(elements):
        held.append(weights(split(inverse_ref[e]), True))
        rows = layer(field, margin, e, 1, 0) + layer(field, margin, e, 1, 1)
        for d in range(3):
            last = layer(field, margin, e, d, G - 1)
            before = layer(field, margin, e, d, G - 2)
            rows += [-(0.5 * a + 0.25 * b) for a, b in zip(last, before)]
            rows += [-0.25 * a for a in last]
        faces = product(jnp.concatenate(rows, 0), held[e], True)
        minus.append(faces[:face])
        plus.append(faces[face : 2 * face].T)
        plus_ref[e, 0] = plus[e]
        plus[e] = faces[2 * face : 3 * face].T
        plus_ref[e, 1] = faces[3 * face :].T

    for e in range(elements):
        both = lax.dot_general(
            inner_ref[e, :, :columns],
            applied_ref[e],
            (((0,), (0,)), ((), ())),
            preferred_element_type=f32,
        )
        raw = both[:, :columns] + both[:, columns:]
        raw = raw + lax.dot_general(
            inner_ref[e, :, columns:],
            applied_ref[e, :, :columns],
            (((0,), (0,)), ((), ())),
            preferred_element_type=f32,
        )
        half = product(inverse_ref[e], weights(split(raw), False), False)
        near_ref[0, e] = product(half, held[e], True)
        following = weights(split(minus[(e + 1) % elements]), False)
        near_ref[1, e] = product(plus[e], following, False)
    send_rows(count, near_ref, out_refs)


def send_rows(count, blocks_ref, out_refs):
    kinds, elements, size = blocks_ref.shape[:3]
    rows = size // count
    me = lax.axis_index("ez")
    for step in range(count):
        at = pl.ds(pl.multiple_of(lax.rem(me + step, count) * rows, rows), rows)
        for kind in range(kinds):
            for e in range(elements):
                out_refs[step][:, elements * kind + e, :] = blocks_ref[kind, e, at, :]


def far_kernel(count, plus_ref, next_x_ref, next_z_ref, *rest):
    out_refs, far_ref = rest[:-1], rest[-1]
    for e in range(plus_ref.shape[0]):
        for d, ref in ((0, next_x_ref), (1, next_z_ref)):
            far_ref[d, e] = product(plus_ref[e, d], weights(split(ref[e]), False), False)
    send_rows(count, far_ref, out_refs)


def assemble_kernel(count, *refs):
    near_refs, far_refs = refs[:count], refs[count : 2 * count]
    diagonal_ref, coupling_ref = refs[2 * count :]
    elements = diagonal_ref.shape[2]
    me = lax.axis_index("ez")
    for step in range(count):
        z = lax.rem(me + (count - step), count)
        diagonal_ref[:, z] = near_refs[step][:, :elements]
        coupling_ref[:, z, 1] = near_refs[step][:, elements:]
        coupling_ref[:, z, 0] = far_refs[step][:, :elements]
        coupling_ref[:, z, 2] = far_refs[step][:, elements:]


def vmem(count):
    return [pl.BlockSpec(memory_space=pltpu.VMEM)] * count


def shift(block, axis, distance):
    count = lax.axis_size(axis)
    return lax.ppermute(block, axis, [(i, (i + distance) % count) for i in range(count)])


def local(potential, basis_start):
    elements, points, columns = basis_start.shape[2:]
    side = round(points ** (1 / 3))
    margin = (side - G) // 2
    y_points = potential.shape[1]
    count = lax.axis_size("ez")
    starts = basis_start.reshape(elements, points, columns)
    own = potential.transpose(0, 2, 1)
    own_scaled = lax.optimization_barrier((own + (3.0 - center)) * (2.0 / halfwidth))
    x_before = (shift(own, "ex", 1)[G - margin :] + (3.0 - center)) * (2.0 / halfwidth)
    x_after = shift(own_scaled[:margin], "ex", -1)

    shape = jax.ShapeDtypeStruct
    field = shape((elements, side + 2, LEAD + COL * side + LEAD, columns), f32)
    scaled = shape((side, y_points, COL, columns), f32)
    start, first = pl.pallas_call(
        first_kernel,
        out_shape=[field, field],
        in_specs=vmem(1),
        out_specs=vmem(2),
        scratch_shapes=[pltpu.VMEM((elements, side * side + COL, columns), f32)],
        compiler_params=pltpu.CompilerParams(vmem_limit_bytes=24 * 2**20),
        cost_estimate=pl.CostEstimate(flops=10**5, bytes_accessed=10**4, transcendentals=0),
        name="first",
    )(starts)
    low = lax.optimization_barrier(jnp.concatenate([x_before, own_scaled], axis=0))
    z_before = shift(low[:, G - margin :], "ez", 1)
    z_after = shift(low[:, :margin], "ez", -1)
    edge_before = shift(x_after[:, G - margin :], "ez", 1)
    edge_after = shift(x_after[:, :margin], "ez", -1)
    pair = shape((elements, side * side * COL, 2 * columns), bf16)
    overlap = shape((elements, columns, 2 * columns), f32)
    box = pltpu.VMEM((side, COL, 128), f32)
    start, first, most_scaled, pairs, overlapped = pl.pallas_call(
        functools.partial(middle_kernel, margin),
        out_shape=[field, field, scaled, pair, overlap],
        in_specs=vmem(5),
        out_specs=vmem(5),
        input_output_aliases={3: 0, 4: 1},
        scratch_shapes=[box],
        compiler_params=pltpu.CompilerParams(vmem_limit_bytes=32 * 2**20),
        cost_estimate=pl.CostEstimate(flops=10**8, bytes_accessed=10**7, transcendentals=0),
        name="middle",
    )(low, z_before, z_after, start, first)

    face = shape((elements, 2 * G * G, columns), f32)
    square = shape((elements, columns, columns), f32)
    minus_x, minus_z, inverse, _, filtered, whole_scaled, _ = pl.pallas_call(
        functools.partial(basis_kernel, margin),
        out_shape=[face, face, square, field, field, scaled, pair],
        in_specs=vmem(8),
        out_specs=vmem(7),
        input_output_aliases={3: 3, 4: 4, 5: 5, 6: 6},
        scratch_shapes=[
            box,
            pltpu.VMEM((4, columns, columns), f32),
            pltpu.VMEM((2, columns, columns), f32),
        ],
        compiler_params=pltpu.CompilerParams(vmem_limit_bytes=32 * 2**20),
        name="basis",
    )(x_after, edge_before, edge_after, start, first, most_scaled, pairs, overlapped)

    next_x = shift(minus_x, "ex", -1)
    next_z = shift(minus_z, "ez", -1)
    block = shape((columns // count, 2 * elements, columns), f32)
    plus, *near = pl.pallas_call(
        functools.partial(near_kernel, count, margin),
        out_shape=[shape((elements, 2, columns, 2 * G * G), f32)] + [block] * count,
        in_specs=vmem(3),
        out_specs=vmem(1 + count),
        scratch_shapes=[
            pltpu.VMEM((elements, G**3, 2 * columns), bf16),
            pltpu.VMEM((elements, G**3, 2 * columns), bf16),
            pltpu.VMEM((2, elements, columns, columns), f32),
        ],
        compiler_params=pltpu.CompilerParams(vmem_limit_bytes=24 * 2**20),
        cost_estimate=pl.CostEstimate(flops=10**8, bytes_accessed=10**7, transcendentals=0),
        name="near",
    )(inverse, filtered, whole_scaled)
    near = list(near[:1]) + [shift(near[step], "ez", step) for step in range(1, count)]

    far = pl.pallas_call(
        functools.partial(far_kernel, count),
        out_shape=[block] * count,
        in_specs=vmem(3),
        out_specs=vmem(count),
        scratch_shapes=[pltpu.VMEM((2, elements, columns, columns), f32)],
        compiler_params=pltpu.CompilerParams(vmem_limit_bytes=16 * 2**20),
        name="far",
    )(plus, next_x, next_z)
    far = list(far[:1]) + [shift(far[step], "ez", step) for step in range(1, count)]

    rows = columns // count
    diagonal, coupled = pl.pallas_call(
        functools.partial(assemble_kernel, count),
        out_shape=[
            shape((rows, count, elements, columns), f32),
            shape((rows, count, 3, elements, columns), f32),
        ],
        in_specs=vmem(2 * count),
        out_specs=vmem(2),
        compiler_params=pltpu.CompilerParams(vmem_limit_bytes=16 * 2**20),
        name="assemble",
    )(*near, *far)
    return (diagonal[None], coupled.transpose(0, 1, 3, 2, 4)[None])


def solution(mesh):
    return jax.shard_map(
        local,
        mesh=mesh,
        in_specs=(P("ex", None, "ez"), P("ex", "ez", None, None, None)),
        out_specs=(P("ex", "ez", None, None, None), P("ex", "ez", None, None, None, None)),
        check_vma=False,
    )
```

```python
import functools

import jax
import jax.numpy as jnp
from jax import lax
from jax.experimental import pallas as pl
from jax.experimental.pallas import tpu as pltpu
from jax.sharding import PartitionSpec as P

G = 8
FILTER = 3

center = 6.5
halfwidth = 5.5

f32 = jnp.float32
bf16 = jnp.bfloat16

LEAD = 8
AHEAD = 1
COL = 16
BLOCK = 16


def split(value):
    high = value.astype(bf16)
    return high, (value - high.astype(f32)).astype(bf16)


def weights(pair, transposed):
    high, low = pair
    empty = jnp.zeros_like(low)
    if transposed:
        upper = jnp.concatenate([high, high], axis=1)
        lower = jnp.concatenate([low, empty], axis=1)
        return jnp.concatenate([upper, lower], axis=0)
    upper = jnp.concatenate([high, low], axis=1)
    lower = jnp.concatenate([high, empty], axis=1)
    return jnp.concatenate([upper, lower], axis=0)


def product(value, held, transposed):
    pair = jnp.concatenate(split(value), axis=1)
    dims = (((1,), (1 if transposed else 0,)), ((), ()))
    both = lax.dot_general(pair, held, dims, preferred_element_type=f32)
    half = both.shape[1] // 2
    return both[:, :half] + both[:, half:]


def bcast_row(value, k):
    return jnp.broadcast_to(value[k : k + 1, :], value.shape)


def bcast_lane(value, k, lanes):
    return jnp.broadcast_to(value[:, k : k + 1], (value.shape[0], lanes))


def triple(value):
    high, rest = split(value)
    low = (value - high.astype(f32) - rest.astype(f32)).astype(bf16)
    return high, rest, low


def pack(values):
    first, second = values
    half = first.shape[1] // 2
    left = lax.broadcasted_iota(jnp.int32, first.shape, 1) < half
    return (
        jnp.where(left, first, pltpu.roll(second, half, 1)),
        jnp.where(left, pltpu.roll(first, half, 1), second),
    )


def tree_sum(terms):
    while len(terms) > 1:
        terms = [a + b for a, b in zip(terms[::2], terms[1::2])] + terms[len(terms) & ~1 :]
    return terms[0]


def inverse_factors(matrix_ref, inverse_ref):
    size = matrix_ref.shape[1]
    half = size // 2
    row = lax.broadcasted_iota(jnp.int32, (BLOCK, size), 0)
    lane = lax.broadcasted_iota(jnp.int32, (BLOCK, size), 1)
    other = jnp.where(lane < half, 0, half)

    def columns_of(value, at):
        return jnp.take_along_axis(value, other + at, axis=1)

    for top in (0, half):
        parts = (0, 1, 2) if top == 0 else (1, 2, 3)
        pivot_part = 0 if top == 0 else 1
        kept = []
        for start in range(top, top + half, BLOCK):
            rows = slice(start, start + BLOCK)
            panel = [matrix_ref[part, rows, :] for part in parts]
            at = start - top
            columns = [columns_of(panel[0], at + j) for j in range(BLOCK)]
            pivot_rows = list(panel)
            pivot = bcast_row(columns[0], 0)
            pivots = pivot
            for k in range(BLOCK):
                reciprocal = 1.0 / pivot
                if k > 0:
                    pivots = jnp.where(row >= k, pivot, pivots)
                    pivot_rows = [
                        jnp.where(row >= k, new, old) for new, old in zip(panel, pivot_rows)
                    ]
                if k + 1 < BLOCK:
                    beside = bcast_row(columns[k + 1], k)
                    pivot = bcast_row(columns[k + 1], k + 1) - (beside * beside) * reciprocal
                factor = jnp.where(row == k, 0.0, columns[k]) * reciprocal
                for j in range(k + 1, BLOCK):
                    columns[j] = columns[j] - factor * bcast_row(columns[j], k)
                panel = [value - factor * bcast_row(value, k) for value in panel]
            reciprocals = 1.0 / pivots
            solved = [value * reciprocals for value in panel]
            scale = lax.rsqrt(pivots)
            kept.append([value * scale for value in pivot_rows])
            inverse_ref[0, rows, :] = kept[-1][parts.index(2)]
            if 3 in parts:
                inverse_ref[1, rows, :] = kept[-1][parts.index(3)]
            else:
                inverse_ref[1, rows, :] = jnp.zeros((BLOCK, size), f32)
            for below in range(start + BLOCK, top + half, BLOCK):
                rows = slice(below, below + BLOCK)
                values = [matrix_ref[part, rows, :] for part in parts]
                factors = [columns_of(values[0], at + k) for k in range(BLOCK)]
                for part, value, taken in zip(parts, values, solved):
                    terms = [factors[k] * bcast_row(taken, k) for k in range(BLOCK)]
                    matrix_ref[part, rows, :] = value - tree_sum(terms)
        if top == 0:
            right = [jnp.concatenate([k[i] for k in kept], axis=0) for i in (1, 2)]
            left = triple(right[0])
            both = [jnp.concatenate(p, axis=1) for p in zip(left, triple(right[1]))]
            order = ((0, 0), (0, 1), (1, 0), (0, 2), (2, 0), (1, 1))
            taken = lax.dot_general(
                jnp.concatenate([left[i] for i, _ in order], axis=0),
                jnp.concatenate([both[j] for _, j in order], axis=0),
                (((0,), (0,)), ((), ())),
                preferred_element_type=f32,
            )
            is_left = lax.broadcasted_iota(jnp.int32, (half, size), 1) < half
            for i, part in enumerate((1, 2)):
                at = slice(size * i, size * (i + 1))
                mine = jnp.where(is_left, taken[:half, at], taken[half:, at])
                matrix_ref[part, half:, :] = matrix_ref[part, half:, :] - mine


def zero_ends(ref, elements, side):
    for e in range(elements):
        ref[e, 0] = jnp.zeros(ref.shape[2:], f32)
        ref[e, side + 1] = jnp.zeros(ref.shape[2:], f32)
        for x in range(side):
            ref[e, x + 1, :LEAD] = jnp.zeros((LEAD, ref.shape[-1]), f32)
            ref[e, x + 1, LEAD + COL * side :] = jnp.zeros((LEAD, ref.shape[-1]), f32)


def beside_weight(side, columns):
    inside = lax.broadcasted_iota(jnp.int32, (COL, columns), 0) < side
    return jnp.where(inside, 1.0 / halfwidth, 0.0)


def slab_step(x, source, scaled_ref, previous, target, pair_ref, margin):
    elements, side = source.shape[0], source.shape[1] - 2
    columns = source.shape[-1]
    weight = beside_weight(side, columns)
    if previous is None:
        weight = 0.5 * weight
    for e in range(elements):

        def column(y):
            return source[e, x + 1, LEAD + COL * y : LEAD + COL * (y + 1)]

        before, here = None, column(0)
        for y in range(side):
            low = LEAD + COL * y
            after = column(y + 1) if y + 1 < side else None
            beside = source[e, x, low : low + COL] + source[e, x + 2, low : low + COL]
            beside = beside + (
                source[e, x + 1, low - 1 : low - 1 + COL]
                + source[e, x + 1, low + 1 : low + 1 + COL]
            )
            if before is not None:
                beside = beside + before
            if after is not None:
                beside = beside + after
            if previous is None:
                value = -weight * beside
            else:
                scaled = scaled_ref[x, (e * G - margin + y) % scaled_ref.shape[1]]
                value = scaled * here - weight * beside - previous[e, x + 1, low : low + COL]
            target[e, x + 1, low : low + COL] = value
            if pair_ref is not None:
                high, rest = split(value)
                at = pl.multiple_of(x * (side * COL), COL) + COL * y
                pair_ref[e, pl.ds(at, COL), :columns] = high
                pair_ref[e, pl.ds(at, COL), columns:] = rest
            before, here = here, after


def first_kernel(start_ref, field_ref, first_ref, flat_ref):
    elements, columns = start_ref.shape[0], start_ref.shape[-1]
    side = field_ref.shape[1] - 2
    slab = side * side
    zero_ends(field_ref, elements, side)
    zero_ends(first_ref, elements, side)
    inside = lax.broadcasted_iota(jnp.int32, (COL, columns), 0) < side

    def prepare(x, carry):
        for e in range(elements):
            flat_ref[e, :slab] = start_ref[e, pl.ds(pl.multiple_of(x * slab, 16), slab), :].astype(f32)
            for y in range(side):
                value = jnp.where(inside, flat_ref[e, side * y : side * y + COL], 0.0)
                field_ref[e, x + 1, LEAD + COL * y : LEAD + COL * (y + 1)] = value
        return carry

    lax.fori_loop(0, side, prepare, 0)

    def step(x, carry):
        slab_step(x, field_ref, None, None, first_ref, None, 0)
        return carry

    lax.fori_loop(0, side, step, 0)


def point_rows(field, margin, e, x, y):
    low = LEAD + COL * (margin + y) + margin
    return field[e, margin + x + 1, low : low + G]


def layer(field, margin, e, d, i):
    if d == 0:
        return [point_rows(field, margin, e, i, y) for y in range(G)]
    if d == 1:
        return [point_rows(field, margin, e, x, i) for x in range(G)]
    low = LEAD + COL * margin + margin + i
    return [field[e, margin + x + 1, pl.ds(low, G, stride=COL)] for x in range(G)]


def potential_part(x, box_ref, margin, scaled_ref, first_in, start_in, first_ref):
    elements, columns = start_in.shape[0], start_in.shape[-1]
    side, y_points = scaled_ref.shape[:2]
    rows = box_ref[x]
    for y in range(y_points):
        scaled = bcast_lane(rows, y, columns)
        scaled_ref[x, y] = scaled
        scaled = 0.5 * scaled
        for e in range(elements):
            box_y = (y - e * G + margin) % y_points
            if box_y < side:
                at = slice(LEAD + COL * box_y, LEAD + COL * (box_y + 1))
                first_ref[e, x + 1, at] = first_in[e, x + 1, at] + scaled * start_in[e, x + 1, at]


def steps(ranges, first_ref, start_ref, scaled_ref, pair_ref, margin):
    fields = (first_ref, start_ref)
    for index in range(1, FILTER):
        source, target = fields
        pair = pair_ref if index == FILTER - 1 else None

        def next_step(x, carry):
            slab_step(x, source, scaled_ref, target, target, pair, margin)
            return carry

        lax.fori_loop(*ranges(index), next_step, 0, unroll=2)
        fields = fields[::-1]
    return fields[0]


def overlaps(pair_ref, low, high):
    columns = pair_ref.shape[-1] // 2
    return [
        lax.dot_general(
            pair_ref[e, low:high, :columns],
            pair_ref[e, low:high],
            (((0,), (0,)), ((), ())),
            preferred_element_type=f32,
        )
        for e in range(pair_ref.shape[0])
    ]


def middle_kernel(
    margin,
    low_ref,
    z_before_ref,
    z_after_ref,
    start_in,
    first_in,
    start_ref,
    first_ref,
    scaled_ref,
    pair_ref,
    overlap_ref,
    box_ref,
):
    side, y_points = scaled_ref.shape[:2]
    end = side - margin
    box_ref[...] = jnp.zeros_like(box_ref)
    box_ref[:end, margin : margin + G, :y_points] = low_ref[...]
    box_ref[:end, :margin, :y_points] = z_before_ref[...]
    box_ref[:end, margin + G : side, :y_points] = z_after_ref[...]

    def complete(x, carry):
        potential_part(x, box_ref, margin, scaled_ref, first_in, start_in, first_ref)
        return carry

    lax.fori_loop(0, end, complete, 0, unroll=2)
    steps(lambda i: (0, end - i), first_ref, start_ref, scaled_ref, pair_ref, margin)
    for e, value in enumerate(overlaps(pair_ref, 0, (end - FILTER + 1) * side * COL)):
        overlap_ref[e] = value


def basis_kernel(
    margin,
    x_after_ref,
    z_before_ref,
    z_after_ref,
    start_in,
    first_in,
    scaled_in,
    pair_in,
    overlap_ref,
    minus_x_ref,
    minus_z_ref,
    inverse_ref,
    start_ref,
    first_ref,
    scaled_ref,
    pair_ref,
    box_ref,
    matrix_ref,
    packed_ref,
):
    elements, columns = start_ref.shape[0], start_ref.shape[-1]
    side, y_points = scaled_ref.shape[:2]
    end = side - margin
    box_ref[...] = jnp.zeros_like(box_ref)
    box_ref[end:, margin : margin + G, :y_points] = x_after_ref[...]
    box_ref[end:, :margin, :y_points] = z_before_ref[...]
    box_ref[end:, margin + G : side, :y_points] = z_after_ref[...]
    for x in range(end, side):
        potential_part(x, box_ref, margin, scaled_ref, first_in, start_in, first_ref)
    field = steps(
        lambda i: (end - i, side), first_ref, start_ref, scaled_ref, pair_ref, margin
    )
    rest = overlaps(pair_ref, (end - FILTER + 1) * side * COL, side * side * COL)

    identity = (
        lax.broadcasted_iota(jnp.int32, (columns, columns), 0)
        == lax.broadcasted_iota(jnp.int32, (columns, columns), 1)
    ).astype(f32)
    grams = []
    for e in range(elements):
        products = overlap_ref[e] + rest[e]
        cross = products[:, columns:]
        grams.append(products[:, :columns] + (cross + cross.T))
    for e in range(0, elements, 2):
        pairs = [grams[e], grams[min(e + 1, elements - 1)]]
        for i, value in enumerate(pack(pairs) + pack([identity, identity])):
            matrix_ref[i] = value
        inverse_factors(matrix_ref, packed_ref)
        solved = pack([packed_ref[0], packed_ref[1]])
        for i in range(min(2, elements - e)):
            inverse_ref[e + i] = solved[i]

    for e in range(elements):
        held = weights(split(inverse_ref[e]), True)
        for d, ref in ((0, minus_x_ref), (2, minus_z_ref)):
            rows = layer(field, margin, e, d, 0) + layer(field, margin, e, d, 1)
            ref[e] = product(jnp.concatenate(rows, 0), held, True)


def near_kernel(
    count,
    margin,
    inverse_ref,
    field,
    scaled_ref,
    plus_ref,
    near_ref,
    *rest,
):
    *out_refs, inner_ref, applied_ref = rest
    elements, columns = inverse_ref.shape[0], inverse_ref.shape[-1]
    y_points = scaled_ref.shape[1]

    z = lax.broadcasted_iota(jnp.int32, (G, columns), 0)
    edge = (z == 1) | (z == G - 1)
    weight_down = jnp.where(z == 0, 0.0, jnp.where(edge, 0.25, 0.5))
    edge = (z == 0) | (z == G - 2)
    weight_up = jnp.where(z == G - 1, 0.0, jnp.where(edge, 0.25, 0.5))

    def link(i):
        return 0.25 if i in (0, G - 2) else 0.5

    for e in range(elements):
        for x in range(G):
            for y in range(0, G, 2):
                inner_pair, applied_pair = [], []
                for yy in (y, y + 1):
                    here = point_rows(field, margin, e, x, yy)
                    potential = scaled_ref[margin + x, (e * G + yy) % y_points, margin : margin + G]
                    value = (0.5 * halfwidth * potential + center) * here
                    value = value - weight_down * pltpu.roll(here, 1, 0)
                    value = value - weight_up * pltpu.roll(here, G - 1, 0)
                    if x > 0:
                        value = value - link(x - 1) * point_rows(field, margin, e, x - 1, yy)
                    if x < G - 1:
                        value = value - link(x) * point_rows(field, margin, e, x + 1, yy)
                    if yy > 0:
                        value = value - link(yy - 1) * point_rows(field, margin, e, x, yy - 1)
                    if yy < G - 1:
                        value = value - link(yy) * point_rows(field, margin, e, x, yy + 1)
                    inner_pair.append(here)
                    applied_pair.append(value)
                at = slice((x * G + y) * G, (x * G + y + 2) * G)
                for ref, pair in ((inner_ref, inner_pair), (applied_ref, applied_pair)):
                    high, low = split(jnp.concatenate(pair, axis=0))
                    ref[e, at, :columns] = high
                    ref[e, at, columns:] = low

    face = 2 * G * G
    minus, plus, held = [], [], []
    for e in range(elements):
        held.append(weights(split(inverse_ref[e]), True))
        rows = layer(field, margin, e, 1, 0) + layer(field, margin, e, 1, 1)
        for d in range(3):
            last = layer(field, margin, e, d, G - 1)
            before = layer(field, margin, e, d, G - 2)
            rows += [-(0.5 * a + 0.25 * b) for a, b in zip(last, before)]
            rows += [-0.25 * a for a in last]
        faces = product(jnp.concatenate(rows, 0), held[e], True)
        minus.append(faces[:face])
        plus.append(faces[face : 2 * face].T)
        plus_ref[e, 0] = plus[e]
        plus[e] = faces[2 * face : 3 * face].T
        plus_ref[e, 1] = faces[3 * face :].T

    for e in range(elements):
        both = lax.dot_general(
            inner_ref[e, :, :columns],
            applied_ref[e],
            (((0,), (0,)), ((), ())),
            preferred_element_type=f32,
        )
        raw = both[:, :columns] + both[:, columns:]
        raw = raw + lax.dot_general(
            inner_ref[e, :, columns:],
            applied_ref[e, :, :columns],
            (((0,), (0,)), ((), ())),
            preferred_element_type=f32,
        )
        half = product(inverse_ref[e], weights(split(raw), False), False)
        near_ref[0, e] = product(half, held[e], True)
        following = weights(split(minus[(e + 1) % elements]), False)
        near_ref[1, e] = product(plus[e], following, False)
    send_rows(count, [near_ref], out_refs, parted(count)[1])


def partner(index, step, count):
    return index ^ step if count & (count - 1) == 0 else (index + step) % count


def send_rows(count, sources, out_refs, steps):
    elements, size = sources[0].shape[1:3]
    rows = size // count
    me = lax.axis_index("ez")
    for out_ref, step in zip(out_refs, steps):
        owner = me ^ step if count & (count - 1) == 0 else lax.rem(me + step, count)
        at = pl.ds(pl.multiple_of(owner * rows, rows), rows)
        slot = 0
        for blocks_ref in sources:
            for kind in range(blocks_ref.shape[0]):
                for e in range(elements):
                    out_ref[:, slot, :] = blocks_ref[kind, e, at, :]
                    slot += 1


def far_kernel(count, plus_ref, next_x_ref, next_z_ref, near_ref, *rest):
    out_refs, far_ref = rest[:-1], rest[-1]
    for e in range(plus_ref.shape[0]):
        for d, ref in ((0, next_x_ref), (1, next_z_ref)):
            far_ref[d, e] = product(plus_ref[e, d], weights(split(ref[e]), False), False)
    whole, ahead = parted(count)
    send_rows(count, [near_ref, far_ref], out_refs[: len(whole)], whole)
    send_rows(count, [far_ref], out_refs[len(whole) :], ahead)


def parted(count):
    return [step for step in range(count) if step < AHEAD], [
        step for step in range(count) if step >= AHEAD
    ]


def assemble_kernel(count, *refs):
    whole, ahead = parted(count)
    whole_refs, refs = refs[: len(whole)], refs[len(whole) :]
    near_refs, refs = refs[: len(ahead)], refs[len(ahead) :]
    far_refs, (diagonal_ref, coupling_ref) = refs[: len(ahead)], refs[len(ahead) :]
    elements = diagonal_ref.shape[2]
    me = lax.axis_index("ez")

    def place(step, near_ref, far_ref, far_at):
        z = me ^ step if count & (count - 1) == 0 else lax.rem(me + (count - step), count)
        diagonal_ref[:, z] = near_ref[:, :elements]
        coupling_ref[:, z, 1] = near_ref[:, elements : 2 * elements]
        coupling_ref[:, z, 0] = far_ref[:, far_at : far_at + elements]
        coupling_ref[:, z, 2] = far_ref[:, far_at + elements : far_at + 2 * elements]

    for step, ref in zip(whole, whole_refs):
        place(step, ref, ref, 2 * elements)
    for step, near_ref, far_ref in zip(ahead, near_refs, far_refs):
        place(step, near_ref, far_ref, 0)


def vmem(count):
    return [pl.BlockSpec(memory_space=pltpu.VMEM)] * count


def shift(block, axis, distance):
    count = lax.axis_size(axis)
    return lax.ppermute(block, axis, [(i, (i + distance) % count) for i in range(count)])


def exchange(block, step):
    count = lax.axis_size("ez")
    if step == 0:
        return block
    return lax.ppermute(block, "ez", [(i, partner(i, step, count)) for i in range(count)])


def local(potential, basis_start):
    elements, points, columns = basis_start.shape[2:]
    side = round(points ** (1 / 3))
    margin = (side - G) // 2
    y_points = potential.shape[1]
    count = lax.axis_size("ez")
    starts = basis_start.reshape(elements, points, columns)
    own = potential.transpose(0, 2, 1)
    own_scaled = lax.optimization_barrier((own + (3.0 - center)) * (2.0 / halfwidth))
    x_before = (shift(own, "ex", 1)[G - margin :] + (3.0 - center)) * (2.0 / halfwidth)
    x_after = shift(own_scaled[:margin], "ex", -1)

    shape = jax.ShapeDtypeStruct
    field = shape((elements, side + 2, LEAD + COL * side + LEAD, columns), f32)
    scaled = shape((side, y_points, COL, columns), f32)
    start, first = pl.pallas_call(
        first_kernel,
        out_shape=[field, field],
        in_specs=vmem(1),
        out_specs=vmem(2),
        scratch_shapes=[pltpu.VMEM((elements, side * side + COL, columns), f32)],
        compiler_params=pltpu.CompilerParams(vmem_limit_bytes=24 * 2**20),
        cost_estimate=pl.CostEstimate(flops=10**5, bytes_accessed=10**4, transcendentals=0),
        name="first",
    )(starts)
    low = lax.optimization_barrier(jnp.concatenate([x_before, own_scaled], axis=0))
    z_before = shift(low[:, G - margin :], "ez", 1)
    z_after = shift(low[:, :margin], "ez", -1)
    edge_before = shift(x_after[:, G - margin :], "ez", 1)
    edge_after = shift(x_after[:, :margin], "ez", -1)
    pair = shape((elements, side * side * COL, 2 * columns), bf16)
    overlap = shape((elements, columns, 2 * columns), f32)
    box = pltpu.VMEM((side, COL, 128), f32)
    start, first, most_scaled, pairs, overlapped = pl.pallas_call(
        functools.partial(middle_kernel, margin),
        out_shape=[field, field, scaled, pair, overlap],
        in_specs=vmem(5),
        out_specs=vmem(5),
        input_output_aliases={3: 0, 4: 1},
        scratch_shapes=[box],
        compiler_params=pltpu.CompilerParams(vmem_limit_bytes=32 * 2**20),
        cost_estimate=pl.CostEstimate(flops=10**8, bytes_accessed=10**7, transcendentals=0),
        name="middle",
    )(low, z_before, z_after, start, first)

    face = shape((elements, 2 * G * G, columns), f32)
    square = shape((elements, columns, columns), f32)
    minus_x, minus_z, inverse, _, filtered, whole_scaled, _ = pl.pallas_call(
        functools.partial(basis_kernel, margin),
        out_shape=[face, face, square, field, field, scaled, pair],
        in_specs=vmem(8),
        out_specs=vmem(7),
        input_output_aliases={3: 3, 4: 4, 5: 5, 6: 6},
        scratch_shapes=[
            box,
            pltpu.VMEM((4, columns, columns), f32),
            pltpu.VMEM((2, columns, columns), f32),
        ],
        compiler_params=pltpu.CompilerParams(vmem_limit_bytes=32 * 2**20),
        name="basis",
    )(x_after, edge_before, edge_after, start, first, most_scaled, pairs, overlapped)

    next_x = shift(minus_x, "ex", -1)
    next_z = shift(minus_z, "ez", -1)
    whole, ahead = parted(count)
    block = shape((columns // count, 2 * elements, columns), f32)
    double = shape((columns // count, 4 * elements, columns), f32)
    squares = shape((2, elements, columns, columns), f32)
    plus, own_near, *near = pl.pallas_call(
        functools.partial(near_kernel, count, margin),
        out_shape=[shape((elements, 2, columns, 2 * G * G), f32), squares] + [block] * len(ahead),
        in_specs=vmem(3),
        out_specs=vmem(2 + len(ahead)),
        scratch_shapes=[
            pltpu.VMEM((elements, G**3, 2 * columns), bf16),
            pltpu.VMEM((elements, G**3, 2 * columns), bf16),
        ],
        compiler_params=pltpu.CompilerParams(vmem_limit_bytes=24 * 2**20),
        cost_estimate=pl.CostEstimate(flops=10**8, bytes_accessed=10**7, transcendentals=0),
        name="near",
    )(inverse, filtered, whole_scaled)
    near = [exchange(value, step) for value, step in zip(near, ahead)]

    far = pl.pallas_call(
        functools.partial(far_kernel, count),
        out_shape=[double] * len(whole) + [block] * len(ahead),
        in_specs=vmem(4),
        out_specs=vmem(count),
        scratch_shapes=[pltpu.VMEM(squares.shape, f32)],
        compiler_params=pltpu.CompilerParams(vmem_limit_bytes=16 * 2**20),
        name="far",
    )(plus, next_x, next_z, own_near)
    far = [exchange(value, step) for value, step in zip(far, whole + ahead)]

    rows = columns // count
    diagonal, coupled = pl.pallas_call(
        functools.partial(assemble_kernel, count),
        out_shape=[
            shape((rows, count, elements, columns), f32),
            shape((rows, count, 3, elements, columns), f32),
        ],
        in_specs=vmem(len(whole) + 2 * len(ahead)),
        out_specs=vmem(2),
        compiler_params=pltpu.CompilerParams(vmem_limit_bytes=16 * 2**20),
        name="assemble",
    )(*far[: len(whole)], *near, *far[len(whole) :])
    return (diagonal[None], coupled.transpose(0, 1, 3, 2, 4)[None])


def solution(mesh):
    return jax.shard_map(
        local,
        mesh=mesh,
        in_specs=(P("ex", None, "ez"), P("ex", "ez", None, None, None)),
        out_specs=(P("ex", "ez", None, None, None), P("ex", "ez", None, None, None, None)),
        check_vma=False,
    )
```

```python
import functools

import jax
import jax.numpy as jnp
from jax import lax
from jax.experimental import pallas as pl
from jax.experimental.pallas import tpu as pltpu
from jax.sharding import PartitionSpec as P

G = 8
FILTER = 3

center = 6.5
halfwidth = 5.5

f32 = jnp.float32
bf16 = jnp.bfloat16

LEAD = 8
AHEAD = 1
COL = 16
BLOCK = 16


def split(value):
    high = value.astype(bf16)
    return high, (value - high.astype(f32)).astype(bf16)


def weights(pair, transposed):
    high, low = pair
    empty = jnp.zeros_like(low)
    if transposed:
        upper = jnp.concatenate([high, high], axis=1)
        lower = jnp.concatenate([low, empty], axis=1)
        return jnp.concatenate([upper, lower], axis=0)
    upper = jnp.concatenate([high, low], axis=1)
    lower = jnp.concatenate([high, empty], axis=1)
    return jnp.concatenate([upper, lower], axis=0)


def product(value, held, transposed):
    pair = jnp.concatenate(split(value), axis=1)
    dims = (((1,), (1 if transposed else 0,)), ((), ()))
    both = lax.dot_general(pair, held, dims, preferred_element_type=f32)
    half = both.shape[1] // 2
    return both[:, :half] + both[:, half:]


def bcast_row(value, k):
    return jnp.broadcast_to(value[k : k + 1, :], value.shape)


def bcast_lane(value, k, lanes):
    return jnp.broadcast_to(value[:, k : k + 1], (value.shape[0], lanes))


def pack(values):
    first, second = values
    half = first.shape[1] // 2
    left = lax.broadcasted_iota(jnp.int32, first.shape, 1) < half
    return (
        jnp.where(left, first, pltpu.roll(second, half, 1)),
        jnp.where(left, pltpu.roll(first, half, 1), second),
    )


def tree_sum(terms):
    while len(terms) > 1:
        terms = [a + b for a, b in zip(terms[::2], terms[1::2])] + terms[len(terms) & ~1 :]
    return terms[0]


def triple(value):
    high = value.astype(bf16).astype(f32)
    middle = (value - high).astype(bf16).astype(f32)
    return high, middle, value - high - middle


def far_rows(value, solved, at):
    size = value.shape[1]
    half = size // 2
    lane = lax.broadcasted_iota(jnp.int32, value.shape, 1) % half
    parts = triple(jnp.where((lane >= at) & (lane < at + BLOCK), value, 0.0))
    left = lax.broadcasted_iota(jnp.int32, (BLOCK, size), 1) < half
    taken = [[], []]
    for part in solved:
        pieces = triple(part)
        taken[0].append([jnp.where(left, piece, 0.0).astype(bf16) for piece in pieces])
        taken[1].append([jnp.where(left, 0.0, piece).astype(bf16) for piece in pieces])
    nothing = jnp.zeros((BLOCK, size * len(solved)), bf16)
    spots = half // BLOCK
    pairs = ((0, 0), (0, 1), (1, 0), (0, 2), (2, 0), (1, 1))
    operands, tiles = [], []
    for first in range(0, len(pairs), spots):
        operand, group = None, [nothing] * (2 * spots)
        for i, (mine, theirs) in enumerate(pairs[first : first + spots]):
            moved = pltpu.roll(parts[mine], i * BLOCK, 1) if i else parts[mine]
            operand = moved if operand is None else operand + moved
            for side in range(2):
                spot = (side * spots + at // BLOCK + i) % (2 * spots)
                group[spot] = jnp.concatenate([t[theirs] for t in taken[side]], axis=1)
        operands.append(operand.astype(bf16))
        tiles += group
    return jnp.dot(
        jnp.concatenate(operands, axis=1),
        jnp.concatenate(tiles, axis=0),
        preferred_element_type=f32,
    )


def inverse_factors(matrix_ref, inverse_ref):
    size = matrix_ref.shape[1]
    half = size // 2
    row = lax.broadcasted_iota(jnp.int32, (BLOCK, size), 0)
    lane = lax.broadcasted_iota(jnp.int32, (BLOCK, size), 1)
    other = jnp.where(lane < half, 0, half)

    def columns_of(value, at):
        return jnp.take_along_axis(value, other + at, axis=1)

    parts = (0, 1, 2)
    panel = [matrix_ref[part, :BLOCK, :] for part in parts]
    columns = [columns_of(panel[0], j) for j in range(BLOCK)]
    for start in range(0, size, BLOCK):
        rows = slice(start, start + BLOCK)
        at = start % half
        pivot_rows = list(panel)
        pivot = bcast_row(columns[0], 0)
        for k in range(BLOCK):
            reciprocal = 1.0 / pivot
            if k == 0:
                pivots, reciprocals = pivot, reciprocal
            else:
                later = row >= k
                pivots = jnp.where(later, pivot, pivots)
                reciprocals = jnp.where(later, reciprocal, reciprocals)
                pivot_rows = [jnp.where(later, new, old) for new, old in zip(panel, pivot_rows)]
            if k + 1 < BLOCK:
                beside = bcast_row(columns[k + 1], k)
                pivot = bcast_row(columns[k + 1], k + 1) - (beside * beside) * reciprocal
            factor = jnp.where(row == k, 0.0, columns[k]) * reciprocal
            for j in range(k + 1, BLOCK):
                columns[j] = columns[j] - factor * bcast_row(columns[j], k)
            panel = [value - factor * bcast_row(value, k) for value in panel]
        solved = [value * reciprocals for value in panel]
        scale = lax.rsqrt(pivots)
        kept = [value * scale for value in pivot_rows]
        inverse_ref[0, rows, :] = kept[parts.index(2)]
        inverse_ref[1, rows, :] = kept[parts.index(3)] if 3 in parts else jnp.zeros_like(scale)
        below = start + BLOCK
        if below == size:
            break
        values = [matrix_ref[part, below : below + BLOCK, :] for part in parts]
        factors = [columns_of(values[0], at + k) for k in range(BLOCK)]
        panel = []
        for value, taken in zip(values, solved):
            terms = [factors[k] * bcast_row(taken, k) for k in range(BLOCK)]
            panel.append(value - tree_sum(terms))
        if below == half:
            panel = panel[1:] + [matrix_ref[3, below : below + BLOCK, :]]
        columns = [columns_of(panel[0], below % half + j) for j in range(BLOCK)]
        rest = slice(below + BLOCK, size)
        if below + BLOCK < size:
            taken = far_rows(matrix_ref[parts[0], rest, :], solved, at)
            for i, part in enumerate(parts):
                mine = taken[:, i * size : (i + 1) * size]
                matrix_ref[part, rest, :] = matrix_ref[part, rest, :] - mine
        if below == half:
            parts = (1, 2, 3)


def zero_ends(ref, elements, side):
    for e in range(elements):
        ref[e, 0] = jnp.zeros(ref.shape[2:], f32)
        ref[e, side + 1] = jnp.zeros(ref.shape[2:], f32)
        for x in range(side):
            ref[e, x + 1, :LEAD] = jnp.zeros((LEAD, ref.shape[-1]), f32)
            ref[e, x + 1, LEAD + COL * side :] = jnp.zeros((LEAD, ref.shape[-1]), f32)


def beside_weight(side, columns):
    inside = lax.broadcasted_iota(jnp.int32, (COL, columns), 0) < side
    return jnp.where(inside, 1.0 / halfwidth, 0.0)


def slab_step(x, source, scaled_ref, previous, target, pair_ref, margin):
    elements, side = source.shape[0], source.shape[1] - 2
    columns = source.shape[-1]
    weight = beside_weight(side, columns)
    if previous is None:
        weight = 0.5 * weight
    for e in range(elements):

        def column(y):
            return source[e, x + 1, LEAD + COL * y : LEAD + COL * (y + 1)]

        before, here = None, column(0)
        for y in range(side):
            low = LEAD + COL * y
            after = column(y + 1) if y + 1 < side else None
            beside = source[e, x, low : low + COL] + source[e, x + 2, low : low + COL]
            beside = beside + (
                source[e, x + 1, low - 1 : low - 1 + COL]
                + source[e, x + 1, low + 1 : low + 1 + COL]
            )
            if before is not None:
                beside = beside + before
            if after is not None:
                beside = beside + after
            if previous is None:
                value = -weight * beside
            else:
                scaled = scaled_ref[x, (e * G - margin + y) % scaled_ref.shape[1]]
                value = scaled * here - weight * beside - previous[e, x + 1, low : low + COL]
            target[e, x + 1, low : low + COL] = value
            if pair_ref is not None:
                high, rest = split(value)
                at = pl.multiple_of(x * (side * COL), COL) + COL * y
                pair_ref[e, pl.ds(at, COL), :columns] = high
                pair_ref[e, pl.ds(at, COL), columns:] = rest
            before, here = here, after


def first_kernel(start_ref, field_ref, first_ref, flat_ref):
    elements, columns = start_ref.shape[0], start_ref.shape[-1]
    side = field_ref.shape[1] - 2
    slab = side * side
    zero_ends(field_ref, elements, side)
    zero_ends(first_ref, elements, side)
    inside = lax.broadcasted_iota(jnp.int32, (COL, columns), 0) < side

    def prepare(x, carry):
        for e in range(elements):
            flat_ref[e, :slab] = start_ref[e, pl.ds(pl.multiple_of(x * slab, 16), slab), :].astype(f32)
            for y in range(side):
                value = jnp.where(inside, flat_ref[e, side * y : side * y + COL], 0.0)
                field_ref[e, x + 1, LEAD + COL * y : LEAD + COL * (y + 1)] = value
        return carry

    lax.fori_loop(0, side, prepare, 0)

    def step(x, carry):
        slab_step(x, field_ref, None, None, first_ref, None, 0)
        return carry

    lax.fori_loop(0, side, step, 0)


def point_rows(field, margin, e, x, y):
    low = LEAD + COL * (margin + y) + margin
    return field[e, margin + x + 1, low : low + G]


def layer(field, margin, e, d, i):
    if d == 0:
        return [point_rows(field, margin, e, i, y) for y in range(G)]
    if d == 1:
        return [point_rows(field, margin, e, x, i) for x in range(G)]
    low = LEAD + COL * margin + margin + i
    return [field[e, margin + x + 1, pl.ds(low, G, stride=COL)] for x in range(G)]


def potential_part(x, box_ref, margin, scaled_ref, first_in, start_in, first_ref):
    elements, columns = start_in.shape[0], start_in.shape[-1]
    side, y_points = scaled_ref.shape[:2]
    rows = box_ref[x]
    for y in range(y_points):
        scaled = bcast_lane(rows, y, columns)
        scaled_ref[x, y] = scaled
        scaled = 0.5 * scaled
        for e in range(elements):
            box_y = (y - e * G + margin) % y_points
            if box_y < side:
                at = slice(LEAD + COL * box_y, LEAD + COL * (box_y + 1))
                first_ref[e, x + 1, at] = first_in[e, x + 1, at] + scaled * start_in[e, x + 1, at]


def steps(ranges, first_ref, start_ref, scaled_ref, pair_ref, margin):
    fields = (first_ref, start_ref)
    for index in range(1, FILTER):
        source, target = fields
        pair = pair_ref if index == FILTER - 1 else None

        def next_step(x, carry):
            slab_step(x, source, scaled_ref, target, target, pair, margin)
            return carry

        lax.fori_loop(*ranges(index), next_step, 0, unroll=2)
        fields = fields[::-1]
    return fields[0]


def overlaps(pair_ref, low, high):
    columns = pair_ref.shape[-1] // 2
    return [
        lax.dot_general(
            pair_ref[e, low:high, :columns],
            pair_ref[e, low:high],
            (((0,), (0,)), ((), ())),
            preferred_element_type=f32,
        )
        for e in range(pair_ref.shape[0])
    ]


def middle_kernel(
    margin,
    low_ref,
    z_before_ref,
    z_after_ref,
    start_in,
    first_in,
    start_ref,
    first_ref,
    scaled_ref,
    pair_ref,
    overlap_ref,
    box_ref,
):
    side, y_points = scaled_ref.shape[:2]
    end = side - margin
    box_ref[...] = jnp.zeros_like(box_ref)
    box_ref[:end, margin : margin + G, :y_points] = low_ref[...]
    box_ref[:end, :margin, :y_points] = z_before_ref[...]
    box_ref[:end, margin + G : side, :y_points] = z_after_ref[...]

    def complete(x, carry):
        potential_part(x, box_ref, margin, scaled_ref, first_in, start_in, first_ref)
        return carry

    lax.fori_loop(0, end, complete, 0, unroll=2)
    steps(lambda i: (0, end - i), first_ref, start_ref, scaled_ref, pair_ref, margin)
    for e, value in enumerate(overlaps(pair_ref, 0, (end - FILTER + 1) * side * COL)):
        overlap_ref[e] = value


def basis_kernel(
    margin,
    x_after_ref,
    z_before_ref,
    z_after_ref,
    start_in,
    first_in,
    scaled_in,
    pair_in,
    overlap_ref,
    minus_x_ref,
    minus_z_ref,
    inverse_ref,
    start_ref,
    first_ref,
    scaled_ref,
    pair_ref,
    box_ref,
    matrix_ref,
    packed_ref,
):
    elements, columns = start_ref.shape[0], start_ref.shape[-1]
    side, y_points = scaled_ref.shape[:2]
    end = side - margin
    box_ref[...] = jnp.zeros_like(box_ref)
    box_ref[end:, margin : margin + G, :y_points] = x_after_ref[...]
    box_ref[end:, :margin, :y_points] = z_before_ref[...]
    box_ref[end:, margin + G : side, :y_points] = z_after_ref[...]
    for x in range(end, side):
        potential_part(x, box_ref, margin, scaled_ref, first_in, start_in, first_ref)
    field = steps(
        lambda i: (end - i, side), first_ref, start_ref, scaled_ref, pair_ref, margin
    )
    rest = overlaps(pair_ref, (end - FILTER + 1) * side * COL, side * side * COL)

    identity = (
        lax.broadcasted_iota(jnp.int32, (columns, columns), 0)
        == lax.broadcasted_iota(jnp.int32, (columns, columns), 1)
    ).astype(f32)
    grams = []
    for e in range(elements):
        products = overlap_ref[e] + rest[e]
        cross = products[:, columns:]
        grams.append(products[:, :columns] + (cross + cross.T))
    for e in range(0, elements, 2):
        pairs = [grams[e], grams[min(e + 1, elements - 1)]]
        for i, value in enumerate(pack(pairs) + pack([identity, identity])):
            matrix_ref[i] = value
        inverse_factors(matrix_ref, packed_ref)
        solved = pack([packed_ref[0], packed_ref[1]])
        for i in range(min(2, elements - e)):
            inverse_ref[e + i] = solved[i]

    for e in range(elements):
        held = weights(split(inverse_ref[e]), True)
        rows = []
        for d in (0, 2):
            rows += layer(field, margin, e, d, 0) + layer(field, margin, e, d, 1)
        faces = product(jnp.concatenate(rows, 0), held, True)
        minus_x_ref[e] = faces[: 2 * G * G]
        minus_z_ref[e] = faces[2 * G * G :]


def near_kernel(
    count,
    margin,
    inverse_ref,
    field,
    scaled_ref,
    plus_ref,
    near_ref,
    *rest,
):
    *out_refs, inner_ref, applied_ref = rest
    elements, columns = inverse_ref.shape[0], inverse_ref.shape[-1]
    y_points = scaled_ref.shape[1]

    z = lax.broadcasted_iota(jnp.int32, (G, columns), 0)
    edge = (z == 1) | (z == G - 1)
    weight_down = jnp.where(z == 0, 0.0, jnp.where(edge, 0.25, 0.5))
    edge = (z == 0) | (z == G - 2)
    weight_up = jnp.where(z == G - 1, 0.0, jnp.where(edge, 0.25, 0.5))

    def link(i):
        return 0.25 if i in (0, G - 2) else 0.5

    for e in range(elements):
        for x in range(G):
            for y in range(0, G, 2):
                inner_pair, applied_pair = [], []
                for yy in (y, y + 1):
                    here = point_rows(field, margin, e, x, yy)
                    potential = scaled_ref[margin + x, (e * G + yy) % y_points, margin : margin + G]
                    value = (0.5 * halfwidth * potential + center) * here
                    value = value - weight_down * pltpu.roll(here, 1, 0)
                    value = value - weight_up * pltpu.roll(here, G - 1, 0)
                    if x > 0:
                        value = value - link(x - 1) * point_rows(field, margin, e, x - 1, yy)
                    if x < G - 1:
                        value = value - link(x) * point_rows(field, margin, e, x + 1, yy)
                    if yy > 0:
                        value = value - link(yy - 1) * point_rows(field, margin, e, x, yy - 1)
                    if yy < G - 1:
                        value = value - link(yy) * point_rows(field, margin, e, x, yy + 1)
                    inner_pair.append(here)
                    applied_pair.append(value)
                at = slice((x * G + y) * G, (x * G + y + 2) * G)
                for ref, pair in ((inner_ref, inner_pair), (applied_ref, applied_pair)):
                    high, low = split(jnp.concatenate(pair, axis=0))
                    ref[e, at, :columns] = high
                    ref[e, at, columns:] = low

    face = 2 * G * G
    minus, plus, held = [], [], []
    for e in range(elements):
        held.append(weights(split(inverse_ref[e]), True))
        rows = layer(field, margin, e, 1, 0) + layer(field, margin, e, 1, 1)
        for d in range(3):
            last = layer(field, margin, e, d, G - 1)
            before = layer(field, margin, e, d, G - 2)
            rows += [-(0.5 * a + 0.25 * b) for a, b in zip(last, before)]
            rows += [-0.25 * a for a in last]
        faces = product(jnp.concatenate(rows, 0), held[e], True)
        minus.append(faces[:face])
        plus.append(faces[face : 2 * face].T)
        plus_ref[e, 0] = plus[e]
        plus[e] = faces[2 * face : 3 * face].T
        plus_ref[e, 1] = faces[3 * face :].T

    for e in range(elements):
        both = lax.dot_general(
            inner_ref[e, :, :columns],
            applied_ref[e],
            (((0,), (0,)), ((), ())),
            preferred_element_type=f32,
        )
        raw = both[:, :columns] + both[:, columns:]
        raw = raw + lax.dot_general(
            inner_ref[e, :, columns:],
            applied_ref[e, :, :columns],
            (((0,), (0,)), ((), ())),
            preferred_element_type=f32,
        )
        half = product(inverse_ref[e], weights(split(raw), False), False)
        near_ref[0, e] = product(half, held[e], True)
        following = weights(split(minus[(e + 1) % elements]), False)
        near_ref[1, e] = product(plus[e], following, False)
    send_rows(count, [near_ref], out_refs, parted(count)[1])


def partner(index, step, count):
    return index ^ step if count & (count - 1) == 0 else (index + step) % count


def send_rows(count, sources, out_refs, steps):
    elements, size = sources[0].shape[1:3]
    rows = size // count
    me = lax.axis_index("ez")
    for out_ref, step in zip(out_refs, steps):
        owner = me ^ step if count & (count - 1) == 0 else lax.rem(me + step, count)
        at = pl.ds(pl.multiple_of(owner * rows, rows), rows)
        slot = 0
        for blocks_ref in sources:
            for kind in range(blocks_ref.shape[0]):
                for e in range(elements):
                    out_ref[:, slot, :] = blocks_ref[kind, e, at, :]
                    slot += 1


def far_kernel(count, plus_ref, next_x_ref, next_z_ref, near_ref, *rest):
    out_refs, far_ref = rest[:-1], rest[-1]
    for e in range(plus_ref.shape[0]):
        for d, ref in ((0, next_x_ref), (1, next_z_ref)):
            far_ref[d, e] = product(plus_ref[e, d], weights(split(ref[e]), False), False)
    whole, ahead = parted(count)
    send_rows(count, [near_ref, far_ref], out_refs[: len(whole)], whole)
    send_rows(count, [far_ref], out_refs[len(whole) :], ahead)


def parted(count):
    return [step for step in range(count) if step < AHEAD], [
        step for step in range(count) if step >= AHEAD
    ]


def assemble_kernel(count, *refs):
    whole, ahead = parted(count)
    whole_refs, refs = refs[: len(whole)], refs[len(whole) :]
    near_refs, refs = refs[: len(ahead)], refs[len(ahead) :]
    far_refs, (diagonal_ref, coupling_ref) = refs[: len(ahead)], refs[len(ahead) :]
    elements = diagonal_ref.shape[2]
    me = lax.axis_index("ez")

    def place(step, near_ref, far_ref, far_at):
        z = me ^ step if count & (count - 1) == 0 else lax.rem(me + (count - step), count)
        diagonal_ref[:, z] = near_ref[:, :elements]
        coupling_ref[:, z, 1] = near_ref[:, elements : 2 * elements]
        coupling_ref[:, z, 0] = far_ref[:, far_at : far_at + elements]
        coupling_ref[:, z, 2] = far_ref[:, far_at + elements : far_at + 2 * elements]

    for step, ref in zip(whole, whole_refs):
        place(step, ref, ref, 2 * elements)
    for step, near_ref, far_ref in zip(ahead, near_refs, far_refs):
        place(step, near_ref, far_ref, 0)


def vmem(count):
    return [pl.BlockSpec(memory_space=pltpu.VMEM)] * count


def shift(block, axis, distance):
    count = lax.axis_size(axis)
    return lax.ppermute(block, axis, [(i, (i + distance) % count) for i in range(count)])


def exchange(block, step):
    count = lax.axis_size("ez")
    if step == 0:
        return block
    return lax.ppermute(block, "ez", [(i, partner(i, step, count)) for i in range(count)])


def local(potential, basis_start):
    elements, points, columns = basis_start.shape[2:]
    side = round(points ** (1 / 3))
    margin = (side - G) // 2
    y_points = potential.shape[1]
    count = lax.axis_size("ez")
    starts = basis_start.reshape(elements, points, columns)
    own = potential.transpose(0, 2, 1)
    own_scaled = lax.optimization_barrier((own + (3.0 - center)) * (2.0 / halfwidth))
    x_before = (shift(own, "ex", 1)[G - margin :] + (3.0 - center)) * (2.0 / halfwidth)
    x_after = shift(own_scaled[:margin], "ex", -1)

    shape = jax.ShapeDtypeStruct
    field = shape((elements, side + 2, LEAD + COL * side + LEAD, columns), f32)
    scaled = shape((side, y_points, COL, columns), f32)
    start, first = pl.pallas_call(
        first_kernel,
        out_shape=[field, field],
        in_specs=vmem(1),
        out_specs=vmem(2),
        scratch_shapes=[pltpu.VMEM((elements, side * side + COL, columns), f32)],
        compiler_params=pltpu.CompilerParams(vmem_limit_bytes=24 * 2**20),
        cost_estimate=pl.CostEstimate(flops=10**5, bytes_accessed=10**4, transcendentals=0),
        name="first",
    )(starts)
    low = lax.optimization_barrier(jnp.concatenate([x_before, own_scaled], axis=0))
    z_before = shift(low[:, G - margin :], "ez", 1)
    z_after = shift(low[:, :margin], "ez", -1)
    edge_before = shift(x_after[:, G - margin :], "ez", 1)
    edge_after = shift(x_after[:, :margin], "ez", -1)
    pair = shape((elements, side * side * COL, 2 * columns), bf16)
    overlap = shape((elements, columns, 2 * columns), f32)
    box = pltpu.VMEM((side, COL, 128), f32)
    start, first, most_scaled, pairs, overlapped = pl.pallas_call(
        functools.partial(middle_kernel, margin),
        out_shape=[field, field, scaled, pair, overlap],
        in_specs=vmem(5),
        out_specs=vmem(5),
        input_output_aliases={3: 0, 4: 1},
        scratch_shapes=[box],
        compiler_params=pltpu.CompilerParams(vmem_limit_bytes=32 * 2**20),
        cost_estimate=pl.CostEstimate(flops=10**8, bytes_accessed=10**7, transcendentals=0),
        name="middle",
    )(low, z_before, z_after, start, first)

    face = shape((elements, 2 * G * G, columns), f32)
    square = shape((elements, columns, columns), f32)
    minus_x, minus_z, inverse, _, filtered, whole_scaled, _ = pl.pallas_call(
        functools.partial(basis_kernel, margin),
        out_shape=[face, face, square, field, field, scaled, pair],
        in_specs=vmem(8),
        out_specs=vmem(7),
        input_output_aliases={3: 3, 4: 4, 5: 5, 6: 6},
        scratch_shapes=[
            box,
            pltpu.VMEM((4, columns, columns), f32),
            pltpu.VMEM((2, columns, columns), f32),
        ],
        compiler_params=pltpu.CompilerParams(vmem_limit_bytes=32 * 2**20),
        name="basis",
    )(x_after, edge_before, edge_after, start, first, most_scaled, pairs, overlapped)

    next_x = shift(minus_x, "ex", -1)
    next_z = shift(minus_z, "ez", -1)
    whole, ahead = parted(count)
    block = shape((columns // count, 2 * elements, columns), f32)
    double = shape((columns // count, 4 * elements, columns), f32)
    squares = shape((2, elements, columns, columns), f32)
    plus, own_near, *near = pl.pallas_call(
        functools.partial(near_kernel, count, margin),
        out_shape=[shape((elements, 2, columns, 2 * G * G), f32), squares] + [block] * len(ahead),
        in_specs=vmem(3),
        out_specs=vmem(2 + len(ahead)),
        scratch_shapes=[
            pltpu.VMEM((elements, G**3, 2 * columns), bf16),
            pltpu.VMEM((elements, G**3, 2 * columns), bf16),
        ],
        compiler_params=pltpu.CompilerParams(vmem_limit_bytes=24 * 2**20),
        cost_estimate=pl.CostEstimate(flops=10**8, bytes_accessed=10**7, transcendentals=0),
        name="near",
    )(inverse, filtered, whole_scaled)
    near = [exchange(value, step) for value, step in zip(near, ahead)]

    far = pl.pallas_call(
        functools.partial(far_kernel, count),
        out_shape=[double] * len(whole) + [block] * len(ahead),
        in_specs=vmem(4),
        out_specs=vmem(count),
        scratch_shapes=[pltpu.VMEM(squares.shape, f32)],
        compiler_params=pltpu.CompilerParams(vmem_limit_bytes=16 * 2**20),
        name="far",
    )(plus, next_x, next_z, own_near)
    far = [exchange(value, step) for value, step in zip(far, whole + ahead)]

    rows = columns // count
    diagonal, coupled = pl.pallas_call(
        functools.partial(assemble_kernel, count),
        out_shape=[
            shape((rows, count, elements, columns), f32),
            shape((rows, count, 3, elements, columns), f32),
        ],
        in_specs=vmem(len(whole) + 2 * len(ahead)),
        out_specs=vmem(2),
        compiler_params=pltpu.CompilerParams(vmem_limit_bytes=16 * 2**20),
        name="assemble",
    )(*far[: len(whole)], *near, *far[len(whole) :])
    return (diagonal[None], coupled.transpose(0, 1, 3, 2, 4)[None])


def solution(mesh):
    return jax.shard_map(
        local,
        mesh=mesh,
        in_specs=(P("ex", None, "ez"), P("ex", "ez", None, None, None)),
        out_specs=(P("ex", "ez", None, None, None), P("ex", "ez", None, None, None, None)),
        check_vma=False,
    )
```

```python
import functools

import jax
import jax.numpy as jnp
from jax import lax
from jax.experimental import pallas as pl
from jax.experimental.pallas import tpu as pltpu
from jax.sharding import PartitionSpec as P

G = 8
FILTER = 3

center = 6.5
halfwidth = 5.5

f32 = jnp.float32
bf16 = jnp.bfloat16

LEAD = 8
AHEAD = 1
COL = 16
BLOCK = 16


def split(value):
    high = value.astype(bf16)
    return high, (value - high.astype(f32)).astype(bf16)


def weights(pair, transposed):
    high, low = pair
    empty = jnp.zeros_like(low)
    if transposed:
        upper = jnp.concatenate([high, high], axis=1)
        lower = jnp.concatenate([low, empty], axis=1)
        return jnp.concatenate([upper, lower], axis=0)
    upper = jnp.concatenate([high, low], axis=1)
    lower = jnp.concatenate([high, empty], axis=1)
    return jnp.concatenate([upper, lower], axis=0)


def product(value, held, transposed):
    pair = jnp.concatenate(split(value), axis=1)
    dims = (((1,), (1 if transposed else 0,)), ((), ()))
    both = lax.dot_general(pair, held, dims, preferred_element_type=f32)
    half = both.shape[1] // 2
    return both[:, :half] + both[:, half:]


def bcast_row(value, k):
    return jnp.broadcast_to(value[k : k + 1, :], value.shape)


def bcast_lane(value, k, lanes):
    return jnp.broadcast_to(value[:, k : k + 1], (value.shape[0], lanes))


def pack(values):
    first, second = values
    half = first.shape[1] // 2
    left = lax.broadcasted_iota(jnp.int32, first.shape, 1) < half
    return (
        jnp.where(left, first, pltpu.roll(second, half, 1)),
        jnp.where(left, pltpu.roll(first, half, 1), second),
    )


def tree_sum(terms):
    while len(terms) > 1:
        terms = [a + b for a, b in zip(terms[::2], terms[1::2])] + terms[len(terms) & ~1 :]
    return terms[0]


def triple(value):
    high = value.astype(bf16).astype(f32)
    middle = (value - high).astype(bf16).astype(f32)
    return high, middle, value - high - middle


def far_rows(value, solved, at):
    size = value.shape[1]
    half = size // 2
    lane = lax.broadcasted_iota(jnp.int32, value.shape, 1) % half
    parts = triple(jnp.where((lane >= at) & (lane < at + BLOCK), value, 0.0))
    left = lax.broadcasted_iota(jnp.int32, (BLOCK, size), 1) < half
    taken = [[], []]
    for part in solved:
        pieces = triple(part)
        taken[0].append([jnp.where(left, piece, 0.0).astype(bf16) for piece in pieces])
        taken[1].append([jnp.where(left, 0.0, piece).astype(bf16) for piece in pieces])
    nothing = jnp.zeros((BLOCK, size * len(solved)), bf16)
    spots = half // BLOCK
    pairs = ((0, 0), (0, 1), (1, 0), (0, 2), (2, 0), (1, 1))
    operands, tiles = [], []
    for first in range(0, len(pairs), spots):
        operand, group = None, [nothing] * (2 * spots)
        for i, (mine, theirs) in enumerate(pairs[first : first + spots]):
            moved = pltpu.roll(parts[mine], i * BLOCK, 1) if i else parts[mine]
            operand = moved if operand is None else operand + moved
            for side in range(2):
                spot = (side * spots + at // BLOCK + i) % (2 * spots)
                group[spot] = jnp.concatenate([t[theirs] for t in taken[side]], axis=1)
        operands.append(operand.astype(bf16))
        tiles += group
    return jnp.dot(
        jnp.concatenate(operands, axis=1),
        jnp.concatenate(tiles, axis=0),
        preferred_element_type=f32,
    )


def inverse_factors(matrix_ref, inverse_ref):
    size = matrix_ref.shape[1]
    half = size // 2
    row = lax.broadcasted_iota(jnp.int32, (BLOCK, size), 0)
    lane = lax.broadcasted_iota(jnp.int32, (BLOCK, size), 1)
    other = jnp.where(lane < half, 0, half)

    def columns_of(value, at):
        return jnp.take_along_axis(value, other + at, axis=1)

    parts = (0, 1, 2)
    panel = [matrix_ref[part, :BLOCK, :] for part in parts]
    columns = [columns_of(panel[0], j) for j in range(BLOCK)]
    for start in range(0, size, BLOCK):
        rows = slice(start, start + BLOCK)
        at = start % half
        below = start + BLOCK
        if below < size:
            values = [matrix_ref[part, below : below + BLOCK, :] for part in parts]
        pivot_rows = list(panel)
        pivot = bcast_row(columns[0], 0)
        for k in range(BLOCK):
            reciprocal = 1.0 / pivot
            if k == 0:
                pivots, reciprocals = pivot, reciprocal
            else:
                later = row >= k
                pivots = jnp.where(later, pivot, pivots)
                reciprocals = jnp.where(later, reciprocal, reciprocals)
                pivot_rows = [jnp.where(later, new, old) for new, old in zip(panel, pivot_rows)]
            if k + 1 < BLOCK:
                beside = bcast_row(columns[k + 1], k)
                pivot = bcast_row(columns[k + 1], k + 1) - (beside * beside) * reciprocal
            factor = jnp.where(row == k, 0.0, columns[k]) * reciprocal
            for j in range(k + 1, BLOCK):
                columns[j] = columns[j] - factor * bcast_row(columns[j], k)
            panel = [value - factor * bcast_row(value, k) for value in panel]
            if k == 3 and below < size:
                factors = [columns_of(values[0], at + j) for j in range(BLOCK)]
        solved = [value * reciprocals for value in panel]
        scale = lax.rsqrt(pivots)
        kept = [value * scale for value in pivot_rows]
        inverse_ref[0, rows, :] = kept[parts.index(2)]
        inverse_ref[1, rows, :] = kept[parts.index(3)] if 3 in parts else jnp.zeros_like(scale)
        if below == size:
            break
        panel = []
        for value, taken in zip(values, solved):
            terms = [factors[k] * bcast_row(taken, k) for k in range(BLOCK)]
            panel.append(value - tree_sum(terms))
        if below == half:
            panel = panel[1:] + [matrix_ref[3, below : below + BLOCK, :]]
        columns = [columns_of(panel[0], below % half + j) for j in range(BLOCK)]
        rest = slice(below + BLOCK, size)
        if below + BLOCK < size:
            taken = far_rows(matrix_ref[parts[0], rest, :], solved, at)
            for i, part in enumerate(parts):
                mine = taken[:, i * size : (i + 1) * size]
                matrix_ref[part, rest, :] = matrix_ref[part, rest, :] - mine
        if below == half:
            parts = (1, 2, 3)


def zero_ends(ref, elements, side):
    for e in range(elements):
        ref[e, 0] = jnp.zeros(ref.shape[2:], f32)
        ref[e, side + 1] = jnp.zeros(ref.shape[2:], f32)
        for x in range(side):
            ref[e, x + 1, :LEAD] = jnp.zeros((LEAD, ref.shape[-1]), f32)
            ref[e, x + 1, LEAD + COL * side :] = jnp.zeros((LEAD, ref.shape[-1]), f32)


def beside_weight(side, columns):
    inside = lax.broadcasted_iota(jnp.int32, (COL, columns), 0) < side
    return jnp.where(inside, 1.0 / halfwidth, 0.0)


def slab_step(x, source, scaled_ref, previous, target, pair_ref, margin):
    elements, side = source.shape[0], source.shape[1] - 2
    columns = source.shape[-1]
    weight = beside_weight(side, columns)
    for e in range(elements):

        def column(y):
            return source[e, x + 1, LEAD + COL * y : LEAD + COL * (y + 1)]

        before, here = None, column(0)
        for y in range(side):
            low = LEAD + COL * y
            after = column(y + 1) if y + 1 < side else None
            beside = source[e, x, low : low + COL] + source[e, x + 2, low : low + COL]
            beside = beside + (
                source[e, x + 1, low - 1 : low - 1 + COL]
                + source[e, x + 1, low + 1 : low + 1 + COL]
            )
            if before is not None:
                beside = beside + before
            if after is not None:
                beside = beside + after
            scaled = scaled_ref[x, (e * G - margin + y) % scaled_ref.shape[1]]
            value = scaled * here - weight * beside
            if previous is None:
                value = 0.5 * value
            else:
                value = value - previous[e, x + 1, low : low + COL]
            target[e, x + 1, low : low + COL] = value
            if pair_ref is not None:
                high, rest = split(value)
                at = pl.multiple_of(x * (side * COL), COL) + COL * y
                pair_ref[e, pl.ds(at, COL), :columns] = high
                pair_ref[e, pl.ds(at, COL), columns:] = rest
            before, here = here, after


def first_kernel(start_ref, field_ref, next_ref, flat_ref):
    elements, columns = start_ref.shape[0], start_ref.shape[-1]
    side = field_ref.shape[1] - 2
    slab = side * side
    zero_ends(field_ref, elements, side)
    zero_ends(next_ref, elements, side)
    inside = lax.broadcasted_iota(jnp.int32, (COL, columns), 0) < side

    def prepare(x, carry):
        for e in range(elements):
            flat_ref[e, :slab] = start_ref[e, pl.ds(pl.multiple_of(x * slab, 16), slab), :].astype(f32)
            for y in range(side):
                value = jnp.where(inside, flat_ref[e, side * y : side * y + COL], 0.0)
                field_ref[e, x + 1, LEAD + COL * y : LEAD + COL * (y + 1)] = value
        return carry

    lax.fori_loop(0, side, prepare, 0, unroll=2)


def point_rows(field, margin, e, x, y):
    low = LEAD + COL * (margin + y) + margin
    return field[e, margin + x + 1, low : low + G]


def layer(field, margin, e, d, i):
    if d == 0:
        return [point_rows(field, margin, e, i, y) for y in range(G)]
    if d == 1:
        return [point_rows(field, margin, e, x, i) for x in range(G)]
    low = LEAD + COL * margin + margin + i
    return [field[e, margin + x + 1, pl.ds(low, G, stride=COL)] for x in range(G)]


def spread_potential(x, box_ref, scaled_ref):
    rows = box_ref[x]
    for y in range(scaled_ref.shape[1]):
        scaled_ref[x, y] = bcast_lane(rows, y, scaled_ref.shape[-1])


def steps(ranges, first_ref, start_ref, scaled_ref, pair_ref, margin):
    fields = (first_ref, start_ref)
    for index in range(1, FILTER):
        source, target = fields
        pair = pair_ref if index == FILTER - 1 else None

        def next_step(x, carry):
            slab_step(x, source, scaled_ref, target, target, pair, margin)
            return carry

        lax.fori_loop(*ranges(index), next_step, 0, unroll=4)
        fields = fields[::-1]
    return fields[0]


def overlaps(pair_ref, low, high):
    columns = pair_ref.shape[-1] // 2
    return [
        lax.dot_general(
            pair_ref[e, low:high, :columns],
            pair_ref[e, low:high],
            (((0,), (0,)), ((), ())),
            preferred_element_type=f32,
        )
        for e in range(pair_ref.shape[0])
    ]


def own_operator(field, scaled_ref, inner_ref, applied_ref, raw_ref, margin):
    elements, columns = field.shape[0], field.shape[-1]
    y_points = scaled_ref.shape[1]

    z = lax.broadcasted_iota(jnp.int32, (G, columns), 0)
    edge = (z == 1) | (z == G - 1)
    weight_down = jnp.where(z == 0, 0.0, jnp.where(edge, 0.25, 0.5))
    edge = (z == 0) | (z == G - 2)
    weight_up = jnp.where(z == G - 1, 0.0, jnp.where(edge, 0.25, 0.5))

    def link(i):
        return 0.25 if i in (0, G - 2) else 0.5

    for e in range(elements):
        for x in range(G):
            for y in range(0, G, 2):
                inner_pair, applied_pair = [], []
                for yy in (y, y + 1):
                    here = point_rows(field, margin, e, x, yy)
                    potential = scaled_ref[margin + x, (e * G + yy) % y_points, margin : margin + G]
                    value = (0.5 * halfwidth * potential + center) * here
                    value = value - weight_down * pltpu.roll(here, 1, 0)
                    value = value - weight_up * pltpu.roll(here, G - 1, 0)
                    if x > 0:
                        value = value - link(x - 1) * point_rows(field, margin, e, x - 1, yy)
                    if x < G - 1:
                        value = value - link(x) * point_rows(field, margin, e, x + 1, yy)
                    if yy > 0:
                        value = value - link(yy - 1) * point_rows(field, margin, e, x, yy - 1)
                    if yy < G - 1:
                        value = value - link(yy) * point_rows(field, margin, e, x, yy + 1)
                    inner_pair.append(here)
                    applied_pair.append(value)
                at = slice((x * G + y) * G, (x * G + y + 2) * G)
                for ref, pair in ((inner_ref, inner_pair), (applied_ref, applied_pair)):
                    high, low = split(jnp.concatenate(pair, axis=0))
                    ref[e, at, :columns] = high
                    ref[e, at, columns:] = low

    for e in range(elements):
        both = lax.dot_general(
            inner_ref[e, :, :columns],
            applied_ref[e],
            (((0,), (0,)), ((), ())),
            preferred_element_type=f32,
        )
        raw = both[:, :columns] + both[:, columns:]
        raw = raw + lax.dot_general(
            inner_ref[e, :, columns:],
            applied_ref[e, :, :columns],
            (((0,), (0,)), ((), ())),
            preferred_element_type=f32,
        )
        raw_ref[e] = raw


def middle_kernel(
    margin,
    low_ref,
    z_before_ref,
    z_after_ref,
    start_in,
    first_in,
    start_ref,
    first_ref,
    scaled_ref,
    pair_ref,
    overlap_ref,
    box_ref,
):
    side, y_points = scaled_ref.shape[:2]
    end = side - margin
    box_ref[...] = jnp.zeros_like(box_ref)
    box_ref[:end, margin : margin + G, :y_points] = low_ref[...]
    box_ref[:end, :margin, :y_points] = z_before_ref[...]
    box_ref[:end, margin + G : side, :y_points] = z_after_ref[...]

    spread_potential(0, box_ref, scaled_ref)

    def first_step(x, carry):
        spread_potential(x + 1, box_ref, scaled_ref)
        slab_step(x, start_ref, scaled_ref, None, first_ref, None, margin)
        return carry

    lax.fori_loop(0, end, first_step, 0, unroll=5)
    steps(lambda i: (0, end - i), first_ref, start_ref, scaled_ref, pair_ref, margin)
    for e, value in enumerate(overlaps(pair_ref, 0, (end - FILTER + 1) * side * COL)):
        overlap_ref[e] = value


def basis_kernel(
    margin,
    x_after_ref,
    z_before_ref,
    z_after_ref,
    start_in,
    first_in,
    scaled_in,
    pair_in,
    overlap_ref,
    minus_x_ref,
    minus_z_ref,
    inverse_ref,
    raw_ref,
    start_ref,
    first_ref,
    scaled_ref,
    pair_ref,
    box_ref,
    matrix_ref,
    packed_ref,
    inner_ref,
    applied_ref,
):
    elements, columns = start_ref.shape[0], start_ref.shape[-1]
    side, y_points = scaled_ref.shape[:2]
    end = side - margin
    box_ref[...] = jnp.zeros_like(box_ref)
    box_ref[end:, margin : margin + G, :y_points] = x_after_ref[...]
    box_ref[end:, :margin, :y_points] = z_before_ref[...]
    box_ref[end:, margin + G : side, :y_points] = z_after_ref[...]
    for x in range(end, side):
        spread_potential(x, box_ref, scaled_ref)
    for x in range(end, side):
        slab_step(x, start_ref, scaled_ref, None, first_ref, None, margin)
    field = steps(
        lambda i: (end - i, side), first_ref, start_ref, scaled_ref, pair_ref, margin
    )
    rest = overlaps(pair_ref, (end - FILTER + 1) * side * COL, side * side * COL)

    own_operator(field, scaled_ref, inner_ref, applied_ref, raw_ref, margin)

    identity = (
        lax.broadcasted_iota(jnp.int32, (columns, columns), 0)
        == lax.broadcasted_iota(jnp.int32, (columns, columns), 1)
    ).astype(f32)
    grams = []
    for e in range(elements):
        products = overlap_ref[e] + rest[e]
        cross = products[:, columns:]
        grams.append(products[:, :columns] + (cross + cross.T))
    for e in range(0, elements, 2):
        pairs = [grams[e], grams[min(e + 1, elements - 1)]]
        for i, value in enumerate(pack(pairs) + pack([identity, identity])):
            matrix_ref[i] = value
        inverse_factors(matrix_ref, packed_ref)
        solved = pack([packed_ref[0], packed_ref[1]])
        for i in range(min(2, elements - e)):
            inverse_ref[e + i] = solved[i]

    for e in range(elements):
        held = weights(split(inverse_ref[e]), True)
        rows = []
        for d in (0, 2):
            rows += layer(field, margin, e, d, 0) + layer(field, margin, e, d, 1)
        faces = product(jnp.concatenate(rows, 0), held, True)
        minus_x_ref[e] = faces[: 2 * G * G]
        minus_z_ref[e] = faces[2 * G * G :]


def near_kernel(
    count,
    margin,
    inverse_ref,
    raw_ref,
    field,
    plus_ref,
    near_ref,
    *out_refs,
):
    elements, columns = inverse_ref.shape[0], inverse_ref.shape[-1]
    face = 2 * G * G
    minus, plus, held = [], [], []
    for e in range(elements):
        held.append(weights(split(inverse_ref[e]), True))
        rows = layer(field, margin, e, 1, 0) + layer(field, margin, e, 1, 1)
        for d in range(3):
            last = layer(field, margin, e, d, G - 1)
            before = layer(field, margin, e, d, G - 2)
            rows += [-(0.5 * a + 0.25 * b) for a, b in zip(last, before)]
            rows += [-0.25 * a for a in last]
        faces = product(jnp.concatenate(rows, 0), held[e], True)
        minus.append(faces[:face])
        plus.append(faces[face : 2 * face].T)
        plus_ref[e, 0] = plus[e]
        plus[e] = faces[2 * face : 3 * face].T
        plus_ref[e, 1] = faces[3 * face :].T

    for e in range(elements):
        half = product(inverse_ref[e], weights(split(raw_ref[e]), False), False)
        near_ref[0, e] = product(half, held[e], True)
        following = weights(split(minus[(e + 1) % elements]), False)
        near_ref[1, e] = product(plus[e], following, False)
    send_rows(count, [near_ref], out_refs, parted(count)[1])


def partner(index, step, count):
    return index ^ step if count & (count - 1) == 0 else (index + step) % count


def send_rows(count, sources, out_refs, steps):
    elements, size = sources[0].shape[1:3]
    rows = size // count
    me = lax.axis_index("ez")
    for out_ref, step in zip(out_refs, steps):
        owner = me ^ step if count & (count - 1) == 0 else lax.rem(me + step, count)
        at = pl.ds(pl.multiple_of(owner * rows, rows), rows)
        slot = 0
        for blocks_ref in sources:
            for kind in range(blocks_ref.shape[0]):
                for e in range(elements):
                    out_ref[:, slot, :] = blocks_ref[kind, e, at, :]
                    slot += 1


def far_kernel(count, plus_ref, next_x_ref, next_z_ref, near_ref, *rest):
    out_refs, far_ref = rest[:-1], rest[-1]
    for e in range(plus_ref.shape[0]):
        for d, ref in ((0, next_x_ref), (1, next_z_ref)):
            far_ref[d, e] = product(plus_ref[e, d], weights(split(ref[e]), False), False)
    whole, ahead = parted(count)
    send_rows(count, [near_ref, far_ref], out_refs[: len(whole)], whole)
    send_rows(count, [far_ref], out_refs[len(whole) :], ahead)


def parted(count):
    return [step for step in range(count) if step < AHEAD], [
        step for step in range(count) if step >= AHEAD
    ]


def assemble_kernel(count, *refs):
    whole, ahead = parted(count)
    whole_refs, refs = refs[: len(whole)], refs[len(whole) :]
    near_refs, refs = refs[: len(ahead)], refs[len(ahead) :]
    far_refs, (diagonal_ref, coupling_ref) = refs[: len(ahead)], refs[len(ahead) :]
    elements = diagonal_ref.shape[2]
    me = lax.axis_index("ez")

    def place(step, near_ref, far_ref, far_at):
        z = me ^ step if count & (count - 1) == 0 else lax.rem(me + (count - step), count)
        diagonal_ref[:, z] = near_ref[:, :elements]
        coupling_ref[:, z, 1] = near_ref[:, elements : 2 * elements]
        coupling_ref[:, z, 0] = far_ref[:, far_at : far_at + elements]
        coupling_ref[:, z, 2] = far_ref[:, far_at + elements : far_at + 2 * elements]

    for step, ref in zip(whole, whole_refs):
        place(step, ref, ref, 2 * elements)
    for step, near_ref, far_ref in zip(ahead, near_refs, far_refs):
        place(step, near_ref, far_ref, 0)


def vmem(count):
    return [pl.BlockSpec(memory_space=pltpu.VMEM)] * count


def shift(block, axis, distance):
    count = lax.axis_size(axis)
    return lax.ppermute(block, axis, [(i, (i + distance) % count) for i in range(count)])


def exchange(block, step):
    count = lax.axis_size("ez")
    if step == 0:
        return block
    return lax.ppermute(block, "ez", [(i, partner(i, step, count)) for i in range(count)])


def local(potential, basis_start):
    elements, points, columns = basis_start.shape[2:]
    side = round(points ** (1 / 3))
    margin = (side - G) // 2
    y_points = potential.shape[1]
    count = lax.axis_size("ez")
    starts = basis_start.reshape(elements, points, columns)
    own = potential.transpose(0, 2, 1)
    own_scaled = lax.optimization_barrier((own + (3.0 - center)) * (2.0 / halfwidth))
    x_before = (shift(own, "ex", 1)[G - margin :] + (3.0 - center)) * (2.0 / halfwidth)
    x_after = shift(own_scaled[:margin], "ex", -1)

    shape = jax.ShapeDtypeStruct
    field = shape((elements, side + 2, LEAD + COL * side + LEAD, columns), f32)
    scaled = shape((side, y_points, COL, columns), f32)
    start, first = pl.pallas_call(
        first_kernel,
        out_shape=[field, field],
        in_specs=vmem(1),
        out_specs=vmem(2),
        scratch_shapes=[pltpu.VMEM((elements, side * side + COL, columns), f32)],
        compiler_params=pltpu.CompilerParams(vmem_limit_bytes=24 * 2**20),
        cost_estimate=pl.CostEstimate(flops=10**5, bytes_accessed=10**4, transcendentals=0),
        name="first",
    )(starts)
    low = lax.optimization_barrier(jnp.concatenate([x_before, own_scaled], axis=0))
    z_before = shift(low[:, G - margin :], "ez", 1)
    z_after = shift(low[:, :margin], "ez", -1)
    edge_before = shift(x_after[:, G - margin :], "ez", 1)
    edge_after = shift(x_after[:, :margin], "ez", -1)
    pair = shape((elements, side * side * COL, 2 * columns), bf16)
    overlap = shape((elements, columns, 2 * columns), f32)
    box = pltpu.VMEM((side, COL, 128), f32)
    start, first, most_scaled, pairs, overlapped = pl.pallas_call(
        functools.partial(middle_kernel, margin),
        out_shape=[field, field, scaled, pair, overlap],
        in_specs=vmem(5),
        out_specs=vmem(5),
        input_output_aliases={3: 0, 4: 1},
        scratch_shapes=[box],
        compiler_params=pltpu.CompilerParams(vmem_limit_bytes=32 * 2**20),
        cost_estimate=pl.CostEstimate(flops=10**8, bytes_accessed=10**7, transcendentals=0),
        name="middle",
    )(low, z_before, z_after, start, first)

    face = shape((elements, 2 * G * G, columns), f32)
    square = shape((elements, columns, columns), f32)
    minus_x, minus_z, inverse, raw, _, filtered, _, _ = pl.pallas_call(
        functools.partial(basis_kernel, margin),
        out_shape=[face, face, square, square, field, field, scaled, pair],
        in_specs=vmem(8),
        out_specs=vmem(8),
        input_output_aliases={3: 4, 4: 5, 5: 6, 6: 7},
        scratch_shapes=[
            box,
            pltpu.VMEM((4, columns, columns), f32),
            pltpu.VMEM((2, columns, columns), f32),
            pltpu.VMEM((elements, G**3, 2 * columns), bf16),
            pltpu.VMEM((elements, G**3, 2 * columns), bf16),
        ],
        compiler_params=pltpu.CompilerParams(vmem_limit_bytes=32 * 2**20),
        name="basis",
    )(x_after, edge_before, edge_after, start, first, most_scaled, pairs, overlapped)

    next_x = shift(minus_x, "ex", -1)
    next_z = shift(minus_z, "ez", -1)
    whole, ahead = parted(count)
    block = shape((columns // count, 2 * elements, columns), f32)
    double = shape((columns // count, 4 * elements, columns), f32)
    squares = shape((2, elements, columns, columns), f32)
    plus, own_near, *near = pl.pallas_call(
        functools.partial(near_kernel, count, margin),
        out_shape=[shape((elements, 2, columns, 2 * G * G), f32), squares] + [block] * len(ahead),
        in_specs=vmem(3),
        out_specs=vmem(2 + len(ahead)),
        compiler_params=pltpu.CompilerParams(vmem_limit_bytes=24 * 2**20),
        cost_estimate=pl.CostEstimate(flops=10**8, bytes_accessed=10**7, transcendentals=0),
        name="near",
    )(inverse, raw, filtered)
    near = [exchange(value, step) for value, step in zip(near, ahead)]

    far = pl.pallas_call(
        functools.partial(far_kernel, count),
        out_shape=[double] * len(whole) + [block] * len(ahead),
        in_specs=vmem(4),
        out_specs=vmem(count),
        scratch_shapes=[pltpu.VMEM(squares.shape, f32)],
        compiler_params=pltpu.CompilerParams(vmem_limit_bytes=16 * 2**20),
        name="far",
    )(plus, next_x, next_z, own_near)
    far = [exchange(value, step) for value, step in zip(far, whole + ahead)]

    rows = columns // count
    diagonal, coupled = pl.pallas_call(
        functools.partial(assemble_kernel, count),
        out_shape=[
            shape((rows, count, elements, columns), f32),
            shape((rows, count, 3, elements, columns), f32),
        ],
        in_specs=vmem(len(whole) + 2 * len(ahead)),
        out_specs=vmem(2),
        compiler_params=pltpu.CompilerParams(vmem_limit_bytes=16 * 2**20),
        name="assemble",
    )(*far[: len(whole)], *near, *far[len(whole) :])
    return (diagonal[None], coupled.transpose(0, 1, 3, 2, 4)[None])


def solution(mesh):
    return jax.shard_map(
        local,
        mesh=mesh,
        in_specs=(P("ex", None, "ez"), P("ex", "ez", None, None, None)),
        out_specs=(P("ex", "ez", None, None, None), P("ex", "ez", None, None, None, None)),
        check_vma=False,
    )
```

```python
import functools

import jax
import jax.numpy as jnp
from jax import lax
from jax.experimental import pallas as pl
from jax.experimental.pallas import tpu as pltpu
from jax.sharding import PartitionSpec as P

G = 8
FILTER = 3

center = 6.5
halfwidth = 5.5

f32 = jnp.float32
bf16 = jnp.bfloat16

LEAD = 8
COL = 16
BLOCK = 16


def split(value):
    high = value.astype(bf16)
    return high, (value - high.astype(f32)).astype(bf16)


def weights(pair, transposed):
    high, low = pair
    empty = jnp.zeros_like(low)
    if transposed:
        upper = jnp.concatenate([high, high], axis=1)
        lower = jnp.concatenate([low, empty], axis=1)
        return jnp.concatenate([upper, lower], axis=0)
    upper = jnp.concatenate([high, low], axis=1)
    lower = jnp.concatenate([high, empty], axis=1)
    return jnp.concatenate([upper, lower], axis=0)


def product(value, held, transposed):
    pair = jnp.concatenate(split(value), axis=1)
    dims = (((1,), (1 if transposed else 0,)), ((), ()))
    both = lax.dot_general(pair, held, dims, preferred_element_type=f32)
    half = both.shape[1] // 2
    return both[:, :half] + both[:, half:]


def bcast_row(value, k):
    return jnp.broadcast_to(value[k : k + 1, :], value.shape)


def bcast_lane(value, k, lanes):
    return jnp.broadcast_to(value[:, k : k + 1], (value.shape[0], lanes))


def pack(values):
    first, second = values
    half = first.shape[1] // 2
    left = lax.broadcasted_iota(jnp.int32, first.shape, 1) < half
    return (
        jnp.where(left, first, pltpu.roll(second, half, 1)),
        jnp.where(left, pltpu.roll(first, half, 1), second),
    )


def tree_sum(terms):
    while len(terms) > 1:
        terms = [a + b for a, b in zip(terms[::2], terms[1::2])] + terms[len(terms) & ~1 :]
    return terms[0]


def triple(value):
    high = value.astype(bf16).astype(f32)
    middle = (value - high).astype(bf16).astype(f32)
    return high, middle, value - high - middle


def far_rows(value, solved, at):
    size = value.shape[1]
    half = size // 2
    lane = lax.broadcasted_iota(jnp.int32, value.shape, 1) % half
    parts = triple(jnp.where((lane >= at) & (lane < at + BLOCK), value, 0.0))
    left = lax.broadcasted_iota(jnp.int32, (BLOCK, size), 1) < half
    taken = [[], []]
    for part in solved:
        pieces = triple(part)
        taken[0].append([jnp.where(left, piece, 0.0).astype(bf16) for piece in pieces])
        taken[1].append([jnp.where(left, 0.0, piece).astype(bf16) for piece in pieces])
    nothing = jnp.zeros((BLOCK, size * len(solved)), bf16)
    spots = half // BLOCK
    pairs = ((0, 0), (0, 1), (1, 0), (0, 2), (2, 0), (1, 1))
    operands, tiles = [], []
    for first in range(0, len(pairs), spots):
        operand, group = None, [nothing] * (2 * spots)
        for i, (mine, theirs) in enumerate(pairs[first : first + spots]):
            moved = pltpu.roll(parts[mine], i * BLOCK, 1) if i else parts[mine]
            operand = moved if operand is None else operand + moved
            for side in range(2):
                spot = (side * spots + at // BLOCK + i) % (2 * spots)
                group[spot] = jnp.concatenate([t[theirs] for t in taken[side]], axis=1)
        operands.append(operand.astype(bf16))
        tiles += group
    return jnp.dot(
        jnp.concatenate(operands, axis=1),
        jnp.concatenate(tiles, axis=0),
        preferred_element_type=f32,
    )


def inverse_factors(matrix_ref, inverse_ref):
    size = matrix_ref.shape[1]
    half = size // 2
    row = lax.broadcasted_iota(jnp.int32, (BLOCK, size), 0)
    lane = lax.broadcasted_iota(jnp.int32, (BLOCK, size), 1)
    other = jnp.where(lane < half, 0, half)

    def columns_of(value, at):
        return jnp.take_along_axis(value, other + at, axis=1)

    parts = (0, 1, 2)
    panel = [matrix_ref[part, :BLOCK, :] for part in parts]
    columns = [columns_of(panel[0], j) for j in range(BLOCK)]
    for start in range(0, size, BLOCK):
        rows = slice(start, start + BLOCK)
        at = start % half
        below = start + BLOCK
        if below < size:
            values = [matrix_ref[part, below : below + BLOCK, :] for part in parts]
        pivot_rows = list(panel)
        pivot = bcast_row(columns[0], 0)
        for k in range(BLOCK):
            reciprocal = 1.0 / pivot
            if k == 0:
                pivots, reciprocals = pivot, reciprocal
            else:
                later = row >= k
                pivots = jnp.where(later, pivot, pivots)
                reciprocals = jnp.where(later, reciprocal, reciprocals)
                pivot_rows = [jnp.where(later, new, old) for new, old in zip(panel, pivot_rows)]
            if k + 1 < BLOCK:
                beside = bcast_row(columns[k + 1], k)
                pivot = bcast_row(columns[k + 1], k + 1) - (beside * beside) * reciprocal
            factor = jnp.where(row == k, 0.0, columns[k]) * reciprocal
            for j in range(k + 1, BLOCK):
                columns[j] = columns[j] - factor * bcast_row(columns[j], k)
            panel = [value - factor * bcast_row(value, k) for value in panel]
            if k == 3 and below < size:
                factors = [columns_of(values[0], at + j) for j in range(BLOCK)]
        solved = [value * reciprocals for value in panel]
        scale = lax.rsqrt(pivots)
        kept = [value * scale for value in pivot_rows]
        inverse_ref[0, rows, :] = kept[parts.index(2)]
        inverse_ref[1, rows, :] = kept[parts.index(3)] if 3 in parts else jnp.zeros_like(scale)
        if below == size:
            break
        panel = []
        for value, taken in zip(values, solved):
            terms = [factors[k] * bcast_row(taken, k) for k in range(BLOCK)]
            panel.append(value - tree_sum(terms))
        if below == half:
            panel = panel[1:] + [matrix_ref[3, below : below + BLOCK, :]]
        columns = [columns_of(panel[0], below % half + j) for j in range(BLOCK)]
        rest = slice(below + BLOCK, size)
        if below + BLOCK < size:
            taken = far_rows(matrix_ref[parts[0], rest, :], solved, at)
            for i, part in enumerate(parts):
                mine = taken[:, i * size : (i + 1) * size]
                matrix_ref[part, rest, :] = matrix_ref[part, rest, :] - mine
        if below == half:
            parts = (1, 2, 3)


def zero_ends(ref, elements, side):
    for e in range(elements):
        ref[e, 0] = jnp.zeros(ref.shape[2:], f32)
        ref[e, side + 1] = jnp.zeros(ref.shape[2:], f32)
        for x in range(side):
            ref[e, x + 1, :LEAD] = jnp.zeros((LEAD, ref.shape[-1]), f32)
            ref[e, x + 1, LEAD + COL * side :] = jnp.zeros((LEAD, ref.shape[-1]), f32)


def beside_weight(side, columns):
    inside = lax.broadcasted_iota(jnp.int32, (COL, columns), 0) < side
    return jnp.where(inside, 1.0 / halfwidth, 0.0)


def slab_step(x, source, scaled_ref, previous, target, pair_ref, margin):
    elements, side = source.shape[0], source.shape[1] - 2
    columns = source.shape[-1]
    weight = beside_weight(side, columns)
    for e in range(elements):

        def column(y):
            return source[e, x + 1, LEAD + COL * y : LEAD + COL * (y + 1)]

        before, here = None, column(0)
        for y in range(side):
            low = LEAD + COL * y
            after = column(y + 1) if y + 1 < side else None
            beside = source[e, x, low : low + COL] + source[e, x + 2, low : low + COL]
            beside = beside + (
                source[e, x + 1, low - 1 : low - 1 + COL]
                + source[e, x + 1, low + 1 : low + 1 + COL]
            )
            if before is not None:
                beside = beside + before
            if after is not None:
                beside = beside + after
            scaled = scaled_ref[x, (e * G - margin + y) % scaled_ref.shape[1]]
            value = scaled * here - weight * beside
            if previous is None:
                value = 0.5 * value
            else:
                value = value - previous[e, x + 1, low : low + COL]
            target[e, x + 1, low : low + COL] = value
            if pair_ref is not None:
                high, rest = split(value)
                at = pl.multiple_of(x * (side * COL), COL) + COL * y
                pair_ref[e, pl.ds(at, COL), :columns] = high
                pair_ref[e, pl.ds(at, COL), columns:] = rest
            before, here = here, after


def first_kernel(start_ref, field_ref, next_ref, flat_ref):
    elements, columns = start_ref.shape[0], start_ref.shape[-1]
    side = field_ref.shape[1] - 2
    slab = side * side
    zero_ends(field_ref, elements, side)
    zero_ends(next_ref, elements, side)
    inside = lax.broadcasted_iota(jnp.int32, (COL, columns), 0) < side

    def prepare(x, carry):
        for e in range(elements):
            flat_ref[e, :slab] = start_ref[e, pl.ds(pl.multiple_of(x * slab, 16), slab), :].astype(f32)
            for y in range(side):
                value = jnp.where(inside, flat_ref[e, side * y : side * y + COL], 0.0)
                field_ref[e, x + 1, LEAD + COL * y : LEAD + COL * (y + 1)] = value
        return carry

    lax.fori_loop(0, side, prepare, 0, unroll=2)


def point_rows(field, margin, e, x, y):
    low = LEAD + COL * (margin + y) + margin
    return field[e, margin + x + 1, low : low + G]


def layer(field, margin, e, d, i):
    if d == 0:
        return [point_rows(field, margin, e, i, y) for y in range(G)]
    if d == 1:
        return [point_rows(field, margin, e, x, i) for x in range(G)]
    low = LEAD + COL * margin + margin + i
    return [field[e, margin + x + 1, pl.ds(low, G, stride=COL)] for x in range(G)]


def spread_potential(x, box_ref, scaled_ref):
    rows = box_ref[x]
    for y in range(scaled_ref.shape[1]):
        scaled_ref[x, y] = bcast_lane(rows, y, scaled_ref.shape[-1])


def steps(ranges, first_ref, start_ref, scaled_ref, pair_ref, margin):
    fields = (first_ref, start_ref)
    for index in range(1, FILTER):
        source, target = fields
        pair = pair_ref if index == FILTER - 1 else None

        def next_step(x, carry):
            slab_step(x, source, scaled_ref, target, target, pair, margin)
            return carry

        lax.fori_loop(*ranges(index), next_step, 0, unroll=4)
        fields = fields[::-1]
    return fields[0]


def overlaps(pair_ref, low, high):
    columns = pair_ref.shape[-1] // 2
    return [
        lax.dot_general(
            pair_ref[e, low:high, :columns],
            pair_ref[e, low:high],
            (((0,), (0,)), ((), ())),
            preferred_element_type=f32,
        )
        for e in range(pair_ref.shape[0])
    ]


def own_operator(field, scaled_ref, inner_ref, applied_ref, raw_ref, margin):
    elements, columns = field.shape[0], field.shape[-1]
    y_points = scaled_ref.shape[1]

    z = lax.broadcasted_iota(jnp.int32, (G, columns), 0)
    edge = (z == 1) | (z == G - 1)
    weight_down = jnp.where(z == 0, 0.0, jnp.where(edge, 0.25, 0.5))
    edge = (z == 0) | (z == G - 2)
    weight_up = jnp.where(z == G - 1, 0.0, jnp.where(edge, 0.25, 0.5))

    def link(i):
        return 0.25 if i in (0, G - 2) else 0.5

    for e in range(elements):
        for x in range(G):
            for y in range(0, G, 2):
                inner_pair, applied_pair = [], []
                for yy in (y, y + 1):
                    here = point_rows(field, margin, e, x, yy)
                    potential = scaled_ref[margin + x, (e * G + yy) % y_points, margin : margin + G]
                    value = (0.5 * halfwidth * potential + center) * here
                    value = value - weight_down * pltpu.roll(here, 1, 0)
                    value = value - weight_up * pltpu.roll(here, G - 1, 0)
                    if x > 0:
                        value = value - link(x - 1) * point_rows(field, margin, e, x - 1, yy)
                    if x < G - 1:
                        value = value - link(x) * point_rows(field, margin, e, x + 1, yy)
                    if yy > 0:
                        value = value - link(yy - 1) * point_rows(field, margin, e, x, yy - 1)
                    if yy < G - 1:
                        value = value - link(yy) * point_rows(field, margin, e, x, yy + 1)
                    inner_pair.append(here)
                    applied_pair.append(value)
                at = slice((x * G + y) * G, (x * G + y + 2) * G)
                for ref, pair in ((inner_ref, inner_pair), (applied_ref, applied_pair)):
                    high, low = split(jnp.concatenate(pair, axis=0))
                    ref[e, at, :columns] = high
                    ref[e, at, columns:] = low

    for e in range(elements):
        both = lax.dot_general(
            inner_ref[e, :, :columns],
            applied_ref[e],
            (((0,), (0,)), ((), ())),
            preferred_element_type=f32,
        )
        raw = both[:, :columns] + both[:, columns:]
        raw = raw + lax.dot_general(
            inner_ref[e, :, columns:],
            applied_ref[e, :, :columns],
            (((0,), (0,)), ((), ())),
            preferred_element_type=f32,
        )
        raw_ref[e] = raw


def middle_kernel(
    margin,
    low_ref,
    z_before_ref,
    z_after_ref,
    start_in,
    first_in,
    start_ref,
    first_ref,
    scaled_ref,
    pair_ref,
    overlap_ref,
    box_ref,
):
    side, y_points = scaled_ref.shape[:2]
    end = side - margin
    box_ref[...] = jnp.zeros_like(box_ref)
    box_ref[:end, margin : margin + G, :y_points] = low_ref[...]
    box_ref[:end, :margin, :y_points] = z_before_ref[...]
    box_ref[:end, margin + G : side, :y_points] = z_after_ref[...]

    spread_potential(0, box_ref, scaled_ref)

    def first_step(x, carry):
        spread_potential(x + 1, box_ref, scaled_ref)
        slab_step(x, start_ref, scaled_ref, None, first_ref, None, margin)
        return carry

    lax.fori_loop(0, end, first_step, 0, unroll=5)
    steps(lambda i: (0, end - i), first_ref, start_ref, scaled_ref, pair_ref, margin)
    for e, value in enumerate(overlaps(pair_ref, 0, (end - FILTER + 1) * side * COL)):
        overlap_ref[e] = value


def basis_kernel(
    margin,
    x_after_ref,
    z_before_ref,
    z_after_ref,
    start_in,
    first_in,
    scaled_in,
    pair_in,
    overlap_ref,
    minus_x_ref,
    minus_z_ref,
    inverse_ref,
    raw_ref,
    start_ref,
    first_ref,
    scaled_ref,
    pair_ref,
    box_ref,
    matrix_ref,
    packed_ref,
    inner_ref,
    applied_ref,
):
    elements, columns = start_ref.shape[0], start_ref.shape[-1]
    side, y_points = scaled_ref.shape[:2]
    end = side - margin
    box_ref[...] = jnp.zeros_like(box_ref)
    box_ref[end:, margin : margin + G, :y_points] = x_after_ref[...]
    box_ref[end:, :margin, :y_points] = z_before_ref[...]
    box_ref[end:, margin + G : side, :y_points] = z_after_ref[...]
    for x in range(end, side):
        spread_potential(x, box_ref, scaled_ref)
    for x in range(end, side):
        slab_step(x, start_ref, scaled_ref, None, first_ref, None, margin)
    field = steps(
        lambda i: (end - i, side), first_ref, start_ref, scaled_ref, pair_ref, margin
    )
    rest = overlaps(pair_ref, (end - FILTER + 1) * side * COL, side * side * COL)

    own_operator(field, scaled_ref, inner_ref, applied_ref, raw_ref, margin)

    identity = (
        lax.broadcasted_iota(jnp.int32, (columns, columns), 0)
        == lax.broadcasted_iota(jnp.int32, (columns, columns), 1)
    ).astype(f32)
    grams = []
    for e in range(elements):
        products = overlap_ref[e] + rest[e]
        cross = products[:, columns:]
        grams.append(products[:, :columns] + (cross + cross.T))
    for e in range(0, elements, 2):
        pairs = [grams[e], grams[min(e + 1, elements - 1)]]
        for i, value in enumerate(pack(pairs) + pack([identity, identity])):
            matrix_ref[i] = value
        inverse_factors(matrix_ref, packed_ref)
        solved = pack([packed_ref[0], packed_ref[1]])
        for i in range(min(2, elements - e)):
            inverse_ref[e + i] = solved[i]

    for e in range(elements):
        held = weights(split(inverse_ref[e]), True)
        rows = []
        for d in (0, 2):
            rows += layer(field, margin, e, d, 0) + layer(field, margin, e, d, 1)
        faces = product(jnp.concatenate(rows, 0), held, True)
        minus_x_ref[e] = faces[: 2 * G * G]
        minus_z_ref[e] = faces[2 * G * G :]


def near_kernel(
    count,
    margin,
    inverse_ref,
    raw_ref,
    field,
    plus_ref,
    *rest,
):
    out_refs, near_ref = rest[:-1], rest[-1]
    elements, columns = inverse_ref.shape[0], inverse_ref.shape[-1]
    face = 2 * G * G
    minus, plus, held = [], [], []
    for e in range(elements):
        held.append(weights(split(inverse_ref[e]), True))
        rows = layer(field, margin, e, 1, 0) + layer(field, margin, e, 1, 1)
        for d in range(3):
            last = layer(field, margin, e, d, G - 1)
            before = layer(field, margin, e, d, G - 2)
            rows += [-(0.5 * a + 0.25 * b) for a, b in zip(last, before)]
            rows += [-0.25 * a for a in last]
        faces = product(jnp.concatenate(rows, 0), held[e], True)
        minus.append(faces[:face])
        plus.append(faces[face : 2 * face].T)
        plus_ref[e, 0] = plus[e]
        plus[e] = faces[2 * face : 3 * face].T
        plus_ref[e, 1] = faces[3 * face :].T

    for e in range(elements):
        half = product(inverse_ref[e], weights(split(raw_ref[e]), False), False)
        near_ref[0, e] = product(half, held[e], True)
        following = weights(split(minus[(e + 1) % elements]), False)
        near_ref[1, e] = product(plus[e], following, False)
    send_rows(count, near_ref, out_refs)


def partner(index, step, count):
    return index ^ step if count & (count - 1) == 0 else (index + step) % count


def partner(index, step, count):
    return index ^ step if count & (count - 1) == 0 else (index + step) % count


def send_rows(count, blocks_ref, out_refs):
    kinds, elements, size = blocks_ref.shape[:3]
    rows = size // count
    me = lax.axis_index("ez")
    for step, out_ref in enumerate(out_refs):
        owner = me ^ step if count & (count - 1) == 0 else lax.rem(me + step, count)
        at = pl.ds(pl.multiple_of(owner * rows, rows), rows)
        for kind in range(kinds):
            for e in range(elements):
                out_ref[:, kind, e, :] = blocks_ref[kind, e, at, :]


def far_kernel(count, plus_ref, next_x_ref, next_z_ref, *rest):
    out_refs, far_ref = rest[:-1], rest[-1]
    for e in range(plus_ref.shape[0]):
        for d, ref in ((0, next_x_ref), (1, next_z_ref)):
            far_ref[d, e] = product(plus_ref[e, d], weights(split(ref[e]), False), False)
    send_rows(count, far_ref, out_refs)


def place(refs, targets, semaphores):
    count = len(refs)
    me = lax.axis_index("ez")
    copies = []
    for step, ref in enumerate(refs):
        z = me ^ step if count & (count - 1) == 0 else lax.rem(me + (count - step), count)
        for kind, target in enumerate(targets(z)):
            copies.append(
                pltpu.make_async_copy(ref.at[:, kind], target, semaphores.at[step, kind])
            )
            copies[-1].start()
    for copy in copies:
        copy.wait()


def place_near_kernel(count, *refs):
    diagonal_ref, coupling_ref, semaphores = refs[count:]
    place(
        refs[:count],
        lambda z: (diagonal_ref.at[:, z], coupling_ref.at[:, z, 1]),
        semaphores,
    )


def place_far_kernel(count, *refs):
    coupling_ref, semaphores = refs[count + 1 :]
    place(
        refs[:count],
        lambda z: (coupling_ref.at[:, z, 0], coupling_ref.at[:, z, 2]),
        semaphores,
    )


def vmem(count):
    return [pl.BlockSpec(memory_space=pltpu.VMEM)] * count


def shift(block, axis, distance):
    count = lax.axis_size(axis)
    return lax.ppermute(block, axis, [(i, (i + distance) % count) for i in range(count)])


def exchange(block, step):
    count = lax.axis_size("ez")
    if step == 0:
        return block
    return lax.ppermute(block, "ez", [(i, partner(i, step, count)) for i in range(count)])


def local(potential, basis_start):
    elements, points, columns = basis_start.shape[2:]
    side = round(points ** (1 / 3))
    margin = (side - G) // 2
    y_points = potential.shape[1]
    count = lax.axis_size("ez")
    starts = basis_start.reshape(elements, points, columns)
    own = potential.transpose(0, 2, 1)
    own_scaled = lax.optimization_barrier((own + (3.0 - center)) * (2.0 / halfwidth))
    x_before = (shift(own, "ex", 1)[G - margin :] + (3.0 - center)) * (2.0 / halfwidth)
    x_after = shift(own_scaled[:margin], "ex", -1)

    shape = jax.ShapeDtypeStruct
    field = shape((elements, side + 2, LEAD + COL * side + LEAD, columns), f32)
    scaled = shape((side, y_points, COL, columns), f32)
    start, first = pl.pallas_call(
        first_kernel,
        out_shape=[field, field],
        in_specs=vmem(1),
        out_specs=vmem(2),
        scratch_shapes=[pltpu.VMEM((elements, side * side + COL, columns), f32)],
        compiler_params=pltpu.CompilerParams(vmem_limit_bytes=24 * 2**20),
        cost_estimate=pl.CostEstimate(flops=10**5, bytes_accessed=10**4, transcendentals=0),
        name="first",
    )(starts)
    low = lax.optimization_barrier(jnp.concatenate([x_before, own_scaled], axis=0))
    z_before = shift(low[:, G - margin :], "ez", 1)
    z_after = shift(low[:, :margin], "ez", -1)
    edge_before = shift(x_after[:, G - margin :], "ez", 1)
    edge_after = shift(x_after[:, :margin], "ez", -1)
    pair = shape((elements, side * side * COL, 2 * columns), bf16)
    overlap = shape((elements, columns, 2 * columns), f32)
    box = pltpu.VMEM((side, COL, 128), f32)
    start, first, most_scaled, pairs, overlapped = pl.pallas_call(
        functools.partial(middle_kernel, margin),
        out_shape=[field, field, scaled, pair, overlap],
        in_specs=vmem(5),
        out_specs=vmem(5),
        input_output_aliases={3: 0, 4: 1},
        scratch_shapes=[box],
        compiler_params=pltpu.CompilerParams(vmem_limit_bytes=32 * 2**20),
        cost_estimate=pl.CostEstimate(flops=10**8, bytes_accessed=10**7, transcendentals=0),
        name="middle",
    )(low, z_before, z_after, start, first)

    face = shape((elements, 2 * G * G, columns), f32)
    square = shape((elements, columns, columns), f32)
    minus_x, minus_z, inverse, raw, _, filtered, _, _ = pl.pallas_call(
        functools.partial(basis_kernel, margin),
        out_shape=[face, face, square, square, field, field, scaled, pair],
        in_specs=vmem(8),
        out_specs=vmem(8),
        input_output_aliases={3: 4, 4: 5, 5: 6, 6: 7},
        scratch_shapes=[
            box,
            pltpu.VMEM((4, columns, columns), f32),
            pltpu.VMEM((2, columns, columns), f32),
            pltpu.VMEM((elements, G**3, 2 * columns), bf16),
            pltpu.VMEM((elements, G**3, 2 * columns), bf16),
        ],
        compiler_params=pltpu.CompilerParams(vmem_limit_bytes=32 * 2**20),
        name="basis",
    )(x_after, edge_before, edge_after, start, first, most_scaled, pairs, overlapped)

    next_x = shift(minus_x, "ex", -1)
    next_z = shift(minus_z, "ez", -1)
    rows = columns // count
    block = shape((rows, 2, elements, columns), f32)
    squares = pltpu.VMEM((2, elements, columns, columns), f32)
    plus, *near = pl.pallas_call(
        functools.partial(near_kernel, count, margin),
        out_shape=[shape((elements, 2, columns, 2 * G * G), f32)] + [block] * count,
        in_specs=vmem(3),
        out_specs=vmem(1 + count),
        scratch_shapes=[squares],
        compiler_params=pltpu.CompilerParams(vmem_limit_bytes=24 * 2**20),
        cost_estimate=pl.CostEstimate(flops=10**8, bytes_accessed=10**7, transcendentals=0),
        name="near",
    )(inverse, raw, filtered)
    near = [exchange(value, step) for step, value in enumerate(near)]

    far = pl.pallas_call(
        functools.partial(far_kernel, count),
        out_shape=[block] * count,
        in_specs=vmem(3),
        out_specs=vmem(count),
        scratch_shapes=[squares],
        compiler_params=pltpu.CompilerParams(vmem_limit_bytes=16 * 2**20),
        name="far",
    )(plus, next_x, next_z)
    far = [exchange(far[step], step) for step in reversed(range(count))][::-1]

    anywhere = pl.BlockSpec(memory_space=pltpu.HBM)
    semaphores = pltpu.SemaphoreType.DMA((count, 2))
    half = shape((rows, count, 3, elements, columns), f32)
    diagonal, coupled = pl.pallas_call(
        functools.partial(place_near_kernel, count),
        out_shape=[shape((rows, count, elements, columns), f32), half],
        in_specs=vmem(count),
        out_specs=[anywhere] * 2,
        scratch_shapes=[semaphores],
        compiler_params=pltpu.CompilerParams(vmem_limit_bytes=16 * 2**20),
        name="place_near",
    )(*near)
    coupled = pl.pallas_call(
        functools.partial(place_far_kernel, count),
        out_shape=half,
        in_specs=vmem(count) + [anywhere],
        out_specs=anywhere,
        input_output_aliases={count: 0},
        scratch_shapes=[semaphores],
        compiler_params=pltpu.CompilerParams(vmem_limit_bytes=16 * 2**20),
        name="place_far",
    )(*far, coupled)
    return (diagonal[None], coupled.transpose(0, 1, 3, 2, 4)[None])


def solution(mesh):
    return jax.shard_map(
        local,
        mesh=mesh,
        in_specs=(P("ex", None, "ez"), P("ex", "ez", None, None, None)),
        out_specs=(P("ex", "ez", None, None, None), P("ex", "ez", None, None, None, None)),
        check_vma=False,
    )
```

```python
import functools

import jax
import jax.numpy as jnp
from jax import lax
from jax.experimental import pallas as pl
from jax.experimental.pallas import tpu as pltpu
from jax.sharding import PartitionSpec as P

G = 8
FILTER = 3

center = 6.5
halfwidth = 5.5

f32 = jnp.float32
bf16 = jnp.bfloat16

LEAD = 8
COL = 16
BLOCK = 16


def split(value):
    high = value.astype(bf16)
    return high, (value - high.astype(f32)).astype(bf16)


def weights(pair, transposed):
    high, low = pair
    empty = jnp.zeros_like(low)
    if transposed:
        upper = jnp.concatenate([high, high], axis=1)
        lower = jnp.concatenate([low, empty], axis=1)
        return jnp.concatenate([upper, lower], axis=0)
    upper = jnp.concatenate([high, low], axis=1)
    lower = jnp.concatenate([high, empty], axis=1)
    return jnp.concatenate([upper, lower], axis=0)


def product(value, held, transposed):
    pair = jnp.concatenate(split(value), axis=1)
    dims = (((1,), (1 if transposed else 0,)), ((), ()))
    both = lax.dot_general(pair, held, dims, preferred_element_type=f32)
    half = both.shape[1] // 2
    return both[:, :half] + both[:, half:]


def bcast_row(value, k):
    return jnp.broadcast_to(value[k : k + 1, :], value.shape)


def bcast_lane(value, k, lanes):
    return jnp.broadcast_to(value[:, k : k + 1], (value.shape[0], lanes))


def pack(values):
    first, second = values
    half = first.shape[1] // 2
    left = lax.broadcasted_iota(jnp.int32, first.shape, 1) < half
    return (
        jnp.where(left, first, pltpu.roll(second, half, 1)),
        jnp.where(left, pltpu.roll(first, half, 1), second),
    )


def tree_sum(terms):
    while len(terms) > 1:
        terms = [a + b for a, b in zip(terms[::2], terms[1::2])] + terms[len(terms) & ~1 :]
    return terms[0]


def triple(value):
    high = value.astype(bf16).astype(f32)
    middle = (value - high).astype(bf16).astype(f32)
    return high, middle, value - high - middle


def far_rows(value, solved, at):
    size = value.shape[1]
    half = size // 2
    lane = lax.broadcasted_iota(jnp.int32, value.shape, 1) % half
    parts = triple(jnp.where((lane >= at) & (lane < at + BLOCK), value, 0.0))
    left = lax.broadcasted_iota(jnp.int32, (BLOCK, size), 1) < half
    taken = [[], []]
    for part in solved:
        pieces = triple(part)
        taken[0].append([jnp.where(left, piece, 0.0).astype(bf16) for piece in pieces])
        taken[1].append([jnp.where(left, 0.0, piece).astype(bf16) for piece in pieces])
    nothing = jnp.zeros((BLOCK, size * len(solved)), bf16)
    spots = half // BLOCK
    pairs = ((0, 0), (0, 1), (1, 0), (0, 2), (2, 0), (1, 1))
    operands, tiles = [], []
    for first in range(0, len(pairs), spots):
        operand, group = None, [nothing] * (2 * spots)
        for i, (mine, theirs) in enumerate(pairs[first : first + spots]):
            moved = pltpu.roll(parts[mine], i * BLOCK, 1) if i else parts[mine]
            operand = moved if operand is None else operand + moved
            for side in range(2):
                spot = (side * spots + at // BLOCK + i) % (2 * spots)
                group[spot] = jnp.concatenate([t[theirs] for t in taken[side]], axis=1)
        operands.append(operand.astype(bf16))
        tiles += group
    return jnp.dot(
        jnp.concatenate(operands, axis=1),
        jnp.concatenate(tiles, axis=0),
        preferred_element_type=f32,
    )


def inverse_factors(matrix_ref, inverse_ref):
    size = matrix_ref.shape[1]
    half = size // 2
    row = lax.broadcasted_iota(jnp.int32, (BLOCK, size), 0)
    lane = lax.broadcasted_iota(jnp.int32, (BLOCK, size), 1)
    other = jnp.where(lane < half, 0, half)

    def columns_of(value, at):
        return jnp.take_along_axis(value, other + at, axis=1)

    parts = (0, 1, 2)
    panel = [matrix_ref[part, :BLOCK, :] for part in parts]
    columns = [columns_of(panel[0], j) for j in range(BLOCK)]
    for start in range(0, size, BLOCK):
        rows = slice(start, start + BLOCK)
        at = start % half
        below = start + BLOCK
        if below < size:
            values = [matrix_ref[part, below : below + BLOCK, :] for part in parts]
        pivot_rows = list(panel)
        pivot = bcast_row(columns[0], 0)
        for k in range(BLOCK):
            reciprocal = 1.0 / pivot
            if k == 0:
                pivots, reciprocals = pivot, reciprocal
            else:
                later = row >= k
                pivots = jnp.where(later, pivot, pivots)
                reciprocals = jnp.where(later, reciprocal, reciprocals)
                pivot_rows = [jnp.where(later, new, old) for new, old in zip(panel, pivot_rows)]
            if k + 1 < BLOCK:
                beside = bcast_row(columns[k + 1], k)
                pivot = bcast_row(columns[k + 1], k + 1) - (beside * beside) * reciprocal
            factor = jnp.where(row == k, 0.0, columns[k]) * reciprocal
            for j in range(k + 1, BLOCK):
                columns[j] = columns[j] - factor * bcast_row(columns[j], k)
            panel = [value - factor * bcast_row(value, k) for value in panel]
            if k == 8 and below < size:
                factors = [columns_of(values[0], at + j) for j in range(BLOCK)]
        solved = [value * reciprocals for value in panel]
        scale = lax.rsqrt(pivots)
        kept = [value * scale for value in pivot_rows]
        inverse_ref[0, rows, :] = kept[parts.index(2)]
        inverse_ref[1, rows, :] = kept[parts.index(3)] if 3 in parts else jnp.zeros_like(scale)
        if below == size:
            break
        panel = []
        for value, taken in zip(values, solved):
            terms = [factors[k] * bcast_row(taken, k) for k in range(BLOCK)]
            panel.append(value - tree_sum(terms))
        if below == half:
            panel = panel[1:] + [matrix_ref[3, below : below + BLOCK, :]]
        columns = [columns_of(panel[0], below % half + j) for j in range(BLOCK)]
        rest = slice(below + BLOCK, size)
        if below + BLOCK < size:
            taken = far_rows(matrix_ref[parts[0], rest, :], solved, at)
            for i, part in enumerate(parts):
                mine = taken[:, i * size : (i + 1) * size]
                matrix_ref[part, rest, :] = matrix_ref[part, rest, :] - mine
        if below == half:
            parts = (1, 2, 3)


def zero_ends(ref, elements, side):
    for e in range(elements):
        ref[e, 0] = jnp.zeros(ref.shape[2:], f32)
        ref[e, side + 1] = jnp.zeros(ref.shape[2:], f32)
        for x in range(side):
            ref[e, x + 1, :LEAD] = jnp.zeros((LEAD, ref.shape[-1]), f32)
            ref[e, x + 1, LEAD + COL * side :] = jnp.zeros((LEAD, ref.shape[-1]), f32)


def beside_weight(side, columns):
    inside = lax.broadcasted_iota(jnp.int32, (COL, columns), 0) < side
    return jnp.where(inside, 1.0 / halfwidth, 0.0)


def slab_step(x, source, scaled_ref, previous, target, pair_ref, margin):
    elements, side = source.shape[0], source.shape[1] - 2
    columns = source.shape[-1]
    weight = beside_weight(side, columns)
    for e in range(elements):

        def column(y):
            return source[e, x + 1, LEAD + COL * y : LEAD + COL * (y + 1)]

        before, here = None, column(0)
        for y in range(side):
            low = LEAD + COL * y
            after = column(y + 1) if y + 1 < side else None
            beside = source[e, x, low : low + COL] + source[e, x + 2, low : low + COL]
            beside = beside + (
                source[e, x + 1, low - 1 : low - 1 + COL]
                + source[e, x + 1, low + 1 : low + 1 + COL]
            )
            if before is not None:
                beside = beside + before
            if after is not None:
                beside = beside + after
            scaled = scaled_ref[x, (e * G - margin + y) % scaled_ref.shape[1]]
            value = scaled * here - weight * beside
            if previous is None:
                value = 0.5 * value
            else:
                value = value - previous[e, x + 1, low : low + COL]
            target[e, x + 1, low : low + COL] = value
            if pair_ref is not None:
                high, rest = split(value)
                at = pl.multiple_of(x * (side * COL), COL) + COL * y
                pair_ref[e, pl.ds(at, COL), :columns] = high
                pair_ref[e, pl.ds(at, COL), columns:] = rest
            before, here = here, after


def first_kernel(start_ref, field_ref, next_ref, flat_ref):
    elements, columns = start_ref.shape[0], start_ref.shape[-1]
    side = field_ref.shape[1] - 2
    slab = side * side
    zero_ends(field_ref, elements, side)
    zero_ends(next_ref, elements, side)
    inside = lax.broadcasted_iota(jnp.int32, (COL, columns), 0) < side

    def prepare(x, carry):
        for e in range(elements):
            flat_ref[e, :slab] = start_ref[e, pl.ds(pl.multiple_of(x * slab, 16), slab), :].astype(f32)
            for y in range(side):
                value = jnp.where(inside, flat_ref[e, side * y : side * y + COL], 0.0)
                field_ref[e, x + 1, LEAD + COL * y : LEAD + COL * (y + 1)] = value
        return carry

    lax.fori_loop(0, side, prepare, 0, unroll=2)


def point_rows(field, margin, e, x, y):
    low = LEAD + COL * (margin + y) + margin
    return field[e, margin + x + 1, low : low + G]


def layer(field, margin, e, d, i):
    if d == 0:
        return [point_rows(field, margin, e, i, y) for y in range(G)]
    if d == 1:
        return [point_rows(field, margin, e, x, i) for x in range(G)]
    low = LEAD + COL * margin + margin + i
    return [field[e, margin + x + 1, pl.ds(low, G, stride=COL)] for x in range(G)]


def spread_potential(x, box_ref, scaled_ref):
    rows = box_ref[x]
    for y in range(scaled_ref.shape[1]):
        scaled_ref[x, y] = bcast_lane(rows, y, scaled_ref.shape[-1])


def steps(ranges, first_ref, start_ref, scaled_ref, pair_ref, margin):
    fields = (first_ref, start_ref)
    for index in range(1, FILTER):
        source, target = fields
        pair = pair_ref if index == FILTER - 1 else None

        def next_step(x, carry):
            slab_step(x, source, scaled_ref, target, target, pair, margin)
            return carry

        low, high = ranges(index)
        lax.fori_loop(low, high, next_step, 0, unroll=min(4, high - low))
        fields = fields[::-1]
    return fields[0]


def overlaps(pair_ref, low, high):
    columns = pair_ref.shape[-1] // 2
    return [
        lax.dot_general(
            pair_ref[e, low:high, :columns],
            pair_ref[e, low:high],
            (((0,), (0,)), ((), ())),
            preferred_element_type=f32,
        )
        for e in range(pair_ref.shape[0])
    ]


def own_operator(field, scaled_ref, inner_ref, applied_ref, raw_ref, margin):
    elements, columns = field.shape[0], field.shape[-1]
    y_points = scaled_ref.shape[1]

    z = lax.broadcasted_iota(jnp.int32, (G, columns), 0)
    edge = (z == 1) | (z == G - 1)
    weight_down = jnp.where(z == 0, 0.0, jnp.where(edge, 0.25, 0.5))
    edge = (z == 0) | (z == G - 2)
    weight_up = jnp.where(z == G - 1, 0.0, jnp.where(edge, 0.25, 0.5))

    def link(i):
        return 0.25 if i in (0, G - 2) else 0.5

    for e in range(elements):
        for x in range(G):
            for y in range(0, G, 2):
                inner_pair, applied_pair = [], []
                for yy in (y, y + 1):
                    here = point_rows(field, margin, e, x, yy)
                    potential = scaled_ref[margin + x, (e * G + yy) % y_points, margin : margin + G]
                    value = (0.5 * halfwidth * potential + center) * here
                    value = value - weight_down * pltpu.roll(here, 1, 0)
                    value = value - weight_up * pltpu.roll(here, G - 1, 0)
                    if x > 0:
                        value = value - link(x - 1) * point_rows(field, margin, e, x - 1, yy)
                    if x < G - 1:
                        value = value - link(x) * point_rows(field, margin, e, x + 1, yy)
                    if yy > 0:
                        value = value - link(yy - 1) * point_rows(field, margin, e, x, yy - 1)
                    if yy < G - 1:
                        value = value - link(yy) * point_rows(field, margin, e, x, yy + 1)
                    inner_pair.append(here)
                    applied_pair.append(value)
                at = slice((x * G + y) * G, (x * G + y + 2) * G)
                for ref, pair in ((inner_ref, inner_pair), (applied_ref, applied_pair)):
                    high, low = split(jnp.concatenate(pair, axis=0))
                    ref[e, at, :columns] = high
                    ref[e, at, columns:] = low

    for e in range(elements):
        both = lax.dot_general(
            inner_ref[e, :, :columns],
            applied_ref[e],
            (((0,), (0,)), ((), ())),
            preferred_element_type=f32,
        )
        raw = both[:, :columns] + both[:, columns:]
        raw = raw + lax.dot_general(
            inner_ref[e, :, columns:],
            applied_ref[e, :, :columns],
            (((0,), (0,)), ((), ())),
            preferred_element_type=f32,
        )
        raw_ref[e] = raw


def middle_kernel(
    margin,
    low_ref,
    z_before_ref,
    z_after_ref,
    start_in,
    first_in,
    start_ref,
    first_ref,
    scaled_ref,
    pair_ref,
    overlap_ref,
    box_ref,
):
    side, y_points = scaled_ref.shape[:2]
    end = side - margin
    box_ref[...] = jnp.zeros_like(box_ref)
    box_ref[:end, margin : margin + G, :y_points] = low_ref[...]
    box_ref[:end, :margin, :y_points] = z_before_ref[...]
    box_ref[:end, margin + G : side, :y_points] = z_after_ref[...]

    spread_potential(0, box_ref, scaled_ref)

    def first_step(x, carry):
        spread_potential(x + 1, box_ref, scaled_ref)
        slab_step(x, start_ref, scaled_ref, None, first_ref, None, margin)
        return carry

    lax.fori_loop(0, end, first_step, 0, unroll=5)
    steps(lambda i: (0, end - i), first_ref, start_ref, scaled_ref, pair_ref, margin)
    for e, value in enumerate(overlaps(pair_ref, 0, (end - FILTER + 1) * side * COL)):
        overlap_ref[e] = value


def basis_kernel(
    margin,
    x_after_ref,
    z_before_ref,
    z_after_ref,
    start_in,
    first_in,
    scaled_in,
    pair_in,
    overlap_ref,
    minus_x_ref,
    minus_z_ref,
    inverse_ref,
    raw_ref,
    start_ref,
    first_ref,
    scaled_ref,
    pair_ref,
    box_ref,
    matrix_ref,
    packed_ref,
    inner_ref,
    applied_ref,
):
    elements, columns = start_ref.shape[0], start_ref.shape[-1]
    side, y_points = scaled_ref.shape[:2]
    end = side - margin
    box_ref[...] = jnp.zeros_like(box_ref)
    box_ref[end:, margin : margin + G, :y_points] = x_after_ref[...]
    box_ref[end:, :margin, :y_points] = z_before_ref[...]
    box_ref[end:, margin + G : side, :y_points] = z_after_ref[...]
    for x in range(end, side):
        spread_potential(x, box_ref, scaled_ref)
    for x in range(end, side):
        slab_step(x, start_ref, scaled_ref, None, first_ref, None, margin)
    field = steps(
        lambda i: (end - i, side), first_ref, start_ref, scaled_ref, pair_ref, margin
    )
    rest = overlaps(pair_ref, (end - FILTER + 1) * side * COL, side * side * COL)

    own_operator(field, scaled_ref, inner_ref, applied_ref, raw_ref, margin)

    identity = (
        lax.broadcasted_iota(jnp.int32, (columns, columns), 0)
        == lax.broadcasted_iota(jnp.int32, (columns, columns), 1)
    ).astype(f32)
    grams = []
    for e in range(elements):
        products = overlap_ref[e] + rest[e]
        cross = products[:, columns:]
        grams.append(products[:, :columns] + (cross + cross.T))
    for e in range(0, elements, 2):
        pairs = [grams[e], grams[min(e + 1, elements - 1)]]
        for i, value in enumerate(pack(pairs) + pack([identity, identity])):
            matrix_ref[i] = value
        inverse_factors(matrix_ref, packed_ref)
        solved = pack([packed_ref[0], packed_ref[1]])
        for i in range(min(2, elements - e)):
            inverse_ref[e + i] = solved[i]

    for e in range(elements):
        held = weights(split(inverse_ref[e]), True)
        rows = []
        for d in (0, 2):
            rows += layer(field, margin, e, d, 0) + layer(field, margin, e, d, 1)
        faces = product(jnp.concatenate(rows, 0), held, True)
        minus_x_ref[e] = faces[: 2 * G * G]
        minus_z_ref[e] = faces[2 * G * G :]


def near_kernel(
    count,
    margin,
    inverse_ref,
    raw_ref,
    field,
    plus_ref,
    *rest,
):
    out_refs, near_ref = rest[:-1], rest[-1]
    elements, columns = inverse_ref.shape[0], inverse_ref.shape[-1]
    face = 2 * G * G
    minus, plus, held = [], [], []
    for e in range(elements):
        held.append(weights(split(inverse_ref[e]), True))
        rows = layer(field, margin, e, 1, 0) + layer(field, margin, e, 1, 1)
        for d in range(3):
            last = layer(field, margin, e, d, G - 1)
            before = layer(field, margin, e, d, G - 2)
            rows += [-(0.5 * a + 0.25 * b) for a, b in zip(last, before)]
            rows += [-0.25 * a for a in last]
        faces = product(jnp.concatenate(rows, 0), held[e], True)
        minus.append(faces[:face])
        plus.append(faces[face : 2 * face].T)
        plus_ref[e, 0] = plus[e]
        plus[e] = faces[2 * face : 3 * face].T
        plus_ref[e, 1] = faces[3 * face :].T

    for e in range(elements):
        half = product(inverse_ref[e], weights(split(raw_ref[e]), False), False)
        near_ref[0, e] = product(half, held[e], True)
        following = weights(split(minus[(e + 1) % elements]), False)
        near_ref[1, e] = product(plus[e], following, False)
    send_rows(count, near_ref, out_refs)


def partner(index, step, count):
    return index ^ step if count & (count - 1) == 0 else (index + step) % count


def partner(index, step, count):
    return index ^ step if count & (count - 1) == 0 else (index + step) % count


def send_rows(count, blocks_ref, out_refs):
    kinds, elements, size = blocks_ref.shape[:3]
    rows = size // count
    me = lax.axis_index("ez")
    for step, out_ref in enumerate(out_refs):
        owner = me ^ step if count & (count - 1) == 0 else lax.rem(me + step, count)
        at = pl.ds(pl.multiple_of(owner * rows, rows), rows)
        for kind in range(kinds):
            for e in range(elements):
                out_ref[:, kind, e, :] = blocks_ref[kind, e, at, :]


def far_kernel(count, plus_ref, next_x_ref, next_z_ref, *rest):
    out_refs, far_ref = rest[:-1], rest[-1]
    for e in range(plus_ref.shape[0]):
        for d, ref in ((0, next_x_ref), (1, next_z_ref)):
            far_ref[d, e] = product(plus_ref[e, d], weights(split(ref[e]), False), False)
    send_rows(count, far_ref, out_refs)


def place(refs, targets, semaphores):
    count = len(refs)
    me = lax.axis_index("ez")
    copies = []
    for step, ref in enumerate(refs):
        z = me ^ step if count & (count - 1) == 0 else lax.rem(me + (count - step), count)
        for kind, target in enumerate(targets(z)):
            copies.append(
                pltpu.make_async_copy(ref.at[:, kind], target, semaphores.at[step, kind])
            )
            copies[-1].start()
    for copy in copies:
        copy.wait()


def place_near_kernel(count, *refs):
    diagonal_ref, coupling_ref, semaphores = refs[count:]
    place(
        refs[:count],
        lambda z: (diagonal_ref.at[:, z], coupling_ref.at[:, z, 1]),
        semaphores,
    )


def place_far_kernel(count, *refs):
    coupling_ref, semaphores = refs[count + 1 :]
    place(
        refs[:count][::-1],
        lambda z: (coupling_ref.at[:, z, 0], coupling_ref.at[:, z, 2]),
        semaphores,
    )


def vmem(count):
    return [pl.BlockSpec(memory_space=pltpu.VMEM)] * count


def shift(block, axis, distance):
    count = lax.axis_size(axis)
    return lax.ppermute(block, axis, [(i, (i + distance) % count) for i in range(count)])


def exchange(block, step):
    count = lax.axis_size("ez")
    if step == 0:
        return block
    return lax.ppermute(block, "ez", [(i, partner(i, step, count)) for i in range(count)])


def local(potential, basis_start):
    elements, points, columns = basis_start.shape[2:]
    side = round(points ** (1 / 3))
    margin = (side - G) // 2
    y_points = potential.shape[1]
    count = lax.axis_size("ez")
    starts = basis_start.reshape(elements, points, columns)
    own = potential.transpose(0, 2, 1)
    own_scaled = lax.optimization_barrier((own + (3.0 - center)) * (2.0 / halfwidth))
    x_before = (shift(own, "ex", 1)[G - margin :] + (3.0 - center)) * (2.0 / halfwidth)
    x_after = shift(own_scaled[:margin], "ex", -1)

    shape = jax.ShapeDtypeStruct
    field = shape((elements, side + 2, LEAD + COL * side + LEAD, columns), f32)
    scaled = shape((side, y_points, COL, columns), f32)
    start, first = pl.pallas_call(
        first_kernel,
        out_shape=[field, field],
        in_specs=vmem(1),
        out_specs=vmem(2),
        scratch_shapes=[pltpu.VMEM((elements, side * side + COL, columns), f32)],
        compiler_params=pltpu.CompilerParams(vmem_limit_bytes=24 * 2**20),
        cost_estimate=pl.CostEstimate(flops=10**5, bytes_accessed=10**4, transcendentals=0),
        name="first",
    )(starts)
    low = lax.optimization_barrier(jnp.concatenate([x_before, own_scaled], axis=0))
    z_before = shift(low[:, G - margin :], "ez", 1)
    z_after = shift(low[:, :margin], "ez", -1)
    edge_before = shift(x_after[:, G - margin :], "ez", 1)
    edge_after = shift(x_after[:, :margin], "ez", -1)
    pair = shape((elements, side * side * COL, 2 * columns), bf16)
    overlap = shape((elements, columns, 2 * columns), f32)
    box = pltpu.VMEM((side, COL, 128), f32)
    start, first, most_scaled, pairs, overlapped = pl.pallas_call(
        functools.partial(middle_kernel, margin),
        out_shape=[field, field, scaled, pair, overlap],
        in_specs=vmem(5),
        out_specs=vmem(5),
        input_output_aliases={3: 0, 4: 1},
        scratch_shapes=[box],
        compiler_params=pltpu.CompilerParams(vmem_limit_bytes=32 * 2**20),
        cost_estimate=pl.CostEstimate(flops=10**8, bytes_accessed=10**7, transcendentals=0),
        name="middle",
    )(low, z_before, z_after, start, first)

    face = shape((elements, 2 * G * G, columns), f32)
    square = shape((elements, columns, columns), f32)
    minus_x, minus_z, inverse, raw, _, filtered, _, _ = pl.pallas_call(
        functools.partial(basis_kernel, margin),
        out_shape=[face, face, square, square, field, field, scaled, pair],
        in_specs=vmem(8),
        out_specs=vmem(8),
        input_output_aliases={3: 4, 4: 5, 5: 6, 6: 7},
        scratch_shapes=[
            box,
            pltpu.VMEM((4, columns, columns), f32),
            pltpu.VMEM((2, columns, columns), f32),
            pltpu.VMEM((elements, G**3, 2 * columns), bf16),
            pltpu.VMEM((elements, G**3, 2 * columns), bf16),
        ],
        compiler_params=pltpu.CompilerParams(vmem_limit_bytes=32 * 2**20),
        name="basis",
    )(x_after, edge_before, edge_after, start, first, most_scaled, pairs, overlapped)

    next_x = shift(minus_x, "ex", -1)
    next_z = shift(minus_z, "ez", -1)
    rows = columns // count
    block = shape((rows, 2, elements, columns), f32)
    squares = pltpu.VMEM((2, elements, columns, columns), f32)
    plus, *near = pl.pallas_call(
        functools.partial(near_kernel, count, margin),
        out_shape=[shape((elements, 2, columns, 2 * G * G), f32)] + [block] * count,
        in_specs=vmem(3),
        out_specs=vmem(1 + count),
        scratch_shapes=[squares],
        compiler_params=pltpu.CompilerParams(vmem_limit_bytes=24 * 2**20),
        cost_estimate=pl.CostEstimate(flops=10**8, bytes_accessed=10**7, transcendentals=0),
        name="near",
    )(inverse, raw, filtered)
    near = [exchange(value, step) for step, value in enumerate(near)]

    far = pl.pallas_call(
        functools.partial(far_kernel, count),
        out_shape=[block] * count,
        in_specs=vmem(3),
        out_specs=vmem(count),
        scratch_shapes=[squares],
        compiler_params=pltpu.CompilerParams(vmem_limit_bytes=16 * 2**20),
        name="far",
    )(plus, next_x, next_z)
    far = [exchange(far[step], step) for step in reversed(range(count))][::-1]

    anywhere = pl.BlockSpec(memory_space=pltpu.HBM)
    semaphores = pltpu.SemaphoreType.DMA((count, 2))
    half = shape((rows, count, 3, elements, columns), f32)
    diagonal, coupled = pl.pallas_call(
        functools.partial(place_near_kernel, count),
        out_shape=[shape((rows, count, elements, columns), f32), half],
        in_specs=vmem(count),
        out_specs=[anywhere] * 2,
        scratch_shapes=[semaphores],
        compiler_params=pltpu.CompilerParams(vmem_limit_bytes=16 * 2**20),
        name="place_near",
    )(*near)
    coupled = pl.pallas_call(
        functools.partial(place_far_kernel, count),
        out_shape=half,
        in_specs=vmem(count) + [anywhere],
        out_specs=anywhere,
        input_output_aliases={count: 0},
        scratch_shapes=[semaphores],
        compiler_params=pltpu.CompilerParams(vmem_limit_bytes=16 * 2**20),
        name="place_far",
    )(*far[::-1], coupled)
    return (diagonal[None], coupled.transpose(0, 1, 3, 2, 4)[None])


def solution(mesh):
    return jax.shard_map(
        local,
        mesh=mesh,
        in_specs=(P("ex", None, "ez"), P("ex", "ez", None, None, None)),
        out_specs=(P("ex", "ez", None, None, None), P("ex", "ez", None, None, None, None)),
        check_vma=False,
    )
```

```python
import functools

import jax
import jax.numpy as jnp
from jax import lax
from jax.experimental import pallas as pl
from jax.experimental.pallas import tpu as pltpu
from jax.sharding import PartitionSpec as P

G = 8
FILTER = 3

center = 6.5
halfwidth = 5.5

f32 = jnp.float32
bf16 = jnp.bfloat16

LEAD = 8
COL = 16
BLOCK = 16


def split(value):
    high = value.astype(bf16)
    return high, (value - high.astype(f32)).astype(bf16)


def weights(pair, transposed):
    high, low = pair
    empty = jnp.zeros_like(low)
    if transposed:
        upper = jnp.concatenate([high, high], axis=1)
        lower = jnp.concatenate([low, empty], axis=1)
        return jnp.concatenate([upper, lower], axis=0)
    upper = jnp.concatenate([high, low], axis=1)
    lower = jnp.concatenate([high, empty], axis=1)
    return jnp.concatenate([upper, lower], axis=0)


def product(value, held, transposed):
    pair = jnp.concatenate(split(value), axis=1)
    dims = (((1,), (1 if transposed else 0,)), ((), ()))
    both = lax.dot_general(pair, held, dims, preferred_element_type=f32)
    half = both.shape[1] // 2
    return both[:, :half] + both[:, half:]


def bcast_row(value, k):
    return jnp.broadcast_to(value[k : k + 1, :], value.shape)


def bcast_lane(value, k, lanes):
    return jnp.broadcast_to(value[:, k : k + 1], (value.shape[0], lanes))


def pack(values):
    first, second = values
    half = first.shape[1] // 2
    left = lax.broadcasted_iota(jnp.int32, first.shape, 1) < half
    return (
        jnp.where(left, first, pltpu.roll(second, half, 1)),
        jnp.where(left, pltpu.roll(first, half, 1), second),
    )


def tree_sum(terms):
    while len(terms) > 1:
        terms = [a + b for a, b in zip(terms[::2], terms[1::2])] + terms[len(terms) & ~1 :]
    return terms[0]


def triple(value):
    high = value.astype(bf16).astype(f32)
    middle = (value - high).astype(bf16).astype(f32)
    return high, middle, value - high - middle


def far_rows(value, solved, at):
    size = value.shape[1]
    half = size // 2
    lane = lax.broadcasted_iota(jnp.int32, value.shape, 1) % half
    parts = triple(jnp.where((lane >= at) & (lane < at + BLOCK), value, 0.0))
    left = lax.broadcasted_iota(jnp.int32, (BLOCK, size), 1) < half
    taken = [[], []]
    for part in solved:
        pieces = triple(part)
        taken[0].append([jnp.where(left, piece, 0.0).astype(bf16) for piece in pieces])
        taken[1].append([jnp.where(left, 0.0, piece).astype(bf16) for piece in pieces])
    nothing = jnp.zeros((BLOCK, size * len(solved)), bf16)
    spots = half // BLOCK
    pairs = ((0, 0), (0, 1), (1, 0), (0, 2), (2, 0), (1, 1))
    operands, tiles = [], []
    for first in range(0, len(pairs), spots):
        operand, group = None, [nothing] * (2 * spots)
        for i, (mine, theirs) in enumerate(pairs[first : first + spots]):
            moved = pltpu.roll(parts[mine], i * BLOCK, 1) if i else parts[mine]
            operand = moved if operand is None else operand + moved
            for side in range(2):
                spot = (side * spots + at // BLOCK + i) % (2 * spots)
                group[spot] = jnp.concatenate([t[theirs] for t in taken[side]], axis=1)
        operands.append(operand.astype(bf16))
        tiles += group
    return jnp.dot(
        jnp.concatenate(operands, axis=1),
        jnp.concatenate(tiles, axis=0),
        preferred_element_type=f32,
    )


def inverse_factors(matrix_ref, inverse_ref):
    size = matrix_ref.shape[1]
    half = size // 2
    row = lax.broadcasted_iota(jnp.int32, (BLOCK, size), 0)
    lane = lax.broadcasted_iota(jnp.int32, (BLOCK, size), 1)
    other = jnp.where(lane < half, 0, half)

    def columns_of(value, at):
        return jnp.take_along_axis(value, other + at, axis=1)

    parts = (0, 1, 2)
    panel = [matrix_ref[part, :BLOCK, :] for part in parts]
    columns = [columns_of(panel[0], j) for j in range(BLOCK)]
    for start in range(0, size, BLOCK):
        rows = slice(start, start + BLOCK)
        at = start % half
        below = start + BLOCK
        if below < size:
            values = [matrix_ref[part, below : below + BLOCK, :] for part in parts]
        pivot_rows = list(panel)
        pivot = bcast_row(columns[0], 0)
        for k in range(BLOCK):
            reciprocal = 1.0 / pivot
            if k == 0:
                pivots, reciprocals = pivot, reciprocal
            else:
                later = row >= k
                pivots = jnp.where(later, pivot, pivots)
                reciprocals = jnp.where(later, reciprocal, reciprocals)
                pivot_rows = [jnp.where(later, new, old) for new, old in zip(panel, pivot_rows)]
            if k + 1 < BLOCK:
                beside = bcast_row(columns[k + 1], k)
                pivot = bcast_row(columns[k + 1], k + 1) - (beside * beside) * reciprocal
            factor = jnp.where(row == k, 0.0, columns[k]) * reciprocal
            for j in range(k + 1, BLOCK):
                columns[j] = columns[j] - factor * bcast_row(columns[j], k)
            panel = [value - factor * bcast_row(value, k) for value in panel]
            if k == 8 and below < size:
                factors = [columns_of(values[0], at + j) for j in range(BLOCK)]
        solved = [value * reciprocals for value in panel]
        scale = lax.rsqrt(pivots)
        kept = [value * scale for value in pivot_rows]
        inverse_ref[0, rows, :] = kept[parts.index(2)]
        inverse_ref[1, rows, :] = kept[parts.index(3)] if 3 in parts else jnp.zeros_like(scale)
        if below == size:
            break
        panel = []
        for value, taken in zip(values, solved):
            terms = [factors[k] * bcast_row(taken, k) for k in range(BLOCK)]
            panel.append(value - tree_sum(terms))
        if below == half:
            panel = panel[1:] + [matrix_ref[3, below : below + BLOCK, :]]
        columns = [columns_of(panel[0], below % half + j) for j in range(BLOCK)]
        rest = slice(below + BLOCK, size)
        if below + BLOCK < size:
            taken = far_rows(matrix_ref[parts[0], rest, :], solved, at)
            for i, part in enumerate(parts):
                mine = taken[:, i * size : (i + 1) * size]
                matrix_ref[part, rest, :] = matrix_ref[part, rest, :] - mine
        if below == half:
            parts = (1, 2, 3)


def zero_ends(ref, elements, side):
    for e in range(elements):
        ref[e, 0] = jnp.zeros(ref.shape[2:], f32)
        ref[e, side + 1] = jnp.zeros(ref.shape[2:], f32)
        for x in range(side):
            ref[e, x + 1, :LEAD] = jnp.zeros((LEAD, ref.shape[-1]), f32)
            ref[e, x + 1, LEAD + COL * side :] = jnp.zeros((LEAD, ref.shape[-1]), f32)


def beside_weight(side, columns):
    inside = lax.broadcasted_iota(jnp.int32, (COL, columns), 0) < side
    return jnp.where(inside, 1.0 / halfwidth, 0.0)


def slab_step(x, source, scaled_ref, previous, target, pair_ref, margin):
    elements, side = source.shape[0], source.shape[1] - 2
    columns = source.shape[-1]
    weight = beside_weight(side, columns)
    for e in range(elements):

        def column(y):
            return source[e, x + 1, LEAD + COL * y : LEAD + COL * (y + 1)]

        before, here = None, column(0)
        for y in range(side):
            low = LEAD + COL * y
            after = column(y + 1) if y + 1 < side else None
            beside = source[e, x, low : low + COL] + source[e, x + 2, low : low + COL]
            beside = beside + (
                source[e, x + 1, low - 1 : low - 1 + COL]
                + source[e, x + 1, low + 1 : low + 1 + COL]
            )
            if before is not None:
                beside = beside + before
            if after is not None:
                beside = beside + after
            scaled = scaled_ref[x, (e * G - margin + y) % scaled_ref.shape[1]]
            value = scaled * here - weight * beside
            if previous is None:
                value = 0.5 * value
            else:
                value = value - previous[e, x + 1, low : low + COL]
            target[e, x + 1, low : low + COL] = value
            if pair_ref is not None:
                high, rest = split(value)
                at = pl.multiple_of(x * (side * COL), COL) + COL * y
                pair_ref[e, pl.ds(at, COL), :columns] = high
                pair_ref[e, pl.ds(at, COL), columns:] = rest
            before, here = here, after


def first_kernel(start_ref, field_ref, next_ref, flat_ref):
    elements, columns = start_ref.shape[0], start_ref.shape[-1]
    side = field_ref.shape[1] - 2
    slab = side * side
    zero_ends(field_ref, elements, side)
    zero_ends(next_ref, elements, side)
    inside = lax.broadcasted_iota(jnp.int32, (COL, columns), 0) < side

    def prepare(x, carry):
        for e in range(elements):
            flat_ref[e, :slab] = start_ref[e, pl.ds(pl.multiple_of(x * slab, 16), slab), :].astype(f32)
            for y in range(side):
                value = jnp.where(inside, flat_ref[e, side * y : side * y + COL], 0.0)
                field_ref[e, x + 1, LEAD + COL * y : LEAD + COL * (y + 1)] = value
        return carry

    lax.fori_loop(0, side, prepare, 0, unroll=2)


def point_rows(field, margin, e, x, y):
    low = LEAD + COL * (margin + y) + margin
    return field[e, margin + x + 1, low : low + G]


def layer(field, margin, e, d, i):
    if d == 0:
        return [point_rows(field, margin, e, i, y) for y in range(G)]
    if d == 1:
        return [point_rows(field, margin, e, x, i) for x in range(G)]
    low = LEAD + COL * margin + margin + i
    return [field[e, margin + x + 1, pl.ds(low, G, stride=COL)] for x in range(G)]


def spread_potential(x, box_ref, scaled_ref):
    rows = box_ref[x]
    for y in range(scaled_ref.shape[1]):
        scaled_ref[x, y] = bcast_lane(rows, y, scaled_ref.shape[-1])


def steps(ranges, first_ref, start_ref, scaled_ref, pair_ref, margin):
    fields = (first_ref, start_ref)
    for index in range(1, FILTER):
        source, target = fields
        pair = pair_ref if index == FILTER - 1 else None

        def next_step(x, carry):
            slab_step(x, source, scaled_ref, target, target, pair, margin)
            return carry

        low, high = ranges(index)
        lax.fori_loop(low, high, next_step, 0, unroll=min(4, high - low))
        fields = fields[::-1]
    return fields[0]


def overlaps(pair_ref, low, high):
    columns = pair_ref.shape[-1] // 2
    return [
        lax.dot_general(
            pair_ref[e, low:high, :columns],
            pair_ref[e, low:high],
            (((0,), (0,)), ((), ())),
            preferred_element_type=f32,
        )
        for e in range(pair_ref.shape[0])
    ]


def own_operator(field, scaled_ref, inner_ref, applied_ref, raw_ref, margin):
    elements, columns = field.shape[0], field.shape[-1]
    y_points = scaled_ref.shape[1]

    z = lax.broadcasted_iota(jnp.int32, (G, columns), 0)
    edge = (z == 1) | (z == G - 1)
    weight_down = jnp.where(z == 0, 0.0, jnp.where(edge, 0.25, 0.5))
    edge = (z == 0) | (z == G - 2)
    weight_up = jnp.where(z == G - 1, 0.0, jnp.where(edge, 0.25, 0.5))

    def link(i):
        return 0.25 if i in (0, G - 2) else 0.5

    for e in range(elements):
        for x in range(G):
            for y in range(0, G, 2):
                inner_pair, applied_pair = [], []
                for yy in (y, y + 1):
                    here = point_rows(field, margin, e, x, yy)
                    potential = scaled_ref[margin + x, (e * G + yy) % y_points, margin : margin + G]
                    value = (0.5 * halfwidth * potential + center) * here
                    value = value - weight_down * pltpu.roll(here, 1, 0)
                    value = value - weight_up * pltpu.roll(here, G - 1, 0)
                    if x > 0:
                        value = value - link(x - 1) * point_rows(field, margin, e, x - 1, yy)
                    if x < G - 1:
                        value = value - link(x) * point_rows(field, margin, e, x + 1, yy)
                    if yy > 0:
                        value = value - link(yy - 1) * point_rows(field, margin, e, x, yy - 1)
                    if yy < G - 1:
                        value = value - link(yy) * point_rows(field, margin, e, x, yy + 1)
                    inner_pair.append(here)
                    applied_pair.append(value)
                at = slice((x * G + y) * G, (x * G + y + 2) * G)
                for ref, pair in ((inner_ref, inner_pair), (applied_ref, applied_pair)):
                    high, low = split(jnp.concatenate(pair, axis=0))
                    ref[e, at, :columns] = high
                    ref[e, at, columns:] = low

    for e in range(elements):
        both = lax.dot_general(
            inner_ref[e, :, :columns],
            applied_ref[e],
            (((0,), (0,)), ((), ())),
            preferred_element_type=f32,
        )
        raw = both[:, :columns] + both[:, columns:]
        raw = raw + lax.dot_general(
            inner_ref[e, :, columns:],
            applied_ref[e, :, :columns],
            (((0,), (0,)), ((), ())),
            preferred_element_type=f32,
        )
        raw_ref[e] = raw


def middle_kernel(
    margin,
    low_ref,
    z_before_ref,
    z_after_ref,
    start_in,
    first_in,
    start_ref,
    first_ref,
    scaled_ref,
    pair_ref,
    overlap_ref,
    box_ref,
):
    side, y_points = scaled_ref.shape[:2]
    end = side - margin
    box_ref[...] = jnp.zeros_like(box_ref)
    box_ref[:end, margin : margin + G, :y_points] = low_ref[...]
    box_ref[:end, :margin, :y_points] = z_before_ref[...]
    box_ref[:end, margin + G : side, :y_points] = z_after_ref[...]

    spread_potential(0, box_ref, scaled_ref)

    def first_step(x, carry):
        spread_potential(x + 1, box_ref, scaled_ref)
        slab_step(x, start_ref, scaled_ref, None, first_ref, None, margin)
        return carry

    lax.fori_loop(0, end, first_step, 0, unroll=5)
    steps(lambda i: (0, end - i), first_ref, start_ref, scaled_ref, pair_ref, margin)
    for e, value in enumerate(overlaps(pair_ref, 0, (end - FILTER + 1) * side * COL)):
        overlap_ref[e] = value


def basis_kernel(
    margin,
    x_after_ref,
    z_before_ref,
    z_after_ref,
    start_in,
    first_in,
    scaled_in,
    pair_in,
    overlap_ref,
    minus_x_ref,
    minus_z_ref,
    inverse_ref,
    raw_ref,
    start_ref,
    first_ref,
    scaled_ref,
    pair_ref,
    box_ref,
    matrix_ref,
    packed_ref,
    inner_ref,
    applied_ref,
):
    elements, columns = start_ref.shape[0], start_ref.shape[-1]
    side, y_points = scaled_ref.shape[:2]
    end = side - margin
    box_ref[...] = jnp.zeros_like(box_ref)
    box_ref[end:, margin : margin + G, :y_points] = x_after_ref[...]
    box_ref[end:, :margin, :y_points] = z_before_ref[...]
    box_ref[end:, margin + G : side, :y_points] = z_after_ref[...]
    for x in range(end, side):
        spread_potential(x, box_ref, scaled_ref)
    for x in range(end, side):
        slab_step(x, start_ref, scaled_ref, None, first_ref, None, margin)
    field = steps(
        lambda i: (end - i, side), first_ref, start_ref, scaled_ref, pair_ref, margin
    )
    rest = overlaps(pair_ref, (end - FILTER + 1) * side * COL, side * side * COL)

    own_operator(field, scaled_ref, inner_ref, applied_ref, raw_ref, margin)

    identity = (
        lax.broadcasted_iota(jnp.int32, (columns, columns), 0)
        == lax.broadcasted_iota(jnp.int32, (columns, columns), 1)
    ).astype(f32)
    grams = []
    for e in range(elements):
        products = overlap_ref[e] + rest[e]
        cross = products[:, columns:]
        grams.append(products[:, :columns] + (cross + cross.T))
    for e in range(0, elements, 2):
        pairs = [grams[e], grams[min(e + 1, elements - 1)]]
        for i, value in enumerate(pack(pairs) + pack([identity, identity])):
            matrix_ref[i] = value
        inverse_factors(matrix_ref, packed_ref)
        solved = pack([packed_ref[0], packed_ref[1]])
        for i in range(min(2, elements - e)):
            inverse_ref[e + i] = solved[i]

    for e in range(elements):
        held = weights(split(inverse_ref[e]), True)
        rows = []
        for d in (0, 2):
            rows += layer(field, margin, e, d, 0) + layer(field, margin, e, d, 1)
        faces = product(jnp.concatenate(rows, 0), held, True)
        minus_x_ref[e] = faces[: 2 * G * G]
        minus_z_ref[e] = faces[2 * G * G :]


def near_kernel(
    count,
    margin,
    inverse_ref,
    raw_ref,
    field,
    plus_ref,
    *rest,
):
    out_refs, near_ref = rest[:-1], rest[-1]
    elements, columns = inverse_ref.shape[0], inverse_ref.shape[-1]
    face = 2 * G * G
    minus, plus, held = [], [], []
    for e in range(elements):
        held.append(weights(split(inverse_ref[e]), True))
        rows = layer(field, margin, e, 1, 0) + layer(field, margin, e, 1, 1)
        for d in range(3):
            last = layer(field, margin, e, d, G - 1)
            before = layer(field, margin, e, d, G - 2)
            rows += [-(0.5 * a + 0.25 * b) for a, b in zip(last, before)]
            rows += [-0.25 * a for a in last]
        faces = product(jnp.concatenate(rows, 0), held[e], True)
        minus.append(faces[:face])
        plus.append(faces[face : 2 * face].T)
        plus_ref[e, 0] = plus[e]
        plus[e] = faces[2 * face : 3 * face].T
        plus_ref[e, 1] = faces[3 * face :].T

    for e in range(elements):
        half = product(inverse_ref[e], weights(split(raw_ref[e]), False), False)
        near_ref[0, e] = product(half, held[e], True)
        following = weights(split(minus[(e + 1) % elements]), False)
        near_ref[1, e] = product(plus[e], following, False)
    send_rows(count, near_ref, out_refs)


def partner(index, step, count):
    return index ^ step if count & (count - 1) == 0 else (index + step) % count


def partner(index, step, count):
    return index ^ step if count & (count - 1) == 0 else (index + step) % count


def send_rows(count, blocks_ref, out_refs):
    kinds, elements, size = blocks_ref.shape[:3]
    rows = size // count
    me = lax.axis_index("ez")
    for step, out_ref in enumerate(out_refs):
        owner = me ^ step if count & (count - 1) == 0 else lax.rem(me + step, count)
        at = pl.ds(pl.multiple_of(owner * rows, rows), rows)
        for kind in range(kinds):
            for e in range(elements):
                out_ref[:, kind, e, :] = blocks_ref[kind, e, at, :]


def far_kernel(count, plus_ref, next_x_ref, next_z_ref, *rest):
    out_refs, far_ref = rest[:-1], rest[-1]
    for e in range(plus_ref.shape[0]):
        for d, ref in ((0, next_x_ref), (1, next_z_ref)):
            far_ref[d, e] = product(plus_ref[e, d], weights(split(ref[e]), False), False)
    send_rows(count, far_ref, out_refs)


def place(refs, targets, semaphores):
    count = len(refs)
    me = lax.axis_index("ez")
    copies = []
    for step, ref in enumerate(refs):
        z = me ^ step if count & (count - 1) == 0 else lax.rem(me + (count - step), count)
        for kind, target in enumerate(targets(z)):
            copies.append(
                pltpu.make_async_copy(ref.at[:, kind], target, semaphores.at[step, kind])
            )
            copies[-1].start()
    for copy in copies:
        copy.wait()


def near_order(count):
    return [*range(2, count), *range(min(2, count))[::-1]]


def place_near_kernel(count, *refs):
    diagonal_ref, coupling_ref, semaphores = refs[count:]
    place(
        [refs[near_order(count).index(step)] for step in range(count)],
        lambda z: (diagonal_ref.at[:, z], coupling_ref.at[:, z, 1]),
        semaphores,
    )


def place_far_kernel(count, *refs):
    coupling_ref, semaphores = refs[count + 1 :]
    place(
        refs[:count][::-1],
        lambda z: (coupling_ref.at[:, z, 0], coupling_ref.at[:, z, 2]),
        semaphores,
    )


def vmem(count):
    return [pl.BlockSpec(memory_space=pltpu.VMEM)] * count


def shift(block, axis, distance):
    count = lax.axis_size(axis)
    return lax.ppermute(block, axis, [(i, (i + distance) % count) for i in range(count)])


def exchange(block, step):
    count = lax.axis_size("ez")
    if step == 0:
        return block
    return lax.ppermute(block, "ez", [(i, partner(i, step, count)) for i in range(count)])


def local(potential, basis_start):
    elements, points, columns = basis_start.shape[2:]
    side = round(points ** (1 / 3))
    margin = (side - G) // 2
    y_points = potential.shape[1]
    count = lax.axis_size("ez")
    starts = basis_start.reshape(elements, points, columns)
    own = potential.transpose(0, 2, 1)
    own_scaled = lax.optimization_barrier((own + (3.0 - center)) * (2.0 / halfwidth))
    x_before = (shift(own, "ex", 1)[G - margin :] + (3.0 - center)) * (2.0 / halfwidth)
    x_after = shift(own_scaled[:margin], "ex", -1)

    shape = jax.ShapeDtypeStruct
    field = shape((elements, side + 2, LEAD + COL * side + LEAD, columns), f32)
    scaled = shape((side, y_points, COL, columns), f32)
    start, first = pl.pallas_call(
        first_kernel,
        out_shape=[field, field],
        in_specs=vmem(1),
        out_specs=vmem(2),
        scratch_shapes=[pltpu.VMEM((elements, side * side + COL, columns), f32)],
        compiler_params=pltpu.CompilerParams(vmem_limit_bytes=24 * 2**20),
        cost_estimate=pl.CostEstimate(flops=10**5, bytes_accessed=10**4, transcendentals=0),
        name="first",
    )(starts)
    low = lax.optimization_barrier(jnp.concatenate([x_before, own_scaled], axis=0))
    z_before = shift(low[:, G - margin :], "ez", 1)
    z_after = shift(low[:, :margin], "ez", -1)
    edge_before = shift(x_after[:, G - margin :], "ez", 1)
    edge_after = shift(x_after[:, :margin], "ez", -1)
    pair = shape((elements, side * side * COL, 2 * columns), bf16)
    overlap = shape((elements, columns, 2 * columns), f32)
    box = pltpu.VMEM((side, COL, 128), f32)
    start, first, most_scaled, pairs, overlapped = pl.pallas_call(
        functools.partial(middle_kernel, margin),
        out_shape=[field, field, scaled, pair, overlap],
        in_specs=vmem(5),
        out_specs=vmem(5),
        input_output_aliases={3: 0, 4: 1},
        scratch_shapes=[box],
        compiler_params=pltpu.CompilerParams(vmem_limit_bytes=32 * 2**20),
        cost_estimate=pl.CostEstimate(flops=10**8, bytes_accessed=10**7, transcendentals=0),
        name="middle",
    )(low, z_before, z_after, start, first)

    face = shape((elements, 2 * G * G, columns), f32)
    square = shape((elements, columns, columns), f32)
    minus_x, minus_z, inverse, raw, _, filtered, _, _ = pl.pallas_call(
        functools.partial(basis_kernel, margin),
        out_shape=[face, face, square, square, field, field, scaled, pair],
        in_specs=vmem(8),
        out_specs=vmem(8),
        input_output_aliases={3: 4, 4: 5, 5: 6, 6: 7},
        scratch_shapes=[
            box,
            pltpu.VMEM((4, columns, columns), f32),
            pltpu.VMEM((2, columns, columns), f32),
            pltpu.VMEM((elements, G**3, 2 * columns), bf16),
            pltpu.VMEM((elements, G**3, 2 * columns), bf16),
        ],
        compiler_params=pltpu.CompilerParams(vmem_limit_bytes=32 * 2**20),
        name="basis",
    )(x_after, edge_before, edge_after, start, first, most_scaled, pairs, overlapped)

    next_x = shift(minus_x, "ex", -1)
    next_z = shift(minus_z, "ez", -1)
    rows = columns // count
    block = shape((rows, 2, elements, columns), f32)
    squares = pltpu.VMEM((2, elements, columns, columns), f32)
    plus, *near = pl.pallas_call(
        functools.partial(near_kernel, count, margin),
        out_shape=[shape((elements, 2, columns, 2 * G * G), f32)] + [block] * count,
        in_specs=vmem(3),
        out_specs=vmem(1 + count),
        scratch_shapes=[squares],
        compiler_params=pltpu.CompilerParams(vmem_limit_bytes=24 * 2**20),
        cost_estimate=pl.CostEstimate(flops=10**8, bytes_accessed=10**7, transcendentals=0),
        name="near",
    )(inverse, raw, filtered)
    near = [exchange(value, step) for step, value in enumerate(near)]

    far = pl.pallas_call(
        functools.partial(far_kernel, count),
        out_shape=[block] * count,
        in_specs=vmem(3),
        out_specs=vmem(count),
        scratch_shapes=[squares],
        compiler_params=pltpu.CompilerParams(vmem_limit_bytes=16 * 2**20),
        name="far",
    )(plus, next_x, next_z)
    far = [exchange(far[step], step) for step in reversed(range(count))][::-1]

    anywhere = pl.BlockSpec(memory_space=pltpu.HBM)
    semaphores = pltpu.SemaphoreType.DMA((count, 2))
    half = shape((rows, count, 3, elements, columns), f32)
    diagonal, coupled = pl.pallas_call(
        functools.partial(place_near_kernel, count),
        out_shape=[shape((rows, count, elements, columns), f32), half],
        in_specs=vmem(count),
        out_specs=[anywhere] * 2,
        scratch_shapes=[semaphores],
        compiler_params=pltpu.CompilerParams(vmem_limit_bytes=16 * 2**20),
        name="place_near",
    )(*[near[step] for step in near_order(count)])
    coupled = pl.pallas_call(
        functools.partial(place_far_kernel, count),
        out_shape=half,
        in_specs=vmem(count) + [anywhere],
        out_specs=anywhere,
        input_output_aliases={count: 0},
        scratch_shapes=[semaphores],
        compiler_params=pltpu.CompilerParams(vmem_limit_bytes=16 * 2**20),
        name="place_far",
    )(*far[::-1], coupled)
    return (diagonal[None], coupled.transpose(0, 1, 3, 2, 4)[None])


def solution(mesh):
    return jax.shard_map(
        local,
        mesh=mesh,
        in_specs=(P("ex", None, "ez"), P("ex", "ez", None, None, None)),
        out_specs=(P("ex", "ez", None, None, None), P("ex", "ez", None, None, None, None)),
        check_vma=False,
    )
```
